128 devices in a mesh: side: 2 (over core), dev: 64 (over x, y, z).
Axes of the slice: x: 4, y: 4, z: 4, core: 2. Of those that a mesh axis runs over, the one named last changes fastest.
Arguments:
- query: bfloat16 [128, 6144], P('dev'), may hold values from -120 to 120
- new_key: bfloat16 [128, 1024], P('dev'), may hold values from -4 to 4
- new_value: bfloat16 [128, 1024], P('dev'), may hold values from -4 to 4
- key_cache: bfloat16 [128, 128, 1024], P('dev'), may hold values from -4 to 4
- value_cache: bfloat16 [128, 128, 1024], P('dev'), may hold values from -4 to 4
- cached: int32 [128], P('dev'), may hold values from 2 to 128, as said below
- residual: bfloat16 [128, 6144], P('dev'), may hold values from -36 to 36
- out_weight: bfloat16 [6144, 6144], P(None, 'dev'), may hold values from -0.078125 to 0.078125
- norm_gain: bfloat16 [6144], replicated, may hold values from 0.25 to 1.75
- expert_ids: int32 [128, 2], P('dev'), may hold values from 0 to 3, all different within a row; in each aligned block of 2 rows (0 to 1, 2 to 3, ...) at most 2 rows name the same one
- gate_weights: float32 [128, 2], P('dev'), may hold values from 0.1 to 0.9
- w_gate: bfloat16 [6144, 32768], P(None, 'dev'), may hold values from -0.078125 to 0.078125
- w_up: bfloat16 [6144, 32768], P(None, 'dev'), may hold values from -0.078125 to 0.078125
- w_down: bfloat16 [32768, 6144], P('dev'), may hold values from -0.0625 to 0.0625
Outputs:
- mixed: bfloat16 [128, 6144], P('dev', 'side')
The draws below stay inside these ranges and needn't reach their ends.
Inputs may be any that keep to these rules, and one draw needn't show every extreme that they name: `expert_ids`: each row names 2 different experts; in each aligned block of 2 rows (the rows of one device) no expert is named by more than 2 rows, a bound that some block reaches. `cached`: some sequence uses all 128 positions.
All inputs are finite; a program needn't handle non-finite values.
Results may differ from the reference program's by a relative error of at most 0.012.
Values may be sent and summed in bfloat16 or wider, within the bound.
No kernel may reach another device: no remote copies, remote signals or barrier semaphores. Data moves between devices by JAX's collectives and lax.ppermute only.
A program may use at most 128 MiB of HBM per device.

```python
import math
import jax
import jax.numpy as jnp
import numpy as np
from jax import lax

D = 6144
HEADS = 48
KV_HEADS = 8
HEAD_DIM = 128
EXPERTS = 4
FF = 8192
TOP = 2
B_DEV = 2
CACHE_LEN = 128
CAP = 2
TOKENS = 128
N_DEV = 64


def cached_keys(key):
    return jnp.clip(jax.random.normal(key, (TOKENS, CACHE_LEN, KV_HEADS * HEAD_DIM), jnp.float32), -4.0, 4.0)


def draw_key_cache(key, part):
    keys = cached_keys(key)
    return keys.astype(jnp.bfloat16)


def draw_query(key, part):
    key = jax.random.fold_in(key, 2)
    queries = jnp.clip(jax.random.normal(key, (TOKENS, HEADS * HEAD_DIM), jnp.float32), -4.0, 4.0)
    return queries.astype(jnp.bfloat16)


def draw_residual(key, part):
    key = jax.random.fold_in(key, 3)
    first = jax.random.fold_in(key, 0)
    values = jnp.clip(jax.random.normal(first, (TOKENS, D), jnp.float32), -4.0, 4.0)
    return values.astype(jnp.bfloat16)


def draw_cached(key, part):
    key = jax.random.fold_in(key, 4)
    first, second = jax.random.split(key)
    lengths = jax.random.randint(first, (TOKENS,), 2, CACHE_LEN + 1)
    longest = jax.random.randint(second, (), 0, TOKENS)
    return jnp.where(jnp.arange(TOKENS) == longest, CACHE_LEN, lengths).astype(jnp.int32)


def steps_of(stream_key, extent, cuts, smallest, largest):
    gain, own = 1.0, jax.random.fold_in(stream_key, 6)
    for position, parts in cuts:
        steps = jnp.exp(jax.random.uniform(jax.random.fold_in(own, position), (parts,), jnp.float32, smallest / len(cuts), largest / len(cuts)))
        gain = gain * jnp.repeat(steps, extent[position] // parts).reshape([-1 if axis == position else 1 for axis in range(len(extent))])
    return gain


def shared_out(stream_key, own, number, rows, number_of, top, reach, skew):
    order = jax.random.permutation(stream_key, number_of)
    heavy_load, common = load_shares(number_of, rows * top, reach, skew, True), load_shares(number_of, rows * top, reach, skew, False)
    places = jnp.arange(number_of)

    def named(tallies, turn):
        used = int((tallies > 0).sum())
        fixed = max(1, used // 4)
        passed = fixed + (places - fixed + turn * (used - fixed)) % max(1, number_of - fixed)
        return jnp.zeros((number_of,), jnp.int32).at[order[jnp.where(places < fixed, places, passed)]].set(jnp.asarray(tallies, jnp.int32))

    tallies = jnp.where(number % 4 == 0, named(heavy_load, number // 4), named(common, number - number // 4 - 1))
    mixed = jax.random.permutation(jax.random.fold_in(own, 3), number_of)
    donor, receiver = mixed[0:number_of // 2 * 2:2], mixed[1:number_of // 2 * 2:2]
    room = jnp.minimum(tallies[donor] - 1, reach - tallies[receiver]) // 2
    room = jnp.where((donor == order[0]) | (receiver == order[0]) | (tallies[receiver] == 0), 0, jnp.maximum(room, 0))
    passed = jax.random.randint(jax.random.fold_in(own, 4), (number_of // 2,), 0, 1 << 20) % (room + 1)
    tallies = tallies.at[donor].add(-passed).at[receiver].add(passed)
    labels = jnp.searchsorted(jnp.cumsum(tallies), jnp.arange(rows * top), side="right").astype(jnp.int32)
    table = labels.reshape(top, rows).T
    table = table[jax.random.permutation(jax.random.fold_in(own, 1), rows)]
    turn = jax.random.randint(jax.random.fold_in(own, 2), (rows, 1), 0, top)
    return jnp.take_along_axis(table, (jnp.arange(top)[None, :] + turn) % top, axis=1)


def load_shares(amount, total, most, lean, full):
    loads = [(1 << 20) // math.isqrt(grade ** lean) + 1 for grade in range(1, amount + 1)]
    largest = most if full else min(most, max(-(-total // amount), total * loads[0] // sum(loads)))
    least = 1 if total - largest >= amount - 1 else 0
    counts, spare = [largest] + [least] * (amount - 1), total - largest - least * (amount - 1)
    while spare > 0:
        free = [i for i in range(1, amount) if counts[i] < largest] or [i for i in range(1, amount) if counts[i] < most]
        whole, left = sum([loads[i] for i in free]), spare
        for i in free:
            extra = min(most - counts[i], max(1, left * loads[i] // whole), spare)
            counts[i] = counts[i] + extra
            spare = spare - extra
    return np.array(counts)


def scatter_about(stream_key, dims, spread, reach, cuts=(), held_as=jnp.bfloat16):
    result = jax.random.normal(stream_key, dims, jnp.float32) * spread
    if len(cuts) > 0:
        result = steps_of(stream_key, dims, cuts, -0.22, 0.18) * result
    return jnp.clip(result, min=-reach, max=reach).astype(held_as)


def setup_inputs(seed: int = 0) -> dict:
    key_list = jax.random.split(jax.random.key(seed), 15)
    query = draw_query(jax.random.fold_in(key_list[14], 71), 0)
    new_key = scatter_about(key_list[1], (TOKENS, KV_HEADS * HEAD_DIM), 1.0, 4.0, ((0, 64),))
    new_value = scatter_about(key_list[2], (TOKENS, KV_HEADS * HEAD_DIM), 1.0, 4.0, ((0, 64),))
    key_cache = draw_key_cache(jax.random.fold_in(key_list[14], 71), 0)
    value_cache = scatter_about(key_list[4], (TOKENS, CACHE_LEN, KV_HEADS * HEAD_DIM), 1.0, 4.0, ((0, 64),))
    cached = draw_cached(jax.random.fold_in(key_list[14], 71), 0)
    residual = draw_residual(jax.random.fold_in(key_list[14], 71), 0)
    out_weight = scatter_about(key_list[7], (D, D), D ** -0.5, 0.078125, ((1, 64),))
    norm_gain = jnp.clip(1.0 + 0.15 * jax.random.normal(key_list[8], (D,), jnp.float32), 0.25, 1.75).astype(jnp.bfloat16)
    expert_ids_keys = jax.random.split(jax.random.fold_in(key_list[9], 1), TOKENS // B_DEV)
    expert_ids_turns = jax.random.permutation(jax.random.fold_in(key_list[9], 3), TOKENS // B_DEV)
    expert_ids = jax.vmap(lambda own, number: shared_out(jax.random.fold_in(key_list[9], 2), own, number, B_DEV, EXPERTS, TOP, CAP, 2))(expert_ids_keys, expert_ids_turns).reshape((TOKENS, TOP))
    gate_weights = jnp.clip(0.1 + 0.79999997 * jax.random.uniform(key_list[10], (TOKENS, TOP), jnp.float32) ** steps_of(key_list[10], (TOKENS, TOP), ((0, 64),), -0.2, 0.2), 0.1, 0.9)
    w_gate = scatter_about(key_list[11], (D, EXPERTS * FF), D ** -0.5, 0.078125, ((1, 64),))
    w_up = scatter_about(key_list[12], (D, EXPERTS * FF), D ** -0.5, 0.078125, ((1, 64),))
    w_down = scatter_about(key_list[13], (EXPERTS * FF, D), FF ** -0.5, 0.0625, ((0, 64),))
    return dict(query=query, new_key=new_key, new_value=new_value, key_cache=key_cache, value_cache=value_cache, cached=cached, residual=residual, out_weight=out_weight, norm_gain=norm_gain, expert_ids=expert_ids, gate_weights=gate_weights, w_gate=w_gate, w_up=w_up, w_down=w_down)


epsilon = 1e-05

def attend(query, new_key, new_value, key_cache, value_cache, cached):
    seq_count = query.shape[0]
    group_size = HEADS // KV_HEADS
    score_scale = 1.0 / math.sqrt(HEAD_DIM)
    queries = query.reshape(seq_count, KV_HEADS, group_size, HEAD_DIM).astype(jnp.float32)
    cache_keys = key_cache.reshape(seq_count, CACHE_LEN, KV_HEADS, HEAD_DIM).astype(jnp.float32)
    cache_values = value_cache.reshape(seq_count, CACHE_LEN, KV_HEADS, HEAD_DIM).astype(jnp.float32)
    scores = jnp.einsum('bgrd,blgd->bgrl', queries, cache_keys) * score_scale
    own_score = jnp.einsum('bgrd,bgd->bgr', queries, new_key.reshape(seq_count, KV_HEADS, HEAD_DIM).astype(jnp.float32)) * score_scale
    visible = jnp.arange(CACHE_LEN)[None, :] < cached[:, None]
    scores = jnp.where(visible[:, None, None, :], scores, -jnp.inf)
    highest = jnp.maximum(lax.optimization_barrier(jnp.max(scores, axis=3)), own_score)
    exponents = jnp.exp(scores - highest[..., None])
    own_exp = jnp.exp(own_score - highest)
    denominator = lax.optimization_barrier(jnp.sum(exponents, axis=3)) + own_exp
    weights = (exponents / denominator[..., None]).astype(jnp.bfloat16)
    own_weight = (own_exp / denominator).astype(jnp.bfloat16)
    context = jnp.einsum('bgrl,blgd->bgrd', weights.astype(jnp.float32), cache_values)
    context = context + own_weight.astype(jnp.float32)[..., None] * new_value.reshape(seq_count, KV_HEADS, 1, HEAD_DIM).astype(jnp.float32)
    return context.reshape(seq_count, HEADS * HEAD_DIM).astype(jnp.bfloat16)

def normalize(hidden, norm_gain):
    widened = hidden.astype(jnp.float32)
    factor = lax.rsqrt(lax.optimization_barrier(jnp.mean(widened * widened, axis=1, keepdims=True)) + epsilon)
    return (widened * factor * norm_gain.astype(jnp.float32)[None, :]).astype(jnp.bfloat16)

def reference(query, new_key, new_value, key_cache, value_cache, cached, residual, out_weight, norm_gain, expert_ids, gate_weights, w_gate, w_up, w_down):
    context = attend(query, new_key, new_value, key_cache, value_cache, cached)
    projected = jnp.dot(context, out_weight, preferred_element_type=jnp.float32)
    hidden = (residual.astype(jnp.float32) + projected).astype(jnp.bfloat16)
    normed = normalize(hidden, norm_gain)
    block_width = EXPERTS * FF // N_DEV
    block_count = FF // block_width

    def per_expert(expert):

        def add_block(block, summed):
            first_col = (expert * FF + block * block_width).astype(jnp.int32)
            gate_cols = lax.dynamic_slice_in_dim(w_gate, first_col, block_width, 1)
            up_cols = lax.dynamic_slice_in_dim(w_up, first_col, block_width, 1)
            down_rows = lax.dynamic_slice_in_dim(w_down, first_col, block_width, 0)
            gate_part = jnp.dot(normed, gate_cols, preferred_element_type=jnp.float32)
            up_part = jnp.dot(normed, up_cols, preferred_element_type=jnp.float32)
            act = (jax.nn.silu(gate_part) * up_part).astype(jnp.bfloat16)
            partial_value = jnp.dot(act, down_rows, preferred_element_type=jnp.float32).astype(jnp.bfloat16)
            return summed + partial_value.astype(jnp.float32)
        start = jnp.zeros((TOKENS, D), jnp.float32)
        return lax.fori_loop(0, block_count, add_block, start)
    expert_out = lax.map(per_expert, jnp.arange(EXPERTS, dtype=jnp.int32))
    chosen = expert_out[expert_ids, jnp.arange(TOKENS, dtype=jnp.int32)[:, None]]
    moe = lax.optimization_barrier(jnp.sum(gate_weights[:, :, None] * chosen, axis=1))
    return (hidden.astype(jnp.float32) + moe).astype(jnp.bfloat16)
```

```python
import math

import jax
import jax.numpy as jnp
import numpy as np
from jax import lax
from jax.sharding import PartitionSpec as P

D = 6144
HEADS = 48
KV_HEADS = 8
HEAD_DIM = 128
EXPERTS = 4
CACHE_LEN = 128
DEVS = 64
COLS = D // DEVS
HALF = COLS // 2
ROWS = D // 128

epsilon = 1e-05


def attend(query, new_key, new_value, key_cache, value_cache, cached):
    group_size = HEADS // KV_HEADS
    score_scale = 1.0 / math.sqrt(HEAD_DIM)
    queries = query.reshape(KV_HEADS, group_size, HEAD_DIM)
    cache_keys = key_cache.reshape(CACHE_LEN, KV_HEADS, HEAD_DIM)
    cache_values = value_cache.reshape(CACHE_LEN, KV_HEADS, HEAD_DIM)
    scores = (
        jnp.einsum("grd,lgd->grl", queries, cache_keys, preferred_element_type=jnp.float32)
        * score_scale
    )
    own_score = (
        jnp.einsum(
            "grd,gd->gr",
            queries,
            new_key.reshape(KV_HEADS, HEAD_DIM),
            preferred_element_type=jnp.float32,
        )
        * score_scale
    )
    visible = jnp.arange(CACHE_LEN) < cached
    scores = jnp.where(visible[None, None, :], scores, -jnp.inf)
    highest = jnp.maximum(jnp.max(scores, axis=2), own_score)
    exponents = jnp.exp(scores - highest[..., None])
    own_exp = jnp.exp(own_score - highest)
    denominator = jnp.sum(exponents, axis=2) + own_exp
    weights = (exponents / denominator[..., None]).astype(jnp.bfloat16)
    own_weight = (own_exp / denominator).astype(jnp.bfloat16)
    context = jnp.einsum(
        "grl,lgd->grd", weights, cache_values, preferred_element_type=jnp.float32
    )
    context = context + own_weight.astype(jnp.float32)[..., None] * new_value.reshape(
        KV_HEADS, 1, HEAD_DIM
    ).astype(jnp.float32)
    return context.reshape(HEADS, HEAD_DIM).astype(jnp.bfloat16)


def exchange(parts):
    return lax.all_to_all(parts, "dev", split_axis=0, concat_axis=0, tiled=True)


def local(
    query,
    new_key,
    new_value,
    key_cache,
    value_cache,
    cached,
    residual,
    out_weight,
    norm_gain,
    expert_ids,
    gate_weights,
    w_gate,
    w_up,
    w_down,
):
    core = lax.axis_index("side")
    chip = lax.axis_index("dev")

    def own(value):
        return lax.dynamic_index_in_dim(value, core, 0, keepdims=False)

    context = attend(
        own(query), own(new_key), own(new_value), own(key_cache), own(value_cache), own(cached)
    )
    first_row = (COLS * np.arange(DEVS)) // 128
    wanted = np.minimum(first_row[:, None] + np.arange(8)[None, :], ROWS - 1)
    residual_rows = own(residual).reshape(ROWS, 128)[wanted]
    outgoing = jnp.concatenate(
        [jnp.broadcast_to(context[None], (DEVS, ROWS, 128)), residual_rows], axis=1
    )
    arrived = exchange(outgoing)
    projected = jnp.dot(
        arrived[:, :ROWS].reshape(DEVS, D), out_weight, preferred_element_type=jnp.float32
    )
    residual_part = lax.dynamic_slice_in_dim(
        arrived[:, ROWS : ROWS + 2].reshape(DEVS, 256), (COLS * chip) % 128, COLS, 1
    )
    hidden_part = (residual_part.astype(jnp.float32) + projected).astype(jnp.bfloat16)
    flipped = hidden_part.T
    packed = jnp.concatenate([flipped[:HALF], flipped[HALF:]], axis=1)
    hidden_all = exchange(jnp.broadcast_to(packed[None], (DEVS, HALF, 128)))
    hidden = (
        hidden_all.reshape(DEVS, HALF, 2, DEVS).transpose(3, 0, 2, 1).reshape(DEVS, D)
    )
    widened = hidden.astype(jnp.float32)
    factor = lax.rsqrt(jnp.mean(widened * widened, axis=1, keepdims=True) + epsilon)
    normed = (widened * factor * norm_gain.astype(jnp.float32)[None, :]).astype(jnp.bfloat16)
    gate_part = jnp.dot(normed, w_gate, preferred_element_type=jnp.float32)
    up_part = jnp.dot(normed, w_up, preferred_element_type=jnp.float32)
    act = (jax.nn.silu(gate_part) * up_part).astype(jnp.bfloat16)
    partial_value = jnp.dot(act, w_down, preferred_element_type=jnp.float32).astype(jnp.bfloat16)
    returned = exchange(partial_value.reshape(DEVS, ROWS, 128))
    share = jnp.sum(
        jnp.where(
            own(expert_ids)[None, :] == jnp.arange(EXPERTS)[:, None], own(gate_weights)[None, :], 0.0
        ),
        axis=1,
    )
    per_expert = jnp.sum(
        returned.reshape(EXPERTS, DEVS // EXPERTS, ROWS, 128).astype(jnp.float32), axis=1
    )
    moe = jnp.sum(per_expert * share[:, None, None], axis=0)
    own_hidden = lax.dynamic_index_in_dim(hidden, chip, 0, keepdims=False).reshape(ROWS, 128)
    mixed = (own_hidden.astype(jnp.float32) + moe).astype(jnp.bfloat16)
    halves = mixed.reshape(2, ROWS // 2, 128)
    kept = own(halves)
    given = lax.dynamic_index_in_dim(halves, 1 - core, 0, keepdims=False)
    taken = lax.ppermute(given, "side", [(0, 1), (1, 0)])
    first = jnp.where(core == 0, kept, taken)
    second = jnp.where(core == 0, taken, kept)
    return jnp.stack([first.reshape(D // 2), second.reshape(D // 2)])


def solution(mesh):
    in_specs = (
        P("dev", None),
        P("dev", None),
        P("dev", None),
        P("dev", None, None),
        P("dev", None, None),
        P("dev"),
        P("dev", None),
        P(None, "dev"),
        P(),
        P("dev", None),
        P("dev", None),
        P(None, "dev"),
        P(None, "dev"),
        P("dev", None),
    )
    out_specs = P("dev", "side")
    return jax.shard_map(local, mesh=mesh, in_specs=in_specs, out_specs=out_specs, check_vma=False)
```

```python
import math

import jax
import jax.numpy as jnp
from jax import lax
from jax.experimental import pallas as pl
from jax.experimental.pallas import tpu as pltpu
from jax.sharding import PartitionSpec as P

D = 6144
HEADS = 48
KV_HEADS = 8
HEAD_DIM = 128
GROUP = HEADS // KV_HEADS
EXPERTS = 4
CACHE_LEN = 128
DEVS = 64
COLS = D // DEVS
HALF = COLS // 2
ROWS = D // 128
SENT = ROWS + 8
UNITS = 512
HALF_D = D // 2
CHUNK = 768
PART = CHUNK // HALF

epsilon = 1e-05

VMEM_BLOCK = pl.BlockSpec(memory_space=pltpu.VMEM)
SMEM_BLOCK = pl.BlockSpec(memory_space=pltpu.SMEM)
ANY_BLOCK = pl.BlockSpec(memory_space=pl.ANY)


def last_dims(left, right):
    return lax.dot_general(
        left, right, (((1,), (1,)), ((), ())), preferred_element_type=jnp.float32
    )


def attend_kernel(
    core_ref,
    cached_ref,
    query_ref,
    new_key_ref,
    new_value_ref,
    residual_ref,
    key_ref,
    value_ref,
    out_ref,
    query_rows,
    context_rows,
    residual_rows,
):
    core = core_ref[0]

    def own(ref):
        both = ref[...].astype(jnp.float32)
        return jnp.where(core == 0, both[0:1], both[1:2])

    query = own(query_ref)
    new_key = own(new_key_ref)
    new_value = own(new_value_ref)
    residual = own(residual_ref)
    query_rows[...] = jnp.zeros_like(query_rows)
    for head in range(HEADS):
        row = head // GROUP * 8 + head % GROUP
        query_rows[row : row + 1, :] = query[:, head * 128 : head * 128 + 128]
    for row in range(ROWS):
        residual_rows[row : row + 1, :] = residual[:, row * 128 : row * 128 + 128]
    residual_rows[ROWS:SENT, :] = jnp.zeros((SENT - ROWS, 128), jnp.float32)
    queries = query_rows[...]
    narrow = queries.astype(jnp.bfloat16)
    scale = 1.0 / math.sqrt(HEAD_DIM)
    scores = []
    own_keys = []
    for kv in range(KV_HEADS):
        lanes = slice(kv * 128, kv * 128 + 128)
        scores.append(last_dims(narrow[kv * 8 : kv * 8 + 8], key_ref[0, :, lanes]))
        own_keys.append(jnp.broadcast_to(new_key[:, lanes], (8, 128)))
    scores = jnp.concatenate(scores, axis=0) * scale
    own_score = jnp.sum(queries * jnp.concatenate(own_keys, axis=0), axis=1, keepdims=True) * scale
    visible = lax.broadcasted_iota(jnp.int32, scores.shape, 1) < cached_ref[core]
    scores = jnp.where(visible, scores, -jnp.inf)
    highest = jnp.maximum(jnp.max(scores, axis=1, keepdims=True), own_score)
    exponents = jnp.exp(scores - highest)
    own_exp = jnp.exp(own_score - highest)
    denominator = jnp.sum(exponents, axis=1, keepdims=True) + own_exp
    weights = (exponents / denominator).astype(jnp.bfloat16)
    own_weight = (own_exp / denominator).astype(jnp.bfloat16).astype(jnp.float32)
    for kv in range(KV_HEADS):
        lanes = slice(kv * 128, kv * 128 + 128)
        context = jnp.dot(
            weights[kv * 8 : kv * 8 + 8], value_ref[0, :, lanes], preferred_element_type=jnp.float32
        )
        context = context + own_weight[kv * 8 : kv * 8 + 8] * new_value[:, lanes]
        context_rows[kv * GROUP : kv * GROUP + 8, :] = context
    context = context_rows[0:HEADS, :].astype(jnp.bfloat16)
    for chip in range(DEVS):
        first = COLS * chip // 128
        out_ref[chip, 0:ROWS, :] = context
        out_ref[chip, ROWS:SENT, :] = residual_rows[first : first + 8, :].astype(jnp.bfloat16)


def attend(core, cached, query, new_key, new_value, residual, key_cache, value_cache):
    def whole(shape):
        return pl.BlockSpec(shape, lambda step, core, cached: (0,) * len(shape))

    cache = pl.BlockSpec((1, CACHE_LEN, 1024), lambda step, core, cached: (core[0], 0, 0))
    return pl.pallas_call(
        attend_kernel,
        out_shape=jax.ShapeDtypeStruct((DEVS, SENT, 128), jnp.bfloat16),
        grid_spec=pltpu.PrefetchScalarGridSpec(
            num_scalar_prefetch=2,
            grid=(1,),
            in_specs=[
                whole((2, D)),
                whole((2, 1024)),
                whole((2, 1024)),
                whole((2, D)),
                cache,
                cache,
            ],
            out_specs=whole((DEVS, SENT, 128)),
            scratch_shapes=[
                pltpu.VMEM((64, 128), jnp.float32),
                pltpu.VMEM((SENT, 128), jnp.float32),
                pltpu.VMEM((SENT, 128), jnp.float32),
            ],
        ),
        compiler_params=pltpu.CompilerParams(vmem_limit_bytes=8 << 20),
        name="attend",
    )(core, cached, query, new_key, new_value, residual, key_cache, value_cache)


def project_kernel(chip_ref, arrived_ref, weight_ref, out_ref, rows, context):
    for source in range(DEVS):
        rows[source * SENT : source * SENT + SENT, :] = arrived_ref[source].astype(jnp.float32)
    for head in range(HEADS):
        context[:, head * 128 : head * 128 + 128] = rows[pl.ds(head, DEVS, stride=SENT), :].astype(
            jnp.bfloat16
        )
    tokens = context[...]
    projected = last_dims(weight_ref[...], jnp.concatenate([tokens, tokens], axis=0))
    flipped = []
    for row in (ROWS, ROWS + 1):
        part = rows[pl.ds(row, DEVS, stride=SENT), :]
        flipped.append(jnp.concatenate([part, part], axis=0).T)
    rows[0:256, :] = jnp.concatenate(flipped, axis=0)
    first = pl.multiple_of(lax.rem(chip_ref[0] * COLS, 128), 32)
    hidden = rows[pl.ds(first, COLS), :] + projected
    lane = lax.broadcasted_iota(jnp.int32, (HALF, 128), 1)
    packed = jnp.where(lane < DEVS, hidden[0:HALF], hidden[HALF:COLS]).astype(jnp.bfloat16)
    for target in range(DEVS):
        out_ref[target] = packed


def project(chip, arrived, weight):
    return pl.pallas_call(
        project_kernel,
        out_shape=jax.ShapeDtypeStruct((DEVS, HALF, 128), jnp.bfloat16),
        in_specs=[SMEM_BLOCK, VMEM_BLOCK, VMEM_BLOCK],
        out_specs=VMEM_BLOCK,
        scratch_shapes=[
            pltpu.VMEM((DEVS * SENT, 128), jnp.float32),
            pltpu.VMEM((DEVS, D), jnp.bfloat16),
        ],
        compiler_params=pltpu.CompilerParams(vmem_limit_bytes=16 << 20),
        name="project",
    )(chip, arrived, weight)


def expert_kernel(
    chip_ref,
    hidden_ref,
    gain_ref,
    gate_hbm,
    up_hbm,
    down_hbm,
    out_ref,
    own_ref,
    gate_vmem,
    up_vmem,
    down_vmem,
    flipped,
    scaled,
    result,
    sems,
):
    copies = []
    for half in range(2):
        for step in range(HALF_D // CHUNK):
            part = pl.ds(step * PART, PART)
            pair = []
            for source, target, which in ((gate_hbm, gate_vmem, 0), (up_hbm, up_vmem, 1)):
                copy = pltpu.make_async_copy(
                    source.at[part, half], target.at[part, half], sems.at[which, half, step]
                )
                copy.start()
                pair.append(copy)
            copies.append(pair)
    down_copies = []
    for step in range(4):
        part = pl.ds(step * (D // 4), D // 4)
        copy = pltpu.make_async_copy(
            down_hbm.at[:, part], down_vmem.at[:, part], sems.at[2, 0, step]
        )
        copy.start()
        down_copies.append(copy)

    squares = jnp.zeros((128, 128), jnp.float32)
    for block in range(HALF_D // 128):
        lanes = slice(block * 128, block * 128 + 128)
        turned = hidden_ref[lanes, :].astype(jnp.float32).T
        flipped[:, lanes] = turned
        squares = squares + turned * turned
        gain = gain_ref[:, lanes].astype(jnp.float32)
        scaled[0:DEVS, lanes] = (turned[0:DEVS] * gain[0:1]).astype(jnp.bfloat16)
        scaled[DEVS:128, lanes] = (turned[DEVS:128] * gain[1:2]).astype(jnp.bfloat16)
    chip = chip_ref[0]
    own_ref[0:1, :] = flipped[pl.ds(chip, 1), :]
    own_ref[1:2, :] = flipped[pl.ds(chip + DEVS, 1), :]
    total = jnp.sum(squares, axis=1, keepdims=True)
    factor = lax.rsqrt((total[0:DEVS] + total[DEVS:128]) * (1.0 / D) + epsilon)

    gate = jnp.zeros((DEVS, UNITS), jnp.float32)
    up = jnp.zeros((DEVS, UNITS), jnp.float32)
    for half in range(2):
        for step in range(HALF_D // CHUNK):
            for copy in copies[half * (HALF_D // CHUNK) + step]:
                copy.wait()
            rows = scaled[half * DEVS : half * DEVS + DEVS, step * CHUNK : step * CHUNK + CHUNK]
            part = slice(step * PART, step * PART + PART)
            gate = gate + jnp.dot(
                rows,
                gate_vmem[part, half].reshape(CHUNK, UNITS),
                preferred_element_type=jnp.float32,
            )
            up = up + jnp.dot(
                rows, up_vmem[part, half].reshape(CHUNK, UNITS), preferred_element_type=jnp.float32
            )
    gate = gate * factor
    up = up * factor
    act = (gate / (1.0 + jnp.exp(-gate)) * up).astype(jnp.bfloat16)
    for step in range(4):
        down_copies[step].wait()
        for piece in range(D // 4 // 512):
            first = step * (D // 4) + piece * 512
            block = jnp.dot(
                act, down_vmem[:, first : first + 512], preferred_element_type=jnp.float32
            )
            for column in range(4):
                result[pl.ds(first // 128 + column, DEVS, stride=ROWS), :] = block[
                    :, column * 128 : column * 128 + 128
                ]
    for target in range(DEVS):
        out_ref[target] = result[target * ROWS : target * ROWS + ROWS, :].astype(jnp.bfloat16)


def run_experts(chip, hidden, gain, w_gate, w_up, w_down):
    return pl.pallas_call(
        expert_kernel,
        out_shape=(
            jax.ShapeDtypeStruct((DEVS, ROWS, 128), jnp.bfloat16),
            jax.ShapeDtypeStruct((2, HALF_D), jnp.float32),
        ),
        in_specs=[SMEM_BLOCK, VMEM_BLOCK, VMEM_BLOCK, ANY_BLOCK, ANY_BLOCK, ANY_BLOCK],
        out_specs=(VMEM_BLOCK, VMEM_BLOCK),
        scratch_shapes=[
            pltpu.VMEM((DEVS, 2, HALF, UNITS), jnp.bfloat16),
            pltpu.VMEM((DEVS, 2, HALF, UNITS), jnp.bfloat16),
            pltpu.VMEM((UNITS, D), jnp.bfloat16),
            pltpu.VMEM((128, HALF_D), jnp.float32),
            pltpu.VMEM((128, HALF_D), jnp.bfloat16),
            pltpu.VMEM((DEVS * ROWS, 128), jnp.float32),
            pltpu.SemaphoreType.DMA((3, 2, HALF_D // CHUNK)),
        ],
        compiler_params=pltpu.CompilerParams(vmem_limit_bytes=40 << 20),
        name="experts",
    )(chip, hidden, gain, w_gate, w_up, w_down)


def mix_kernel(core_ref, ids_ref, gates_ref, returned_ref, hidden_ref, kept_ref, given_ref):
    core = core_ref[0]
    total = hidden_ref[...]
    for expert in range(EXPERTS):
        share = jnp.float32(0.0)
        for choice in range(2):
            share = share + jnp.where(
                ids_ref[core, choice] == expert, gates_ref[core, choice], jnp.float32(0.0)
            )
        block = jnp.zeros((ROWS, 128), jnp.float32)
        for source in range(DEVS // EXPERTS):
            block = block + returned_ref[expert * (DEVS // EXPERTS) + source].astype(jnp.float32)
        total = total + block * share
    lower, upper = total[0 : ROWS // 2], total[ROWS // 2 : ROWS]
    kept_ref[...] = jnp.where(core == 0, lower, upper).astype(jnp.bfloat16)
    given_ref[...] = jnp.where(core == 0, upper, lower).astype(jnp.bfloat16)


def mix(core, expert_ids, gate_weights, returned, hidden):
    half = jax.ShapeDtypeStruct((ROWS // 2, 128), jnp.bfloat16)
    return pl.pallas_call(
        mix_kernel,
        out_shape=(half, half),
        in_specs=[SMEM_BLOCK, SMEM_BLOCK, SMEM_BLOCK, VMEM_BLOCK, VMEM_BLOCK],
        out_specs=(VMEM_BLOCK, VMEM_BLOCK),
        compiler_params=pltpu.CompilerParams(vmem_limit_bytes=8 << 20),
        name="mix",
    )(core, expert_ids, gate_weights, returned, hidden)


def exchange(parts):
    return lax.all_to_all(parts, "dev", split_axis=0, concat_axis=0, tiled=True)


def local(
    query,
    new_key,
    new_value,
    key_cache,
    value_cache,
    cached,
    residual,
    out_weight,
    norm_gain,
    expert_ids,
    gate_weights,
    w_gate,
    w_up,
    w_down,
):
    core = lax.axis_index("side").astype(jnp.int32).reshape(1)
    chip = lax.axis_index("dev").astype(jnp.int32).reshape(1)
    gain = norm_gain.reshape(DEVS, 2, HALF).transpose(1, 0, 2).reshape(2, HALF_D)
    outgoing = attend(
        core, cached, query, new_key, new_value, residual, key_cache, value_cache
    )
    arrived = exchange(outgoing)
    hidden = exchange(project(chip, arrived, out_weight.T)).reshape(HALF_D, 128)
    partial_value, own_hidden = run_experts(
        chip,
        hidden,
        gain,
        w_gate.reshape(DEVS, 2, HALF, UNITS),
        w_up.reshape(DEVS, 2, HALF, UNITS),
        w_down,
    )
    returned = exchange(partial_value)
    own_hidden = own_hidden.reshape(2, DEVS, HALF).transpose(1, 0, 2).reshape(ROWS, 128)
    kept, given = mix(core, expert_ids, gate_weights, returned, own_hidden)
    taken = lax.ppermute(given, "side", [(0, 1), (1, 0)])
    first = jnp.where(core == 0, kept, taken)
    second = jnp.where(core == 0, taken, kept)
    return jnp.stack([first.reshape(D // 2), second.reshape(D // 2)])


def solution(mesh):
    in_specs = (
        P("dev", None),
        P("dev", None),
        P("dev", None),
        P("dev", None, None),
        P("dev", None, None),
        P("dev"),
        P("dev", None),
        P(None, "dev"),
        P(),
        P("dev", None),
        P("dev", None),
        P(None, "dev"),
        P(None, "dev"),
        P("dev", None),
    )
    out_specs = P("dev", "side")
    return jax.shard_map(local, mesh=mesh, in_specs=in_specs, out_specs=out_specs, check_vma=False)
```

```python
import math

import jax
import jax.numpy as jnp
from jax import lax
from jax.experimental import pallas as pl
from jax.experimental.pallas import tpu as pltpu
from jax.sharding import PartitionSpec as P

D = 6144
HEADS = 48
KV_HEADS = 8
HEAD_DIM = 128
GROUP = HEADS // KV_HEADS
EXPERTS = 4
CACHE_LEN = 128
DEVS = 64
COLS = D // DEVS
HALF = COLS // 2
ROWS = D // 128
SENT = ROWS + 8
UNITS = 512
HALF_D = D // 2
CHUNK = 768
PART = CHUNK // HALF

epsilon = 1e-05

VMEM_BLOCK = pl.BlockSpec(memory_space=pltpu.VMEM)
SMEM_BLOCK = pl.BlockSpec(memory_space=pltpu.SMEM)
ANY_BLOCK = pl.BlockSpec(memory_space=pl.ANY)


def in_hbm(*arrays):
    return tuple(pltpu.with_memory_space_constraint(array, pltpu.HBM) for array in arrays)


def in_vmem(*arrays):
    return tuple(pltpu.with_memory_space_constraint(array, pltpu.VMEM) for array in arrays)


def last_dims(left, right):
    return lax.dot_general(
        left, right, (((1,), (1,)), ((), ())), preferred_element_type=jnp.float32
    )


def attend_kernel(
    core_ref,
    cached_ref,
    query_ref,
    new_key_ref,
    new_value_ref,
    residual_ref,
    key_ref,
    value_ref,
    out_ref,
    mark_ref,
    query_rows,
    context_rows,
    residual_rows,
):
    core = core_ref[0]

    def own(ref):
        both = ref[...].astype(jnp.float32)
        return jnp.where(core == 0, both[0:1], both[1:2])

    query = own(query_ref)
    new_key = own(new_key_ref)
    new_value = own(new_value_ref)
    residual = own(residual_ref)
    query_rows[...] = jnp.zeros_like(query_rows)
    for head in range(HEADS):
        row = head // GROUP * 8 + head % GROUP
        query_rows[row : row + 1, :] = query[:, head * 128 : head * 128 + 128]
    for row in range(ROWS):
        residual_rows[row : row + 1, :] = residual[:, row * 128 : row * 128 + 128]
    residual_rows[ROWS:SENT, :] = jnp.zeros((SENT - ROWS, 128), jnp.float32)
    queries = query_rows[...]
    narrow = queries.astype(jnp.bfloat16)
    scale = 1.0 / math.sqrt(HEAD_DIM)
    scores = []
    own_keys = []
    for kv in range(KV_HEADS):
        lanes = slice(kv * 128, kv * 128 + 128)
        scores.append(last_dims(narrow[kv * 8 : kv * 8 + 8], key_ref[0, :, lanes]))
        own_keys.append(jnp.broadcast_to(new_key[:, lanes], (8, 128)))
    scores = jnp.concatenate(scores, axis=0) * scale
    own_score = jnp.sum(queries * jnp.concatenate(own_keys, axis=0), axis=1, keepdims=True) * scale
    visible = lax.broadcasted_iota(jnp.int32, scores.shape, 1) < cached_ref[core]
    scores = jnp.where(visible, scores, -jnp.inf)
    highest = jnp.maximum(jnp.max(scores, axis=1, keepdims=True), own_score)
    exponents = jnp.exp(scores - highest)
    own_exp = jnp.exp(own_score - highest)
    denominator = jnp.sum(exponents, axis=1, keepdims=True) + own_exp
    weights = (exponents / denominator).astype(jnp.bfloat16)
    own_weight = (own_exp / denominator).astype(jnp.bfloat16).astype(jnp.float32)
    for kv in range(KV_HEADS):
        lanes = slice(kv * 128, kv * 128 + 128)
        context = jnp.dot(
            weights[kv * 8 : kv * 8 + 8], value_ref[0, :, lanes], preferred_element_type=jnp.float32
        )
        context = context + own_weight[kv * 8 : kv * 8 + 8] * new_value[:, lanes]
        context_rows[kv * GROUP : kv * GROUP + 8, :] = context
    context = context_rows[0:HEADS, :].astype(jnp.bfloat16)
    mark_ref[...] = context_rows[0:8, :]
    for chip in range(DEVS):
        first = COLS * chip // 128
        out_ref[chip, 0:ROWS, :] = context
        out_ref[chip, ROWS:SENT, :] = residual_rows[first : first + 8, :].astype(jnp.bfloat16)


def attend(core, cached, query, new_key, new_value, residual, key_cache, value_cache):
    def whole(shape):
        return pl.BlockSpec(shape, lambda step, core, cached: (0,) * len(shape))

    cache = pl.BlockSpec((1, CACHE_LEN, 1024), lambda step, core, cached: (core[0], 0, 0))
    return pl.pallas_call(
        attend_kernel,
        out_shape=(
            jax.ShapeDtypeStruct((DEVS, SENT, 128), jnp.bfloat16),
            jax.ShapeDtypeStruct((8, 128), jnp.float32),
        ),
        grid_spec=pltpu.PrefetchScalarGridSpec(
            num_scalar_prefetch=2,
            grid=(1,),
            in_specs=[
                whole((2, D)),
                whole((2, 1024)),
                whole((2, 1024)),
                whole((2, D)),
                cache,
                cache,
            ],
            out_specs=(whole((DEVS, SENT, 128)), whole((8, 128))),
            scratch_shapes=[
                pltpu.VMEM((64, 128), jnp.float32),
                pltpu.VMEM((SENT, 128), jnp.float32),
                pltpu.VMEM((SENT, 128), jnp.float32),
            ],
        ),
        compiler_params=pltpu.CompilerParams(vmem_limit_bytes=8 << 20),
        name="attend",
    )(core, *in_hbm(cached, query, new_key, new_value, residual, key_cache, value_cache))


def fetch_kernel(after_ref, *refs):
    count = (len(refs) - 1) // 2
    copies = [
        pltpu.make_async_copy(refs[i], refs[count + i], refs[-1].at[i]) for i in range(count)
    ]
    for copy in copies:
        copy.start()
    for copy in copies:
        copy.wait()


def fetch(after, *arrays):
    size = sum(array.size * array.dtype.itemsize for array in arrays)
    return pl.pallas_call(
        fetch_kernel,
        out_shape=tuple(pltpu.VMEM(array.shape, array.dtype) for array in arrays),
        in_specs=[ANY_BLOCK] * (len(arrays) + 1),
        out_specs=(VMEM_BLOCK,) * len(arrays),
        scratch_shapes=[pltpu.SemaphoreType.DMA((len(arrays),))],
        compiler_params=pltpu.CompilerParams(vmem_limit_bytes=1 << 20),
        cost_estimate=pl.CostEstimate(flops=0, bytes_accessed=2 * size, transcendentals=0),
        name="fetch",
    )(after, *in_hbm(*arrays))


def project_kernel(chip_ref, arrived_ref, weight_ref, out_ref, rows, context):
    for source in range(DEVS):
        rows[source * SENT : source * SENT + SENT, :] = arrived_ref[source].astype(jnp.float32)
    for head in range(HEADS):
        context[:, head * 128 : head * 128 + 128] = rows[pl.ds(head, DEVS, stride=SENT), :].astype(
            jnp.bfloat16
        )
    tokens = context[...]
    projected = last_dims(weight_ref[...], jnp.concatenate([tokens, tokens], axis=0))
    flipped = []
    for row in (ROWS, ROWS + 1):
        part = rows[pl.ds(row, DEVS, stride=SENT), :]
        flipped.append(jnp.concatenate([part, part], axis=0).T)
    rows[0:256, :] = jnp.concatenate(flipped, axis=0)
    first = pl.multiple_of(lax.rem(chip_ref[0] * COLS, 128), 32)
    hidden = rows[pl.ds(first, COLS), :] + projected
    lane = lax.broadcasted_iota(jnp.int32, (HALF, 128), 1)
    packed = jnp.where(lane < DEVS, hidden[0:HALF], hidden[HALF:COLS]).astype(jnp.bfloat16)
    for target in range(DEVS):
        out_ref[target] = packed


def project(chip, arrived, weight):
    return pl.pallas_call(
        project_kernel,
        out_shape=jax.ShapeDtypeStruct((DEVS, HALF, 128), jnp.bfloat16),
        in_specs=[SMEM_BLOCK, VMEM_BLOCK, VMEM_BLOCK],
        out_specs=VMEM_BLOCK,
        scratch_shapes=[
            pltpu.VMEM((DEVS * SENT, 128), jnp.float32),
            pltpu.VMEM((DEVS, D), jnp.bfloat16),
        ],
        compiler_params=pltpu.CompilerParams(vmem_limit_bytes=16 << 20),
        name="project",
    )(chip, arrived, *in_vmem(weight))


def expert_kernel(
    chip_ref,
    hidden_ref,
    gain_ref,
    gate_vmem,
    up_vmem,
    down_vmem,
    out_ref,
    own_ref,
    flipped,
    scaled,
    result,
):
    squares = jnp.zeros((128, 128), jnp.float32)
    for block in range(HALF_D // 128):
        lanes = slice(block * 128, block * 128 + 128)
        turned = hidden_ref[lanes, :].astype(jnp.float32).T
        flipped[:, lanes] = turned
        squares = squares + turned * turned
        gain = gain_ref[:, lanes].astype(jnp.float32)
        scaled[0:DEVS, lanes] = (turned[0:DEVS] * gain[0:1]).astype(jnp.bfloat16)
        scaled[DEVS:128, lanes] = (turned[DEVS:128] * gain[1:2]).astype(jnp.bfloat16)
    chip = chip_ref[0]
    own_ref[0:1, :] = flipped[pl.ds(chip, 1), :]
    own_ref[1:2, :] = flipped[pl.ds(chip + DEVS, 1), :]
    total = jnp.sum(squares, axis=1, keepdims=True)
    factor = lax.rsqrt((total[0:DEVS] + total[DEVS:128]) * (1.0 / D) + epsilon)

    gate = jnp.zeros((DEVS, UNITS), jnp.float32)
    up = jnp.zeros((DEVS, UNITS), jnp.float32)
    for half in range(2):
        for step in range(HALF_D // CHUNK):
            rows = scaled[half * DEVS : half * DEVS + DEVS, step * CHUNK : step * CHUNK + CHUNK]
            part = slice(step * PART, step * PART + PART)
            gate = gate + jnp.dot(
                rows,
                gate_vmem[part, half].reshape(CHUNK, UNITS),
                preferred_element_type=jnp.float32,
            )
            up = up + jnp.dot(
                rows, up_vmem[part, half].reshape(CHUNK, UNITS), preferred_element_type=jnp.float32
            )
    gate = gate * factor
    up = up * factor
    act = (gate / (1.0 + jnp.exp(-gate)) * up).astype(jnp.bfloat16)
    for step in range(4):
        for piece in range(D // 4 // 512):
            first = step * (D // 4) + piece * 512
            block = jnp.dot(
                act, down_vmem[:, first : first + 512], preferred_element_type=jnp.float32
            )
            for column in range(4):
                result[pl.ds(first // 128 + column, DEVS, stride=ROWS), :] = block[
                    :, column * 128 : column * 128 + 128
                ]
    for target in range(DEVS):
        out_ref[target] = result[target * ROWS : target * ROWS + ROWS, :].astype(jnp.bfloat16)


def run_experts(chip, hidden, gain, w_gate, w_up, w_down):
    return pl.pallas_call(
        expert_kernel,
        out_shape=(
            jax.ShapeDtypeStruct((DEVS, ROWS, 128), jnp.bfloat16),
            jax.ShapeDtypeStruct((2, HALF_D), jnp.float32),
        ),
        in_specs=[SMEM_BLOCK] + [VMEM_BLOCK] * 5,
        out_specs=(VMEM_BLOCK, VMEM_BLOCK),
        scratch_shapes=[
            pltpu.VMEM((128, HALF_D), jnp.float32),
            pltpu.VMEM((128, HALF_D), jnp.bfloat16),
            pltpu.VMEM((DEVS * ROWS, 128), jnp.float32),
        ],
        compiler_params=pltpu.CompilerParams(vmem_limit_bytes=16 << 20),
        name="experts",
    )(chip, hidden, gain, *in_vmem(w_gate, w_up, w_down))


def mix_kernel(core_ref, ids_ref, gates_ref, returned_ref, hidden_ref, kept_ref, given_ref):
    core = core_ref[0]
    total = hidden_ref[...]
    for expert in range(EXPERTS):
        share = jnp.float32(0.0)
        for choice in range(2):
            share = share + jnp.where(
                ids_ref[core, choice] == expert, gates_ref[core, choice], jnp.float32(0.0)
            )
        block = jnp.zeros((ROWS, 128), jnp.float32)
        for source in range(DEVS // EXPERTS):
            block = block + returned_ref[expert * (DEVS // EXPERTS) + source].astype(jnp.float32)
        total = total + block * share
    lower, upper = total[0 : ROWS // 2], total[ROWS // 2 : ROWS]
    kept_ref[...] = jnp.where(core == 0, lower, upper).astype(jnp.bfloat16)
    given_ref[...] = jnp.where(core == 0, upper, lower).astype(jnp.bfloat16)


def mix(core, expert_ids, gate_weights, returned, hidden):
    half = jax.ShapeDtypeStruct((ROWS // 2, 128), jnp.bfloat16)
    return pl.pallas_call(
        mix_kernel,
        out_shape=(half, half),
        in_specs=[SMEM_BLOCK, SMEM_BLOCK, SMEM_BLOCK, VMEM_BLOCK, VMEM_BLOCK],
        out_specs=(VMEM_BLOCK, VMEM_BLOCK),
        compiler_params=pltpu.CompilerParams(vmem_limit_bytes=8 << 20),
        name="mix",
    )(core, expert_ids, gate_weights, returned, hidden)


def exchange(parts):
    return lax.all_to_all(parts, "dev", split_axis=0, concat_axis=0, tiled=True)


def local(
    query,
    new_key,
    new_value,
    key_cache,
    value_cache,
    cached,
    residual,
    out_weight,
    norm_gain,
    expert_ids,
    gate_weights,
    w_gate,
    w_up,
    w_down,
):
    core = lax.axis_index("side").astype(jnp.int32).reshape(1)
    chip = lax.axis_index("dev").astype(jnp.int32).reshape(1)
    gain = norm_gain.reshape(DEVS, 2, HALF).transpose(1, 0, 2).reshape(2, HALF_D)
    outgoing, mark = attend(
        core, cached, query, new_key, new_value, residual, key_cache, value_cache
    )
    projection, gate, up, down = fetch(
        mark,
        out_weight.T,
        w_gate.reshape(DEVS, 2, HALF, UNITS),
        w_up.reshape(DEVS, 2, HALF, UNITS),
        w_down,
    )
    arrived = exchange(outgoing)
    hidden = exchange(project(chip, arrived, projection)).reshape(HALF_D, 128)
    partial_value, own_hidden = run_experts(chip, hidden, gain, gate, up, down)
    returned = exchange(partial_value)
    own_hidden = own_hidden.reshape(2, DEVS, HALF).transpose(1, 0, 2).reshape(ROWS, 128)
    kept, given = mix(core, expert_ids, gate_weights, returned, own_hidden)
    taken = lax.ppermute(given, "side", [(0, 1), (1, 0)])
    first = jnp.where(core == 0, kept, taken)
    second = jnp.where(core == 0, taken, kept)
    return jnp.stack([first.reshape(D // 2), second.reshape(D // 2)])


def solution(mesh):
    in_specs = (
        P("dev", None),
        P("dev", None),
        P("dev", None),
        P("dev", None, None),
        P("dev", None, None),
        P("dev"),
        P("dev", None),
        P(None, "dev"),
        P(),
        P("dev", None),
        P("dev", None),
        P(None, "dev"),
        P(None, "dev"),
        P("dev", None),
    )
    out_specs = P("dev", "side")
    return jax.shard_map(local, mesh=mesh, in_specs=in_specs, out_specs=out_specs, check_vma=False)
```

```python
import math

import jax
import jax.numpy as jnp
from jax import lax
from jax.experimental import pallas as pl
from jax.experimental.pallas import tpu as pltpu
from jax.sharding import PartitionSpec as P

D = 6144
HEADS = 48
KV_HEADS = 8
HEAD_DIM = 128
GROUP = HEADS // KV_HEADS
EXPERTS = 4
CACHE_LEN = 128
DEVS = 64
COLS = D // DEVS
HALF = COLS // 2
ROWS = D // 128
SENT = ROWS + 8
UNITS = 512
HALF_D = D // 2
CHUNK = 768
PART = CHUNK // HALF

epsilon = 1e-05

VMEM_BLOCK = pl.BlockSpec(memory_space=pltpu.VMEM)
SMEM_BLOCK = pl.BlockSpec(memory_space=pltpu.SMEM)
ANY_BLOCK = pl.BlockSpec(memory_space=pl.ANY)


def in_hbm(*arrays):
    return tuple(pltpu.with_memory_space_constraint(array, pltpu.HBM) for array in arrays)


def in_vmem(*arrays):
    return tuple(pltpu.with_memory_space_constraint(array, pltpu.VMEM) for array in arrays)


def last_dims(left, right):
    return lax.dot_general(
        left, right, (((1,), (1,)), ((), ())), preferred_element_type=jnp.float32
    )


def attend_kernel(
    core_ref,
    cached_ref,
    query_ref,
    new_key_ref,
    new_value_ref,
    residual_ref,
    key_ref,
    value_ref,
    out_ref,
    mark_ref,
    query_rows,
    context_rows,
    residual_rows,
):
    core = core_ref[0]

    def own(ref):
        both = ref[...].astype(jnp.float32)
        return jnp.where(core == 0, both[0:1], both[1:2])

    query = own(query_ref)
    new_key = own(new_key_ref)
    new_value = own(new_value_ref)
    residual = own(residual_ref)
    query_rows[...] = jnp.zeros_like(query_rows)
    for head in range(HEADS):
        row = head // GROUP * 8 + head % GROUP
        query_rows[row : row + 1, :] = query[:, head * 128 : head * 128 + 128]
    for row in range(ROWS):
        residual_rows[row : row + 1, :] = residual[:, row * 128 : row * 128 + 128]
    residual_rows[ROWS:SENT, :] = jnp.zeros((SENT - ROWS, 128), jnp.float32)
    queries = query_rows[...]
    narrow = queries.astype(jnp.bfloat16)
    scale = 1.0 / math.sqrt(HEAD_DIM)
    scores = []
    own_keys = []
    for kv in range(KV_HEADS):
        lanes = slice(kv * 128, kv * 128 + 128)
        scores.append(last_dims(narrow[kv * 8 : kv * 8 + 8], key_ref[0, :, lanes]))
        own_keys.append(jnp.broadcast_to(new_key[:, lanes], (8, 128)))
    scores = jnp.concatenate(scores, axis=0) * scale
    own_score = jnp.sum(queries * jnp.concatenate(own_keys, axis=0), axis=1, keepdims=True) * scale
    visible = lax.broadcasted_iota(jnp.int32, scores.shape, 1) < cached_ref[core]
    scores = jnp.where(visible, scores, -jnp.inf)
    highest = jnp.maximum(jnp.max(scores, axis=1, keepdims=True), own_score)
    exponents = jnp.exp(scores - highest)
    own_exp = jnp.exp(own_score - highest)
    denominator = jnp.sum(exponents, axis=1, keepdims=True) + own_exp
    weights = (exponents / denominator).astype(jnp.bfloat16)
    own_weight = (own_exp / denominator).astype(jnp.bfloat16).astype(jnp.float32)
    for kv in range(KV_HEADS):
        lanes = slice(kv * 128, kv * 128 + 128)
        context = jnp.dot(
            weights[kv * 8 : kv * 8 + 8], value_ref[0, :, lanes], preferred_element_type=jnp.float32
        )
        context = context + own_weight[kv * 8 : kv * 8 + 8] * new_value[:, lanes]
        context_rows[kv * GROUP : kv * GROUP + 8, :] = context
    context = context_rows[0:HEADS, :].astype(jnp.bfloat16)
    mark_ref[...] = context_rows[0:8, :]
    for chip in range(DEVS):
        first = COLS * chip // 128
        out_ref[chip, 0:ROWS, :] = context
        out_ref[chip, ROWS:SENT, :] = residual_rows[first : first + 8, :].astype(jnp.bfloat16)


def attend(core, cached, query, new_key, new_value, residual, key_cache, value_cache):
    def whole(shape):
        return pl.BlockSpec(shape, lambda step, core, cached: (0,) * len(shape))

    cache = pl.BlockSpec((1, CACHE_LEN, 1024), lambda step, core, cached: (core[0], 0, 0))
    return pl.pallas_call(
        attend_kernel,
        out_shape=(
            jax.ShapeDtypeStruct((DEVS, SENT, 128), jnp.bfloat16),
            jax.ShapeDtypeStruct((8, 128), jnp.float32),
        ),
        grid_spec=pltpu.PrefetchScalarGridSpec(
            num_scalar_prefetch=2,
            grid=(1,),
            in_specs=[
                whole((2, D)),
                whole((2, 1024)),
                whole((2, 1024)),
                whole((2, D)),
                cache,
                cache,
            ],
            out_specs=(whole((DEVS, SENT, 128)), whole((8, 128))),
            scratch_shapes=[
                pltpu.VMEM((64, 128), jnp.float32),
                pltpu.VMEM((SENT, 128), jnp.float32),
                pltpu.VMEM((SENT, 128), jnp.float32),
            ],
        ),
        compiler_params=pltpu.CompilerParams(vmem_limit_bytes=8 << 20),
        name="attend",
    )(core, *in_hbm(cached, query, new_key, new_value, residual, key_cache, value_cache))


def fetch_kernel(after_ref, *refs):
    count = (len(refs) - 1) // 2
    copies = [
        pltpu.make_async_copy(refs[i], refs[count + i], refs[-1].at[i]) for i in range(count)
    ]
    for copy in copies:
        copy.start()
    for copy in copies:
        copy.wait()


def fetch(after, *arrays):
    size = sum(array.size * array.dtype.itemsize for array in arrays)
    return pl.pallas_call(
        fetch_kernel,
        out_shape=tuple(pltpu.VMEM(array.shape, array.dtype) for array in arrays),
        in_specs=[ANY_BLOCK] * (len(arrays) + 1),
        out_specs=(VMEM_BLOCK,) * len(arrays),
        scratch_shapes=[pltpu.SemaphoreType.DMA((len(arrays),))],
        compiler_params=pltpu.CompilerParams(vmem_limit_bytes=1 << 20),
        cost_estimate=pl.CostEstimate(flops=0, bytes_accessed=2 * size, transcendentals=0),
        name="fetch",
    )(after, *in_hbm(*arrays))


def project_kernel(chip_ref, arrived_ref, weight_ref, out_ref, rows, context):
    for source in range(DEVS):
        rows[source * SENT : source * SENT + SENT, :] = arrived_ref[source].astype(jnp.float32)
    for head in range(HEADS):
        context[:, head * 128 : head * 128 + 128] = rows[pl.ds(head, DEVS, stride=SENT), :].astype(
            jnp.bfloat16
        )
    tokens = context[...]
    projected = last_dims(weight_ref[...], jnp.concatenate([tokens, tokens], axis=0))
    flipped = []
    for row in (ROWS, ROWS + 1):
        part = rows[pl.ds(row, DEVS, stride=SENT), :]
        flipped.append(jnp.concatenate([part, part], axis=0).T)
    rows[0:256, :] = jnp.concatenate(flipped, axis=0)
    first = pl.multiple_of(lax.rem(chip_ref[0] * COLS, 128), 32)
    hidden = rows[pl.ds(first, COLS), :] + projected
    lane = lax.broadcasted_iota(jnp.int32, (HALF, 128), 1)
    packed = jnp.where(lane < DEVS, hidden[0:HALF], hidden[HALF:COLS]).astype(jnp.bfloat16)
    for target in range(DEVS):
        out_ref[target] = packed


def project(chip, arrived, weight):
    return pl.pallas_call(
        project_kernel,
        out_shape=jax.ShapeDtypeStruct((DEVS, HALF, 128), jnp.bfloat16),
        in_specs=[SMEM_BLOCK, VMEM_BLOCK, VMEM_BLOCK],
        out_specs=VMEM_BLOCK,
        scratch_shapes=[
            pltpu.VMEM((DEVS * SENT, 128), jnp.float32),
            pltpu.VMEM((DEVS, D), jnp.bfloat16),
        ],
        compiler_params=pltpu.CompilerParams(vmem_limit_bytes=16 << 20),
        name="project",
    )(chip, arrived, *in_vmem(weight))


def expert_kernel(
    chip_ref,
    hidden_ref,
    gain_ref,
    gate_hbm,
    up_hbm,
    down_hbm,
    out_ref,
    own_ref,
    gate_vmem,
    up_vmem,
    down_vmem,
    flipped,
    scaled,
    result,
    sems,
):
    copies = []
    for half in range(2):
        for step in range(HALF_D // CHUNK):
            part = pl.ds(step * PART, PART)
            pair = []
            for source, target, which in ((gate_hbm, gate_vmem, 0), (up_hbm, up_vmem, 1)):
                copy = pltpu.make_async_copy(
                    source.at[part, half], target.at[part, half], sems.at[which, half, step]
                )
                copy.start()
                pair.append(copy)
            copies.append(pair)
    down_copies = []
    for step in range(4):
        part = pl.ds(step * (D // 4), D // 4)
        copy = pltpu.make_async_copy(
            down_hbm.at[:, part], down_vmem.at[:, part], sems.at[2, 0, step]
        )
        copy.start()
        down_copies.append(copy)

    squares = jnp.zeros((128, 128), jnp.float32)
    for block in range(HALF_D // 128):
        lanes = slice(block * 128, block * 128 + 128)
        turned = hidden_ref[lanes, :].astype(jnp.float32).T
        flipped[:, lanes] = turned
        squares = squares + turned * turned
        gain = gain_ref[:, lanes].astype(jnp.float32)
        scaled[0:DEVS, lanes] = (turned[0:DEVS] * gain[0:1]).astype(jnp.bfloat16)
        scaled[DEVS:128, lanes] = (turned[DEVS:128] * gain[1:2]).astype(jnp.bfloat16)
    chip = chip_ref[0]
    own_ref[0:1, :] = flipped[pl.ds(chip, 1), :]
    own_ref[1:2, :] = flipped[pl.ds(chip + DEVS, 1), :]
    total = jnp.sum(squares, axis=1, keepdims=True)
    factor = lax.rsqrt((total[0:DEVS] + total[DEVS:128]) * (1.0 / D) + epsilon)

    gate = jnp.zeros((DEVS, UNITS), jnp.float32)
    up = jnp.zeros((DEVS, UNITS), jnp.float32)
    for half in range(2):
        for step in range(HALF_D // CHUNK):
            for copy in copies[half * (HALF_D // CHUNK) + step]:
                copy.wait()
            rows = scaled[half * DEVS : half * DEVS + DEVS, step * CHUNK : step * CHUNK + CHUNK]
            part = slice(step * PART, step * PART + PART)
            gate = gate + jnp.dot(
                rows,
                gate_vmem[part, half].reshape(CHUNK, UNITS),
                preferred_element_type=jnp.float32,
            )
            up = up + jnp.dot(
                rows, up_vmem[part, half].reshape(CHUNK, UNITS), preferred_element_type=jnp.float32
            )
    gate = gate * factor
    up = up * factor
    act = (gate / (1.0 + jnp.exp(-gate)) * up).astype(jnp.bfloat16)
    for step in range(4):
        down_copies[step].wait()
        for piece in range(D // 4 // 512):
            first = step * (D // 4) + piece * 512
            block = jnp.dot(
                act, down_vmem[:, first : first + 512], preferred_element_type=jnp.float32
            )
            for column in range(4):
                result[pl.ds(first // 128 + column, DEVS, stride=ROWS), :] = block[
                    :, column * 128 : column * 128 + 128
                ]
    for target in range(DEVS):
        out_ref[target] = result[target * ROWS : target * ROWS + ROWS, :].astype(jnp.bfloat16)


def run_experts(chip, hidden, gain, w_gate, w_up, w_down):
    return pl.pallas_call(
        expert_kernel,
        out_shape=(
            jax.ShapeDtypeStruct((DEVS, ROWS, 128), jnp.bfloat16),
            jax.ShapeDtypeStruct((2, HALF_D), jnp.float32),
        ),
        in_specs=[SMEM_BLOCK, VMEM_BLOCK, VMEM_BLOCK, ANY_BLOCK, ANY_BLOCK, ANY_BLOCK],
        out_specs=(VMEM_BLOCK, VMEM_BLOCK),
        scratch_shapes=[
            pltpu.VMEM((DEVS, 2, HALF, UNITS), jnp.bfloat16),
            pltpu.VMEM((DEVS, 2, HALF, UNITS), jnp.bfloat16),
            pltpu.VMEM((UNITS, D), jnp.bfloat16),
            pltpu.VMEM((128, HALF_D), jnp.float32),
            pltpu.VMEM((128, HALF_D), jnp.bfloat16),
            pltpu.VMEM((DEVS * ROWS, 128), jnp.float32),
            pltpu.SemaphoreType.DMA((3, 2, HALF_D // CHUNK)),
        ],
        compiler_params=pltpu.CompilerParams(vmem_limit_bytes=40 << 20),
        name="experts",
    )(chip, hidden, gain, *in_hbm(w_gate, w_up, w_down))


def mix_kernel(core_ref, ids_ref, gates_ref, returned_ref, hidden_ref, kept_ref, given_ref):
    core = core_ref[0]
    total = hidden_ref[...]
    for expert in range(EXPERTS):
        share = jnp.float32(0.0)
        for choice in range(2):
            share = share + jnp.where(
                ids_ref[core, choice] == expert, gates_ref[core, choice], jnp.float32(0.0)
            )
        block = jnp.zeros((ROWS, 128), jnp.float32)
        for source in range(DEVS // EXPERTS):
            block = block + returned_ref[expert * (DEVS // EXPERTS) + source].astype(jnp.float32)
        total = total + block * share
    lower, upper = total[0 : ROWS // 2], total[ROWS // 2 : ROWS]
    kept_ref[...] = jnp.where(core == 0, lower, upper).astype(jnp.bfloat16)
    given_ref[...] = jnp.where(core == 0, upper, lower).astype(jnp.bfloat16)


def mix(core, expert_ids, gate_weights, returned, hidden):
    half = jax.ShapeDtypeStruct((ROWS // 2, 128), jnp.bfloat16)
    return pl.pallas_call(
        mix_kernel,
        out_shape=(half, half),
        in_specs=[SMEM_BLOCK, SMEM_BLOCK, SMEM_BLOCK, VMEM_BLOCK, VMEM_BLOCK],
        out_specs=(VMEM_BLOCK, VMEM_BLOCK),
        compiler_params=pltpu.CompilerParams(vmem_limit_bytes=8 << 20),
        name="mix",
    )(core, expert_ids, gate_weights, returned, hidden)


def exchange(parts):
    return lax.all_to_all(parts, "dev", split_axis=0, concat_axis=0, tiled=True)


def local(
    query,
    new_key,
    new_value,
    key_cache,
    value_cache,
    cached,
    residual,
    out_weight,
    norm_gain,
    expert_ids,
    gate_weights,
    w_gate,
    w_up,
    w_down,
):
    core = lax.axis_index("side").astype(jnp.int32).reshape(1)
    chip = lax.axis_index("dev").astype(jnp.int32).reshape(1)
    outgoing, mark = attend(
        core, cached, query, new_key, new_value, residual, key_cache, value_cache
    )
    norm_gain, mark = lax.optimization_barrier((norm_gain, mark))
    gain = norm_gain.reshape(DEVS, 2, HALF).transpose(1, 0, 2).reshape(2, HALF_D)
    (projection,) = fetch(mark, out_weight.T)
    arrived = exchange(outgoing)
    hidden = exchange(project(chip, arrived, projection)).reshape(HALF_D, 128)
    partial_value, own_hidden = run_experts(
        chip,
        hidden,
        gain,
        w_gate.reshape(DEVS, 2, HALF, UNITS),
        w_up.reshape(DEVS, 2, HALF, UNITS),
        w_down,
    )
    returned = exchange(partial_value)
    own_hidden = own_hidden.reshape(2, DEVS, HALF).transpose(1, 0, 2).reshape(ROWS, 128)
    kept, given = mix(core, expert_ids, gate_weights, returned, own_hidden)
    taken = lax.ppermute(given, "side", [(0, 1), (1, 0)])
    first = jnp.where(core == 0, kept, taken)
    second = jnp.where(core == 0, taken, kept)
    return jnp.stack([first.reshape(D // 2), second.reshape(D // 2)])


def solution(mesh):
    in_specs = (
        P("dev", None),
        P("dev", None),
        P("dev", None),
        P("dev", None, None),
        P("dev", None, None),
        P("dev"),
        P("dev", None),
        P(None, "dev"),
        P(),
        P("dev", None),
        P("dev", None),
        P(None, "dev"),
        P(None, "dev"),
        P("dev", None),
    )
    out_specs = P("dev", "side")
    return jax.shard_map(local, mesh=mesh, in_specs=in_specs, out_specs=out_specs, check_vma=False)
```

```python
import math

import jax
import jax.numpy as jnp
from jax import lax
from jax.experimental import pallas as pl
from jax.experimental.pallas import tpu as pltpu
from jax.sharding import PartitionSpec as P

D = 6144
HEADS = 48
KV_HEADS = 8
HEAD_DIM = 128
GROUP = HEADS // KV_HEADS
EXPERTS = 4
CACHE_LEN = 128
DEVS = 64
COLS = D // DEVS
HALF = COLS // 2
ROWS = D // 128
SENT = ROWS + 8
UNITS = 512
HALF_D = D // 2
CHUNK = 768
PART = CHUNK // HALF
EARLY = 3

epsilon = 1e-05

VMEM_BLOCK = pl.BlockSpec(memory_space=pltpu.VMEM)
SMEM_BLOCK = pl.BlockSpec(memory_space=pltpu.SMEM)
ANY_BLOCK = pl.BlockSpec(memory_space=pl.ANY)


def in_hbm(*arrays):
    return tuple(pltpu.with_memory_space_constraint(array, pltpu.HBM) for array in arrays)


def in_vmem(*arrays):
    return tuple(pltpu.with_memory_space_constraint(array, pltpu.VMEM) for array in arrays)


def last_dims(left, right):
    return lax.dot_general(
        left, right, (((1,), (1,)), ((), ())), preferred_element_type=jnp.float32
    )


def attend_kernel(
    core_ref,
    cached_ref,
    query_ref,
    new_key_ref,
    new_value_ref,
    residual_ref,
    key_ref,
    value_ref,
    out_ref,
    mark_ref,
    query_rows,
    context_rows,
    residual_rows,
):
    core = core_ref[0]

    def own(ref):
        both = ref[...].astype(jnp.float32)
        return jnp.where(core == 0, both[0:1], both[1:2])

    query = own(query_ref)
    new_key = own(new_key_ref)
    new_value = own(new_value_ref)
    residual = own(residual_ref)
    query_rows[...] = jnp.zeros_like(query_rows)
    for head in range(HEADS):
        row = head // GROUP * 8 + head % GROUP
        query_rows[row : row + 1, :] = query[:, head * 128 : head * 128 + 128]
    for row in range(ROWS):
        residual_rows[row : row + 1, :] = residual[:, row * 128 : row * 128 + 128]
    residual_rows[ROWS:SENT, :] = jnp.zeros((SENT - ROWS, 128), jnp.float32)
    queries = query_rows[...]
    narrow = queries.astype(jnp.bfloat16)
    scale = 1.0 / math.sqrt(HEAD_DIM)
    scores = []
    own_keys = []
    for kv in range(KV_HEADS):
        lanes = slice(kv * 128, kv * 128 + 128)
        scores.append(last_dims(narrow[kv * 8 : kv * 8 + 8], key_ref[0, :, lanes]))
        own_keys.append(jnp.broadcast_to(new_key[:, lanes], (8, 128)))
    scores = jnp.concatenate(scores, axis=0) * scale
    own_score = jnp.sum(queries * jnp.concatenate(own_keys, axis=0), axis=1, keepdims=True) * scale
    visible = lax.broadcasted_iota(jnp.int32, scores.shape, 1) < cached_ref[core]
    scores = jnp.where(visible, scores, -jnp.inf)
    highest = jnp.maximum(jnp.max(scores, axis=1, keepdims=True), own_score)
    exponents = jnp.exp(scores - highest)
    own_exp = jnp.exp(own_score - highest)
    denominator = jnp.sum(exponents, axis=1, keepdims=True) + own_exp
    weights = (exponents / denominator).astype(jnp.bfloat16)
    own_weight = (own_exp / denominator).astype(jnp.bfloat16).astype(jnp.float32)
    for kv in range(KV_HEADS):
        lanes = slice(kv * 128, kv * 128 + 128)
        context = jnp.dot(
            weights[kv * 8 : kv * 8 + 8], value_ref[0, :, lanes], preferred_element_type=jnp.float32
        )
        context = context + own_weight[kv * 8 : kv * 8 + 8] * new_value[:, lanes]
        context_rows[kv * GROUP : kv * GROUP + 8, :] = context
    context = context_rows[0:HEADS, :].astype(jnp.bfloat16)
    mark_ref[...] = context_rows[0:8, :]
    for chip in range(DEVS):
        first = COLS * chip // 128
        out_ref[chip, 0:ROWS, :] = context
        out_ref[chip, ROWS:SENT, :] = residual_rows[first : first + 8, :].astype(jnp.bfloat16)


def attend(core, cached, query, new_key, new_value, residual, key_cache, value_cache):
    def whole(shape):
        return pl.BlockSpec(shape, lambda step, core, cached: (0,) * len(shape))

    cache = pl.BlockSpec((1, CACHE_LEN, 1024), lambda step, core, cached: (core[0], 0, 0))
    return pl.pallas_call(
        attend_kernel,
        out_shape=(
            jax.ShapeDtypeStruct((DEVS, SENT, 128), jnp.bfloat16),
            jax.ShapeDtypeStruct((8, 128), jnp.float32),
        ),
        grid_spec=pltpu.PrefetchScalarGridSpec(
            num_scalar_prefetch=2,
            grid=(1,),
            in_specs=[
                whole((2, D)),
                whole((2, 1024)),
                whole((2, 1024)),
                whole((2, D)),
                cache,
                cache,
            ],
            out_specs=(whole((DEVS, SENT, 128)), whole((8, 128))),
            scratch_shapes=[
                pltpu.VMEM((64, 128), jnp.float32),
                pltpu.VMEM((SENT, 128), jnp.float32),
                pltpu.VMEM((SENT, 128), jnp.float32),
            ],
        ),
        compiler_params=pltpu.CompilerParams(vmem_limit_bytes=8 << 20),
        name="attend",
    )(core, *in_hbm(cached, query, new_key, new_value, residual, key_cache, value_cache))


def fetch_kernel(after_ref, *refs):
    count = (len(refs) - 1) // 2
    copies = [
        pltpu.make_async_copy(refs[i], refs[count + i], refs[-1].at[i]) for i in range(count)
    ]
    for copy in copies:
        copy.start()
    for copy in copies:
        copy.wait()


def fetch(after, *arrays):
    size = sum(array.size * array.dtype.itemsize for array in arrays)
    return pl.pallas_call(
        fetch_kernel,
        out_shape=tuple(pltpu.VMEM(array.shape, array.dtype) for array in arrays),
        in_specs=[ANY_BLOCK] * (len(arrays) + 1),
        out_specs=(VMEM_BLOCK,) * len(arrays),
        scratch_shapes=[pltpu.SemaphoreType.DMA((len(arrays),))],
        compiler_params=pltpu.CompilerParams(vmem_limit_bytes=1 << 20),
        cost_estimate=pl.CostEstimate(flops=0, bytes_accessed=2 * size, transcendentals=0),
        name="fetch",
    )(after, *in_hbm(*arrays))


def early_kernel(after_ref, gate_hbm, out_ref, sems):
    copies = [
        pltpu.make_async_copy(
            gate_hbm.at[pl.ds(step * PART, PART), 0], out_ref.at[step], sems.at[step]
        )
        for step in range(EARLY)
    ]
    for copy in copies:
        copy.start()
    for copy in copies:
        copy.wait()


def fetch_early(after, w_gate):
    return pl.pallas_call(
        early_kernel,
        out_shape=pltpu.VMEM((EARLY, PART, HALF, UNITS), w_gate.dtype),
        in_specs=[ANY_BLOCK] * 2,
        out_specs=VMEM_BLOCK,
        scratch_shapes=[pltpu.SemaphoreType.DMA((EARLY,))],
        compiler_params=pltpu.CompilerParams(vmem_limit_bytes=1 << 20),
        name="fetch_early",
    )(after, *in_hbm(w_gate))


def half_kernel(core_ref, after_ref, down_hbm, out_ref, sems):
    first = core_ref[0] * HALF_D
    copies = [
        pltpu.make_async_copy(
            down_hbm.at[pl.ds(step * 128, 128), pl.ds(pl.multiple_of(first, HALF_D), HALF_D)],
            out_ref.at[pl.ds(step * 128, 128)],
            sems.at[step],
        )
        for step in range(4)
    ]
    for copy in copies:
        copy.start()
    for copy in copies:
        copy.wait()


def fetch_half(core, after, w_down):
    return pl.pallas_call(
        half_kernel,
        out_shape=pltpu.VMEM((UNITS, HALF_D), w_down.dtype),
        in_specs=[SMEM_BLOCK, ANY_BLOCK, ANY_BLOCK],
        out_specs=VMEM_BLOCK,
        scratch_shapes=[pltpu.SemaphoreType.DMA((4,))],
        compiler_params=pltpu.CompilerParams(vmem_limit_bytes=1 << 20),
        name="fetch_half",
    )(core, after, *in_hbm(w_down))


def project_kernel(chip_ref, arrived_ref, weight_ref, out_ref, mark_ref, rows, context):
    for source in range(DEVS):
        rows[source * SENT : source * SENT + SENT, :] = arrived_ref[source].astype(jnp.float32)
    for head in range(HEADS):
        context[:, head * 128 : head * 128 + 128] = rows[pl.ds(head, DEVS, stride=SENT), :].astype(
            jnp.bfloat16
        )
    tokens = context[...]
    projected = last_dims(weight_ref[...], jnp.concatenate([tokens, tokens], axis=0))
    flipped = []
    for row in (ROWS, ROWS + 1):
        part = rows[pl.ds(row, DEVS, stride=SENT), :]
        flipped.append(jnp.concatenate([part, part], axis=0).T)
    rows[0:256, :] = jnp.concatenate(flipped, axis=0)
    first = pl.multiple_of(lax.rem(chip_ref[0] * COLS, 128), 32)
    hidden = rows[pl.ds(first, COLS), :] + projected
    lane = lax.broadcasted_iota(jnp.int32, (HALF, 128), 1)
    packed = jnp.where(lane < DEVS, hidden[0:HALF], hidden[HALF:COLS]).astype(jnp.bfloat16)
    mark_ref[...] = hidden[0:8]
    for target in range(DEVS):
        out_ref[target] = packed


def project(chip, arrived, weight):
    return pl.pallas_call(
        project_kernel,
        out_shape=(
            jax.ShapeDtypeStruct((DEVS, HALF, 128), jnp.bfloat16),
            jax.ShapeDtypeStruct((8, 128), jnp.float32),
        ),
        in_specs=[SMEM_BLOCK, VMEM_BLOCK, VMEM_BLOCK],
        out_specs=(VMEM_BLOCK, VMEM_BLOCK),
        scratch_shapes=[
            pltpu.VMEM((DEVS * SENT, 128), jnp.float32),
            pltpu.VMEM((DEVS, D), jnp.bfloat16),
        ],
        compiler_params=pltpu.CompilerParams(vmem_limit_bytes=16 << 20),
        name="project",
    )(chip, arrived, *in_vmem(weight))


def expert_kernel(
    chip_ref,
    hidden_ref,
    gain_ref,
    early_ref,
    gate_hbm,
    up_hbm,
    act_ref,
    own_ref,
    gate_vmem,
    up_vmem,
    flipped,
    scaled,
    sems,
):
    pieces = [(half, step) for half in range(2) for step in range(HALF_D // CHUNK)]
    copies = {}
    for index, (half, step) in enumerate(pieces):
        part = pl.ds(step * PART, PART)
        for which, source, target in ((0, gate_hbm, gate_vmem), (1, up_hbm, up_vmem)):
            if which == 0 and index < EARLY:
                continue
            copies[which, index] = pltpu.make_async_copy(
                source.at[part, half], target.at[part, half], sems.at[which, index]
            )
    for index in range(EARLY, len(pieces)):
        copies[0, index].start()
        copies[1, index].start()
    for index in range(EARLY):
        copies[1, index].start()

    squares = jnp.zeros((128, 128), jnp.float32)
    for block in range(HALF_D // 128):
        lanes = slice(block * 128, block * 128 + 128)
        turned = hidden_ref[lanes, :].astype(jnp.float32).T
        flipped[:, lanes] = turned
        squares = squares + turned * turned
        gain = gain_ref[:, lanes].astype(jnp.float32)
        scaled[0:DEVS, lanes] = (turned[0:DEVS] * gain[0:1]).astype(jnp.bfloat16)
        scaled[DEVS:128, lanes] = (turned[DEVS:128] * gain[1:2]).astype(jnp.bfloat16)
    chip = chip_ref[0]
    own_ref[0:1, :] = flipped[pl.ds(chip, 1), :]
    own_ref[1:2, :] = flipped[pl.ds(chip + DEVS, 1), :]
    total = jnp.sum(squares, axis=1, keepdims=True)
    factor = lax.rsqrt((total[0:DEVS] + total[DEVS:128]) * (1.0 / D) + epsilon)

    gate = jnp.zeros((DEVS, UNITS), jnp.float32)
    up = jnp.zeros((DEVS, UNITS), jnp.float32)

    def product(index, weights):
        half, step = pieces[index]
        rows = scaled[half * DEVS : half * DEVS + DEVS, step * CHUNK : step * CHUNK + CHUNK]
        return jnp.dot(rows, weights.reshape(CHUNK, UNITS), preferred_element_type=jnp.float32)

    def part_of(ref, index):
        half, step = pieces[index]
        return ref[step * PART : step * PART + PART, half]

    for index in range(EARLY):
        gate = gate + product(index, early_ref[index])
    for index in list(range(EARLY, len(pieces))) + list(range(EARLY)):
        if index >= EARLY:
            copies[0, index].wait()
            gate = gate + product(index, part_of(gate_vmem, index))
        copies[1, index].wait()
        up = up + product(index, part_of(up_vmem, index))
    gate = gate * factor
    up = up * factor
    act_ref[...] = (gate / (1.0 + jnp.exp(-gate)) * up).astype(jnp.bfloat16)


def expert_units(chip, hidden, gain, early, w_gate, w_up):
    return pl.pallas_call(
        expert_kernel,
        out_shape=(
            jax.ShapeDtypeStruct((DEVS, UNITS), jnp.bfloat16),
            jax.ShapeDtypeStruct((2, HALF_D), jnp.float32),
        ),
        in_specs=[SMEM_BLOCK, VMEM_BLOCK, VMEM_BLOCK, VMEM_BLOCK, ANY_BLOCK, ANY_BLOCK],
        out_specs=(VMEM_BLOCK, VMEM_BLOCK),
        scratch_shapes=[
            pltpu.VMEM((DEVS, 2, HALF, UNITS), jnp.bfloat16),
            pltpu.VMEM((DEVS, 2, HALF, UNITS), jnp.bfloat16),
            pltpu.VMEM((128, HALF_D), jnp.float32),
            pltpu.VMEM((128, HALF_D), jnp.bfloat16),
            pltpu.SemaphoreType.DMA((2, 2 * HALF_D // CHUNK)),
        ],
        compiler_params=pltpu.CompilerParams(vmem_limit_bytes=24 << 20),
        name="expert_units",
    )(chip, hidden, gain, *in_vmem(early), *in_hbm(w_gate, w_up))


def down_kernel(core_ref, act_ref, other_ref, down_ref, out_ref, both, result):
    core = core_ref[0]
    both[pl.ds(pl.multiple_of(core * DEVS, DEVS), DEVS), :] = act_ref[...]
    both[pl.ds(pl.multiple_of((1 - core) * DEVS, DEVS), DEVS), :] = other_ref[...]
    act = both[...]
    for first in range(0, HALF_D, 512):
        block = jnp.dot(act, down_ref[:, first : first + 512], preferred_element_type=jnp.float32)
        for column in range(4):
            row = first // 128 + column
            lanes = slice(column * 128, column * 128 + 128)
            result[pl.ds(row, DEVS, stride=ROWS), :] = block[0:DEVS, lanes]
            result[pl.ds(row + ROWS // 2, DEVS, stride=ROWS), :] = block[DEVS:128, lanes]
    for target in range(DEVS):
        out_ref[target] = result[target * ROWS : target * ROWS + ROWS, :].astype(jnp.bfloat16)


def expert_down(core, act, other, w_down):
    return pl.pallas_call(
        down_kernel,
        out_shape=jax.ShapeDtypeStruct((DEVS, ROWS, 128), jnp.bfloat16),
        in_specs=[SMEM_BLOCK, VMEM_BLOCK, VMEM_BLOCK, VMEM_BLOCK],
        out_specs=VMEM_BLOCK,
        scratch_shapes=[
            pltpu.VMEM((128, UNITS), jnp.bfloat16),
            pltpu.VMEM((DEVS * ROWS, 128), jnp.float32),
        ],
        compiler_params=pltpu.CompilerParams(vmem_limit_bytes=16 << 20),
        name="expert_down",
    )(core, act, other, *in_vmem(w_down))


def mix_kernel(core_ref, ids_ref, gates_ref, returned_ref, kept_ref, taken_ref, out_ref, rows):
    core = core_ref[0]
    half = ROWS // 2
    kept, taken = kept_ref[...], taken_ref[...]
    totals = [jnp.where(core == 0, kept, taken), jnp.where(core == 0, taken, kept)]
    for expert in range(EXPERTS):
        block = jnp.zeros((ROWS, 128), jnp.float32)
        for source in range(DEVS // EXPERTS):
            block = block + returned_ref[expert * (DEVS // EXPERTS) + source].astype(jnp.float32)
        for token in range(2):
            share = jnp.float32(0.0)
            for choice in range(2):
                share = share + jnp.where(
                    ids_ref[token, choice] == expert, gates_ref[token, choice], jnp.float32(0.0)
                )
            totals[token] = totals[token] + block[token * half : token * half + half] * share
    for token in range(2):
        for row in range(half):
            rows[token : token + 1, row * 128 : row * 128 + 128] = totals[token][row : row + 1]
    out_ref[...] = rows[...].astype(jnp.bfloat16)


def mix(core, expert_ids, gate_weights, returned, kept, taken):
    return pl.pallas_call(
        mix_kernel,
        out_shape=jax.ShapeDtypeStruct((2, HALF_D), jnp.bfloat16),
        in_specs=[SMEM_BLOCK, SMEM_BLOCK, SMEM_BLOCK, VMEM_BLOCK, VMEM_BLOCK, VMEM_BLOCK],
        out_specs=VMEM_BLOCK,
        scratch_shapes=[pltpu.VMEM((2, HALF_D), jnp.float32)],
        compiler_params=pltpu.CompilerParams(vmem_limit_bytes=8 << 20),
        name="mix",
    )(core, expert_ids, gate_weights, returned, kept, taken)


def exchange(parts):
    return lax.all_to_all(parts, "dev", split_axis=0, concat_axis=0, tiled=True)


def swap(value):
    return lax.ppermute(value, "side", [(0, 1), (1, 0)])


def local(
    query,
    new_key,
    new_value,
    key_cache,
    value_cache,
    cached,
    residual,
    out_weight,
    norm_gain,
    expert_ids,
    gate_weights,
    w_gate,
    w_up,
    w_down,
):
    core = lax.axis_index("side").astype(jnp.int32).reshape(1)
    chip = lax.axis_index("dev").astype(jnp.int32).reshape(1)
    outgoing, mark = attend(
        core, cached, query, new_key, new_value, residual, key_cache, value_cache
    )
    norm_gain, mark = lax.optimization_barrier((norm_gain, mark))
    gain = norm_gain.reshape(DEVS, 2, HALF).transpose(1, 0, 2).reshape(2, HALF_D)
    (projection,) = fetch(mark, out_weight.T)
    arrived = exchange(outgoing)
    packed, mark = project(chip, arrived, projection)
    w_gate = w_gate.reshape(DEVS, 2, HALF, UNITS)
    w_up = w_up.reshape(DEVS, 2, HALF, UNITS)
    early = fetch_early(mark, w_gate)
    hidden = exchange(packed).reshape(HALF_D, 128)
    act, own_hidden = expert_units(chip, hidden, gain, early, w_gate, w_up)
    down = fetch_half(core, own_hidden, w_down)
    partial_value = expert_down(core, act, swap(act), down)
    returned = exchange(partial_value)
    halves = own_hidden.reshape(2, DEVS, HALF).transpose(1, 0, 2).reshape(2, ROWS // 2, 128)
    kept = lax.dynamic_index_in_dim(halves, core[0], 0, keepdims=False)
    given = lax.dynamic_index_in_dim(halves, 1 - core[0], 0, keepdims=False)
    return mix(core, expert_ids, gate_weights, returned, kept, swap(given))


def solution(mesh):
    in_specs = (
        P("dev", None),
        P("dev", None),
        P("dev", None),
        P("dev", None, None),
        P("dev", None, None),
        P("dev"),
        P("dev", None),
        P(None, "dev"),
        P(),
        P("dev", None),
        P("dev", None),
        P(None, "dev"),
        P(None, "dev"),
        P("dev", None),
    )
    out_specs = P("dev", "side")
    return jax.shard_map(local, mesh=mesh, in_specs=in_specs, out_specs=out_specs, check_vma=False)
```

```python
import math

import jax
import jax.numpy as jnp
from jax import lax
from jax.experimental import pallas as pl
from jax.experimental.pallas import tpu as pltpu
from jax.sharding import PartitionSpec as P

D = 6144
HEADS = 48
KV_HEADS = 8
HEAD_DIM = 128
GROUP = HEADS // KV_HEADS
EXPERTS = 4
CACHE_LEN = 128
DEVS = 64
COLS = D // DEVS
HALF = COLS // 2
ROWS = D // 128
SENT = ROWS + 2
BATCH = 8
UNITS = 512
HALF_D = D // 2
CHUNK = 768
PART = CHUNK // HALF
STEPS = HALF_D // CHUNK
EARLY = 3
DOWN = 1024

epsilon = 1e-05

VMEM_BLOCK = pl.BlockSpec(memory_space=pltpu.VMEM)
SMEM_BLOCK = pl.BlockSpec(memory_space=pltpu.SMEM)
ANY_BLOCK = pl.BlockSpec(memory_space=pl.ANY)


def in_hbm(*arrays):
    return tuple(pltpu.with_memory_space_constraint(array, pltpu.HBM) for array in arrays)


def in_vmem(*arrays):
    return tuple(pltpu.with_memory_space_constraint(array, pltpu.VMEM) for array in arrays)


def last_dims(left, right):
    return lax.dot_general(
        left, right, (((1,), (1,)), ((), ())), preferred_element_type=jnp.float32
    )


def attend_kernel(
    core_ref,
    cached_ref,
    query_ref,
    new_key_ref,
    new_value_ref,
    residual_ref,
    key_ref,
    value_ref,
    out_ref,
    mark_ref,
    query_rows,
    residual_rows,
    context_rows,
    pattern,
):
    core = core_ref[0]
    first_row = pl.multiple_of(core * 64, 64)

    def own(ref):
        both = ref[...].astype(jnp.float32)
        return jnp.where(core == 0, both[0:1], both[1:2])

    query_rows[...] = jnp.zeros_like(query_rows)
    residual_rows[...] = jnp.zeros_like(residual_rows)
    both = query_ref[...].astype(jnp.float32)
    for head in range(HEADS):
        row = head // GROUP * 8 + head % GROUP
        query_rows[pl.ds(row, 2, stride=64), :] = both[:, head * 128 : head * 128 + 128]
    both = residual_ref[...].astype(jnp.float32)
    for row in range(ROWS):
        residual_rows[pl.ds(row, 2, stride=64), :] = both[:, row * 128 : row * 128 + 128]
    queries = query_rows[pl.ds(first_row, 64), :]
    narrow = queries.astype(jnp.bfloat16)
    new_key = own(new_key_ref)
    new_value = own(new_value_ref)
    scale = 1.0 / math.sqrt(HEAD_DIM)
    scores = []
    own_keys = []
    for kv in range(KV_HEADS):
        lanes = slice(kv * 128, kv * 128 + 128)
        scores.append(last_dims(narrow[kv * 8 : kv * 8 + 8], key_ref[0, :, lanes]))
        own_keys.append(jnp.broadcast_to(new_key[:, lanes], (8, 128)))
    scores = jnp.concatenate(scores, axis=0) * scale
    own_score = jnp.sum(queries * jnp.concatenate(own_keys, axis=0), axis=1, keepdims=True) * scale
    visible = lax.broadcasted_iota(jnp.int32, scores.shape, 1) < cached_ref[core]
    scores = jnp.where(visible, scores, -jnp.inf)
    highest = jnp.maximum(jnp.max(scores, axis=1, keepdims=True), own_score)
    exponents = jnp.exp(scores - highest)
    own_exp = jnp.exp(own_score - highest)
    denominator = jnp.sum(exponents, axis=1, keepdims=True) + own_exp
    weights = (exponents / denominator).astype(jnp.bfloat16)
    own_weight = (own_exp / denominator).astype(jnp.bfloat16).astype(jnp.float32)
    for kv in range(KV_HEADS):
        lanes = slice(kv * 128, kv * 128 + 128)
        context = jnp.dot(
            weights[kv * 8 : kv * 8 + 8], value_ref[0, :, lanes], preferred_element_type=jnp.float32
        )
        context = context + own_weight[kv * 8 : kv * 8 + 8] * new_value[:, lanes]
        context_rows[kv * GROUP : kv * GROUP + 8, :] = context
    context = context_rows[0:ROWS, :]
    mark_ref[...] = context[0:8]
    for chip in range(BATCH):
        pattern[chip * SENT : chip * SENT + ROWS, :] = context
    for group in range(DEVS // BATCH):
        for chip in range(BATCH):
            wanted = COLS * (group * BATCH + chip) // 128
            pattern[chip * SENT + ROWS : chip * SENT + SENT, :] = residual_rows[
                pl.ds(first_row + wanted, 2), :
            ]
        first = group * BATCH * SENT
        out_ref[first : first + BATCH * SENT, :] = pattern[...].astype(jnp.bfloat16)


def attend(core, cached, query, new_key, new_value, residual, key_cache, value_cache):
    def whole(shape):
        return pl.BlockSpec(shape, lambda step, core, cached: (0,) * len(shape))

    cache = pl.BlockSpec((1, CACHE_LEN, 1024), lambda step, core, cached: (core[0], 0, 0))
    return pl.pallas_call(
        attend_kernel,
        out_shape=(
            jax.ShapeDtypeStruct((DEVS * SENT, 128), jnp.bfloat16),
            jax.ShapeDtypeStruct((8, 128), jnp.float32),
        ),
        grid_spec=pltpu.PrefetchScalarGridSpec(
            num_scalar_prefetch=2,
            grid=(1,),
            in_specs=[
                whole((2, D)),
                whole((2, 1024)),
                whole((2, 1024)),
                whole((2, D)),
                cache,
                cache,
            ],
            out_specs=(whole((DEVS * SENT, 128)), whole((8, 128))),
            scratch_shapes=[
                pltpu.VMEM((128, 128), jnp.float32),
                pltpu.VMEM((128, 128), jnp.float32),
                pltpu.VMEM((ROWS + 8, 128), jnp.float32),
                pltpu.VMEM((BATCH * SENT, 128), jnp.float32),
            ],
        ),
        compiler_params=pltpu.CompilerParams(vmem_limit_bytes=8 << 20),
        name="attend",
    )(core, *in_hbm(cached, query, new_key, new_value, residual, key_cache, value_cache))


def fetch_kernel(after_ref, *refs):
    count = (len(refs) - 1) // 2
    copies = [
        pltpu.make_async_copy(refs[i], refs[count + i], refs[-1].at[i]) for i in range(count)
    ]
    for copy in copies:
        copy.start()
    for copy in copies:
        copy.wait()


def fetch(after, *arrays):
    size = sum(array.size * array.dtype.itemsize for array in arrays)
    return pl.pallas_call(
        fetch_kernel,
        out_shape=tuple(pltpu.VMEM(array.shape, array.dtype) for array in arrays),
        in_specs=[ANY_BLOCK] * (len(arrays) + 1),
        out_specs=(VMEM_BLOCK,) * len(arrays),
        scratch_shapes=[pltpu.SemaphoreType.DMA((len(arrays),))],
        compiler_params=pltpu.CompilerParams(vmem_limit_bytes=1 << 20),
        cost_estimate=pl.CostEstimate(flops=0, bytes_accessed=2 * size, transcendentals=0),
        name="fetch",
    )(after, *in_hbm(*arrays))


def project_kernel(chip_ref, arrived_ref, weight_ref, out_ref, mark_ref, rows, context):
    for source in range(0, DEVS * SENT, 400):
        rows[source : source + 400, :] = arrived_ref[source : source + 400, :].astype(jnp.float32)
    for head in range(HEADS):
        context[:, head * 128 : head * 128 + 128] = rows[pl.ds(head, DEVS, stride=SENT), :].astype(
            jnp.bfloat16
        )
    tokens = context[...]
    projected = last_dims(weight_ref[...], jnp.concatenate([tokens, tokens], axis=0))
    flipped = []
    for row in (ROWS, ROWS + 1):
        part = rows[pl.ds(row, DEVS, stride=SENT), :]
        flipped.append(jnp.concatenate([part, part], axis=0).T)
    rows[0:256, :] = jnp.concatenate(flipped, axis=0)
    first = pl.multiple_of(lax.rem(chip_ref[0] * COLS, 128), 32)
    hidden = rows[pl.ds(first, COLS), :] + projected
    lane = lax.broadcasted_iota(jnp.int32, (HALF, 128), 1)
    packed = jnp.where(lane < DEVS, hidden[0:HALF], hidden[HALF:COLS]).astype(jnp.bfloat16)
    mark_ref[...] = hidden[0:8]
    for target in range(DEVS):
        out_ref[target] = packed


def project(chip, arrived, weight):
    return pl.pallas_call(
        project_kernel,
        out_shape=(
            jax.ShapeDtypeStruct((DEVS, HALF, 128), jnp.bfloat16),
            jax.ShapeDtypeStruct((8, 128), jnp.float32),
        ),
        in_specs=[SMEM_BLOCK, VMEM_BLOCK, VMEM_BLOCK],
        out_specs=(VMEM_BLOCK, VMEM_BLOCK),
        scratch_shapes=[
            pltpu.VMEM((DEVS * SENT, 128), jnp.float32),
            pltpu.VMEM((DEVS, D), jnp.bfloat16),
        ],
        compiler_params=pltpu.CompilerParams(vmem_limit_bytes=16 << 20),
        name="project",
    )(chip, arrived, *in_vmem(weight))


def early_kernel(after_ref, gate_hbm, out_ref, sems):
    copies = [
        pltpu.make_async_copy(
            gate_hbm.at[pl.ds(step * PART, PART), 0], out_ref.at[step], sems.at[step]
        )
        for step in range(EARLY)
    ]
    for copy in copies:
        copy.start()
    for copy in copies:
        copy.wait()


def fetch_early(after, w_gate):
    return pl.pallas_call(
        early_kernel,
        out_shape=pltpu.VMEM((EARLY, PART, HALF, UNITS), w_gate.dtype),
        in_specs=[ANY_BLOCK] * 2,
        out_specs=VMEM_BLOCK,
        scratch_shapes=[pltpu.SemaphoreType.DMA((EARLY,))],
        compiler_params=pltpu.CompilerParams(vmem_limit_bytes=1 << 20),
        name="fetch_early",
    )(after, *in_hbm(w_gate))


def expert_kernel(
    chip_ref,
    hidden_ref,
    gain_ref,
    early_ref,
    gate_hbm,
    up_hbm,
    down_hbm,
    out_ref,
    own_ref,
    gate_vmem,
    up_vmem,
    down_vmem,
    flipped,
    scaled,
    result,
    sems,
):
    pieces = [(half, step) for half in range(2) for step in range(STEPS)]
    order = list(range(EARLY, len(pieces))) + list(range(EARLY))
    copies = {}
    for index in order:
        half, step = pieces[index]
        part = pl.ds(step * PART, PART)
        for which, source, target in ((0, gate_hbm, gate_vmem), (1, up_hbm, up_vmem)):
            if which == 1 or index >= EARLY:
                copies[which, index] = pltpu.make_async_copy(
                    source.at[part, half], target.at[part, half], sems.at[which, index]
                )
                copies[which, index].start()
    for step in range(D // DOWN):
        part = pl.ds(step * DOWN, DOWN)
        copies[2, step] = pltpu.make_async_copy(
            down_hbm.at[:, part], down_vmem.at[:, part], sems.at[2, step]
        )
        copies[2, step].start()

    squares = jnp.zeros((128, 128), jnp.float32)
    for block in range(HALF_D // 128):
        lanes = slice(block * 128, block * 128 + 128)
        turned = hidden_ref[lanes, :].astype(jnp.float32).T
        flipped[:, lanes] = turned
        squares = squares + turned * turned
        gain = gain_ref[:, lanes].astype(jnp.float32)
        scaled[0:DEVS, lanes] = (turned[0:DEVS] * gain[0:1]).astype(jnp.bfloat16)
        scaled[DEVS:128, lanes] = (turned[DEVS:128] * gain[1:2]).astype(jnp.bfloat16)
    chip = chip_ref[0]
    own_ref[0:1, :] = flipped[pl.ds(chip, 1), :]
    own_ref[1:2, :] = flipped[pl.ds(chip + DEVS, 1), :]
    total = jnp.sum(squares, axis=1, keepdims=True)
    factor = lax.rsqrt((total[0:DEVS] + total[DEVS:128]) * (1.0 / D) + epsilon)

    def product(index, weights):
        half, step = pieces[index]
        rows = scaled[half * DEVS : half * DEVS + DEVS, step * CHUNK : step * CHUNK + CHUNK]
        return jnp.dot(rows, weights.reshape(CHUNK, UNITS), preferred_element_type=jnp.float32)

    def part_of(ref, index):
        half, step = pieces[index]
        return ref[step * PART : step * PART + PART, half]

    gate = jnp.zeros((DEVS, UNITS), jnp.float32)
    up = jnp.zeros((DEVS, UNITS), jnp.float32)
    for index in range(EARLY):
        gate = gate + product(index, early_ref[index])
    for index in order:
        if index >= EARLY:
            copies[0, index].wait()
            gate = gate + product(index, part_of(gate_vmem, index))
        copies[1, index].wait()
        up = up + product(index, part_of(up_vmem, index))
    gate = gate * factor
    up = up * factor
    act = (gate / (1.0 + jnp.exp(-gate)) * up).astype(jnp.bfloat16)
    span = DOWN // 128
    for step in range(D // DOWN):
        copies[2, step].wait()
        block = jnp.dot(
            act, down_vmem[:, step * DOWN : step * DOWN + DOWN], preferred_element_type=jnp.float32
        )
        for column in range(span):
            result[pl.ds(step * span + column, DEVS, stride=ROWS), :] = block[
                :, column * 128 : column * 128 + 128
            ]
        last = (step + 1) * span
        if last % 16 == 0 and last < ROWS:
            for target in range(DEVS):
                out_ref[target, last - 16 : last, :] = result[
                    target * ROWS + last - 16 : target * ROWS + last, :
                ].astype(jnp.bfloat16)
    for target in range(DEVS):
        out_ref[target, ROWS - 16 : ROWS, :] = result[
            target * ROWS + ROWS - 16 : target * ROWS + ROWS, :
        ].astype(jnp.bfloat16)


def run_experts(chip, hidden, gain, early, w_gate, w_up, w_down):
    return pl.pallas_call(
        expert_kernel,
        out_shape=(
            pltpu.HBM((DEVS, ROWS, 128), jnp.bfloat16),
            jax.ShapeDtypeStruct((2, HALF_D), jnp.float32),
        ),
        in_specs=[SMEM_BLOCK] + [VMEM_BLOCK] * 3 + [ANY_BLOCK] * 3,
        out_specs=(VMEM_BLOCK, VMEM_BLOCK),
        scratch_shapes=[
            pltpu.VMEM((DEVS, 2, HALF, UNITS), jnp.bfloat16),
            pltpu.VMEM((DEVS, 2, HALF, UNITS), jnp.bfloat16),
            pltpu.VMEM((UNITS, D), jnp.bfloat16),
            pltpu.VMEM((128, HALF_D), jnp.float32),
            pltpu.VMEM((128, HALF_D), jnp.bfloat16),
            pltpu.VMEM((DEVS * ROWS, 128), jnp.float32),
            pltpu.SemaphoreType.DMA((3, 2 * STEPS)),
        ],
        compiler_params=pltpu.CompilerParams(vmem_limit_bytes=40 << 20),
        name="experts",
    )(chip, hidden, gain, *in_vmem(early), *in_hbm(w_gate, w_up, w_down))


def mix_kernel(core_ref, ids_ref, gates_ref, returned_ref, hidden_ref, kept_ref, given_ref):
    core = core_ref[0]
    total = hidden_ref[...]
    for expert in range(EXPERTS):
        share = jnp.float32(0.0)
        for choice in range(2):
            share = share + jnp.where(
                ids_ref[core, choice] == expert, gates_ref[core, choice], jnp.float32(0.0)
            )
        block = jnp.zeros((ROWS, 128), jnp.float32)
        for source in range(DEVS // EXPERTS):
            block = block + returned_ref[expert * (DEVS // EXPERTS) + source].astype(jnp.float32)
        total = total + block * share
    lower, upper = total[0 : ROWS // 2], total[ROWS // 2 : ROWS]
    kept_ref[...] = jnp.where(core == 0, lower, upper).astype(jnp.bfloat16)
    given_ref[...] = jnp.where(core == 0, upper, lower).astype(jnp.bfloat16)


def mix(core, expert_ids, gate_weights, returned, hidden):
    half = jax.ShapeDtypeStruct((ROWS // 2, 128), jnp.bfloat16)
    return pl.pallas_call(
        mix_kernel,
        out_shape=(half, half),
        in_specs=[SMEM_BLOCK, SMEM_BLOCK, SMEM_BLOCK, VMEM_BLOCK, VMEM_BLOCK],
        out_specs=(VMEM_BLOCK, VMEM_BLOCK),
        compiler_params=pltpu.CompilerParams(vmem_limit_bytes=8 << 20),
        name="mix",
    )(core, expert_ids, gate_weights, returned, hidden)


def exchange(parts):
    return lax.all_to_all(parts, "dev", split_axis=0, concat_axis=0, tiled=True)


def local(
    query,
    new_key,
    new_value,
    key_cache,
    value_cache,
    cached,
    residual,
    out_weight,
    norm_gain,
    expert_ids,
    gate_weights,
    w_gate,
    w_up,
    w_down,
):
    core = lax.axis_index("side").astype(jnp.int32).reshape(1)
    chip = lax.axis_index("dev").astype(jnp.int32).reshape(1)
    outgoing, mark = attend(
        core, cached, query, new_key, new_value, residual, key_cache, value_cache
    )
    norm_gain, mark = lax.optimization_barrier((norm_gain, mark))
    gain = norm_gain.reshape(DEVS, 2, HALF).transpose(1, 0, 2).reshape(2, HALF_D)
    (projection,) = fetch(mark, out_weight.T)
    arrived = exchange(outgoing.reshape(DEVS, SENT // 2, 2, 128)).reshape(DEVS * SENT, 128)
    packed, mark = project(chip, arrived, projection)
    w_gate = w_gate.reshape(DEVS, 2, HALF, UNITS)
    w_up = w_up.reshape(DEVS, 2, HALF, UNITS)
    early = fetch_early(mark, w_gate)
    hidden = exchange(packed).reshape(HALF_D, 128)
    partial_value, own_hidden = run_experts(chip, hidden, gain, early, w_gate, w_up, w_down)
    returned = exchange(partial_value)
    own_hidden = own_hidden.reshape(2, DEVS, HALF).transpose(1, 0, 2).reshape(ROWS, 128)
    kept, given = mix(core, expert_ids, gate_weights, returned, own_hidden)
    taken = lax.ppermute(given, "side", [(0, 1), (1, 0)])
    first = jnp.where(core == 0, kept, taken)
    second = jnp.where(core == 0, taken, kept)
    return jnp.stack([first.reshape(D // 2), second.reshape(D // 2)])


def solution(mesh):
    in_specs = (
        P("dev", None),
        P("dev", None),
        P("dev", None),
        P("dev", None, None),
        P("dev", None, None),
        P("dev"),
        P("dev", None),
        P(None, "dev"),
        P(),
        P("dev", None),
        P("dev", None),
        P(None, "dev"),
        P(None, "dev"),
        P("dev", None),
    )
    out_specs = P("dev", "side")
    return jax.shard_map(local, mesh=mesh, in_specs=in_specs, out_specs=out_specs, check_vma=False)
```

```python
import math

import jax
import jax.numpy as jnp
from jax import lax
from jax.experimental import pallas as pl
from jax.experimental.pallas import tpu as pltpu
from jax.sharding import PartitionSpec as P

D = 6144
HEADS = 48
KV_HEADS = 8
HEAD_DIM = 128
GROUP = HEADS // KV_HEADS
EXPERTS = 4
CACHE_LEN = 128
DEVS = 64
COLS = D // DEVS
HALF = COLS // 2
ROWS = D // 128
SENT = ROWS + 2
BATCH = 8
UNITS = 512
HALF_D = D // 2
CHUNK = 768
PART = CHUNK // HALF
STEPS = HALF_D // CHUNK
EARLY = 3
DOWN = 1024

epsilon = 1e-05


def walk():
    places = []
    for step in range(DEVS):
        x, y, z = (step * 43 % 64 // 16, step * 43 % 16 // 4, step * 43 % 4)
        places.append((x + 2) % 4 * 16 + (y + 2) % 4 * 4 + (z + 2) % 4)
    return places


ORDER = walk()
PLACE = [ORDER.index(chip) for chip in range(DEVS)]

VMEM_BLOCK = pl.BlockSpec(memory_space=pltpu.VMEM)
SMEM_BLOCK = pl.BlockSpec(memory_space=pltpu.SMEM)
ANY_BLOCK = pl.BlockSpec(memory_space=pl.ANY)


def in_hbm(*arrays):
    return tuple(pltpu.with_memory_space_constraint(array, pltpu.HBM) for array in arrays)


def in_vmem(*arrays):
    return tuple(pltpu.with_memory_space_constraint(array, pltpu.VMEM) for array in arrays)


def last_dims(left, right):
    return lax.dot_general(
        left, right, (((1,), (1,)), ((), ())), preferred_element_type=jnp.float32
    )


def attend_kernel(
    core_ref,
    cached_ref,
    query_ref,
    new_key_ref,
    new_value_ref,
    residual_ref,
    key_ref,
    value_ref,
    out_ref,
    mark_ref,
    query_rows,
    residual_rows,
    context_rows,
    pattern,
):
    core = core_ref[0]
    first_row = pl.multiple_of(core * 64, 64)

    def own(ref):
        both = ref[...].astype(jnp.float32)
        return jnp.where(core == 0, both[0:1], both[1:2])

    query_rows[...] = jnp.zeros_like(query_rows)
    residual_rows[...] = jnp.zeros_like(residual_rows)
    both = query_ref[...].astype(jnp.float32)
    for head in range(HEADS):
        row = head // GROUP * 8 + head % GROUP
        query_rows[pl.ds(row, 2, stride=64), :] = both[:, head * 128 : head * 128 + 128]
    both = residual_ref[...].astype(jnp.float32)
    for row in range(ROWS):
        residual_rows[pl.ds(row, 2, stride=64), :] = both[:, row * 128 : row * 128 + 128]
    queries = query_rows[pl.ds(first_row, 64), :]
    narrow = queries.astype(jnp.bfloat16)
    new_key = own(new_key_ref)
    new_value = own(new_value_ref)
    scale = 1.0 / math.sqrt(HEAD_DIM)
    scores = []
    own_keys = []
    for kv in range(KV_HEADS):
        lanes = slice(kv * 128, kv * 128 + 128)
        scores.append(last_dims(narrow[kv * 8 : kv * 8 + 8], key_ref[0, :, lanes]))
        own_keys.append(jnp.broadcast_to(new_key[:, lanes], (8, 128)))
    scores = jnp.concatenate(scores, axis=0) * scale
    own_score = jnp.sum(queries * jnp.concatenate(own_keys, axis=0), axis=1, keepdims=True) * scale
    visible = lax.broadcasted_iota(jnp.int32, scores.shape, 1) < cached_ref[core]
    scores = jnp.where(visible, scores, -jnp.inf)
    highest = jnp.maximum(jnp.max(scores, axis=1, keepdims=True), own_score)
    exponents = jnp.exp(scores - highest)
    own_exp = jnp.exp(own_score - highest)
    denominator = jnp.sum(exponents, axis=1, keepdims=True) + own_exp
    weights = (exponents / denominator).astype(jnp.bfloat16)
    own_weight = (own_exp / denominator).astype(jnp.bfloat16).astype(jnp.float32)
    for kv in range(KV_HEADS):
        lanes = slice(kv * 128, kv * 128 + 128)
        context = jnp.dot(
            weights[kv * 8 : kv * 8 + 8], value_ref[0, :, lanes], preferred_element_type=jnp.float32
        )
        context = context + own_weight[kv * 8 : kv * 8 + 8] * new_value[:, lanes]
        context_rows[kv * GROUP : kv * GROUP + 8, :] = context
    context = context_rows[0:ROWS, :]
    mark_ref[...] = context[0:8]
    for chip in range(BATCH):
        pattern[chip * SENT : chip * SENT + ROWS, :] = context
    for group in range(DEVS // BATCH):
        for chip in range(BATCH):
            wanted = COLS * ORDER[group * BATCH + chip] // 128
            pattern[chip * SENT + ROWS : chip * SENT + SENT, :] = residual_rows[
                pl.ds(first_row + wanted, 2), :
            ]
        first = group * BATCH * SENT
        out_ref[first : first + BATCH * SENT, :] = pattern[...].astype(jnp.bfloat16)


def attend(core, cached, query, new_key, new_value, residual, key_cache, value_cache):
    def whole(shape):
        return pl.BlockSpec(shape, lambda step, core, cached: (0,) * len(shape))

    cache = pl.BlockSpec((1, CACHE_LEN, 1024), lambda step, core, cached: (core[0], 0, 0))
    return pl.pallas_call(
        attend_kernel,
        out_shape=(
            jax.ShapeDtypeStruct((DEVS * SENT, 128), jnp.bfloat16),
            jax.ShapeDtypeStruct((8, 128), jnp.float32),
        ),
        grid_spec=pltpu.PrefetchScalarGridSpec(
            num_scalar_prefetch=2,
            grid=(1,),
            in_specs=[
                whole((2, D)),
                whole((2, 1024)),
                whole((2, 1024)),
                whole((2, D)),
                cache,
                cache,
            ],
            out_specs=(whole((DEVS * SENT, 128)), whole((8, 128))),
            scratch_shapes=[
                pltpu.VMEM((128, 128), jnp.float32),
                pltpu.VMEM((128, 128), jnp.float32),
                pltpu.VMEM((ROWS + 8, 128), jnp.float32),
                pltpu.VMEM((BATCH * SENT, 128), jnp.float32),
            ],
        ),
        compiler_params=pltpu.CompilerParams(vmem_limit_bytes=8 << 20),
        name="attend",
    )(core, *in_hbm(cached, query, new_key, new_value, residual, key_cache, value_cache))


def fetch_kernel(after_ref, *refs):
    count = (len(refs) - 1) // 2
    copies = [
        pltpu.make_async_copy(refs[i], refs[count + i], refs[-1].at[i]) for i in range(count)
    ]
    for copy in copies:
        copy.start()
    for copy in copies:
        copy.wait()


def fetch(after, *arrays):
    size = sum(array.size * array.dtype.itemsize for array in arrays)
    return pl.pallas_call(
        fetch_kernel,
        out_shape=tuple(pltpu.VMEM(array.shape, array.dtype) for array in arrays),
        in_specs=[ANY_BLOCK] * (len(arrays) + 1),
        out_specs=(VMEM_BLOCK,) * len(arrays),
        scratch_shapes=[pltpu.SemaphoreType.DMA((len(arrays),))],
        compiler_params=pltpu.CompilerParams(vmem_limit_bytes=1 << 20),
        cost_estimate=pl.CostEstimate(flops=0, bytes_accessed=2 * size, transcendentals=0),
        name="fetch",
    )(after, *in_hbm(*arrays))


def project_kernel(chip_ref, arrived_ref, weight_ref, out_ref, mark_ref, rows, context):
    for source in range(0, DEVS * SENT, 400):
        rows[source : source + 400, :] = arrived_ref[source : source + 400, :].astype(jnp.float32)
    for head in range(HEADS):
        context[:, head * 128 : head * 128 + 128] = rows[pl.ds(head, DEVS, stride=SENT), :].astype(
            jnp.bfloat16
        )
    tokens = context[...]
    projected = last_dims(weight_ref[...], jnp.concatenate([tokens, tokens], axis=0))
    flipped = []
    for row in (ROWS, ROWS + 1):
        part = rows[pl.ds(row, DEVS, stride=SENT), :]
        flipped.append(jnp.concatenate([part, part], axis=0).T)
    rows[0:256, :] = jnp.concatenate(flipped, axis=0)
    first = pl.multiple_of(lax.rem(chip_ref[0] * COLS, 128), 32)
    hidden = rows[pl.ds(first, COLS), :] + projected
    lane = lax.broadcasted_iota(jnp.int32, (HALF, 128), 1)
    packed = jnp.where(lane < DEVS, hidden[0:HALF], hidden[HALF:COLS]).astype(jnp.bfloat16)
    mark_ref[...] = hidden[0:8]
    for target in range(DEVS):
        out_ref[target] = packed


def project(chip, arrived, weight):
    return pl.pallas_call(
        project_kernel,
        out_shape=(
            jax.ShapeDtypeStruct((DEVS, HALF, 128), jnp.bfloat16),
            jax.ShapeDtypeStruct((8, 128), jnp.float32),
        ),
        in_specs=[SMEM_BLOCK, VMEM_BLOCK, VMEM_BLOCK],
        out_specs=(VMEM_BLOCK, VMEM_BLOCK),
        scratch_shapes=[
            pltpu.VMEM((DEVS * SENT, 128), jnp.float32),
            pltpu.VMEM((DEVS, D), jnp.bfloat16),
        ],
        compiler_params=pltpu.CompilerParams(vmem_limit_bytes=16 << 20),
        name="project",
    )(chip, arrived, *in_vmem(weight))


def early_kernel(after_ref, gate_hbm, out_ref, sems):
    copies = [
        pltpu.make_async_copy(
            gate_hbm.at[pl.ds(step * PART, PART), 0], out_ref.at[step], sems.at[step]
        )
        for step in range(EARLY)
    ]
    for copy in copies:
        copy.start()
    for copy in copies:
        copy.wait()


def fetch_early(after, w_gate):
    return pl.pallas_call(
        early_kernel,
        out_shape=pltpu.VMEM((EARLY, PART, HALF, UNITS), w_gate.dtype),
        in_specs=[ANY_BLOCK] * 2,
        out_specs=VMEM_BLOCK,
        scratch_shapes=[pltpu.SemaphoreType.DMA((EARLY,))],
        compiler_params=pltpu.CompilerParams(vmem_limit_bytes=1 << 20),
        name="fetch_early",
    )(after, *in_hbm(w_gate))


def expert_kernel(
    place_ref,
    hidden_ref,
    gain_ref,
    early_ref,
    gate_hbm,
    up_hbm,
    down_hbm,
    out_ref,
    own_ref,
    gate_vmem,
    up_vmem,
    down_vmem,
    flipped,
    scaled,
    result,
    sems,
):
    pieces = [(half, step) for half in range(2) for step in range(STEPS)]
    order = list(range(EARLY, len(pieces))) + list(range(EARLY))
    copies = {}
    for index in order:
        half, step = pieces[index]
        part = pl.ds(step * PART, PART)
        for which, source, target in ((0, gate_hbm, gate_vmem), (1, up_hbm, up_vmem)):
            if which == 1 or index >= EARLY:
                copies[which, index] = pltpu.make_async_copy(
                    source.at[part, half], target.at[part, half], sems.at[which, index]
                )
                copies[which, index].start()
    for step in range(D // DOWN):
        part = pl.ds(step * DOWN, DOWN)
        copies[2, step] = pltpu.make_async_copy(
            down_hbm.at[:, part], down_vmem.at[:, part], sems.at[2, step]
        )
        copies[2, step].start()

    squares = jnp.zeros((128, 128), jnp.float32)
    for block in range(HALF_D // 384):
        columns = jnp.concatenate(
            [
                hidden_ref[PLACE[chip] * HALF : PLACE[chip] * HALF + HALF, :].astype(jnp.float32)
                for chip in range(block * 8, block * 8 + 8)
            ],
            axis=0,
        )
        for third in range(3):
            turned = columns[third * 128 : third * 128 + 128].T
            lanes = slice(block * 384 + third * 128, block * 384 + third * 128 + 128)
            flipped[:, lanes] = turned
            squares = squares + turned * turned
            gain = gain_ref[:, lanes].astype(jnp.float32)
            scaled[0:DEVS, lanes] = (turned[0:DEVS] * gain[0:1]).astype(jnp.bfloat16)
            scaled[DEVS:128, lanes] = (turned[DEVS:128] * gain[1:2]).astype(jnp.bfloat16)
    place = place_ref[0]
    own_ref[0:1, :] = flipped[pl.ds(place, 1), :]
    own_ref[1:2, :] = flipped[pl.ds(place + DEVS, 1), :]
    total = jnp.sum(squares, axis=1, keepdims=True)
    factor = lax.rsqrt((total[0:DEVS] + total[DEVS:128]) * (1.0 / D) + epsilon)

    def product(index, weights):
        half, step = pieces[index]
        rows = scaled[half * DEVS : half * DEVS + DEVS, step * CHUNK : step * CHUNK + CHUNK]
        return jnp.dot(rows, weights.reshape(CHUNK, UNITS), preferred_element_type=jnp.float32)

    def part_of(ref, index):
        half, step = pieces[index]
        return ref[step * PART : step * PART + PART, half]

    gate = jnp.zeros((DEVS, UNITS), jnp.float32)
    up = jnp.zeros((DEVS, UNITS), jnp.float32)
    for index in range(EARLY):
        gate = gate + product(index, early_ref[index])
    for index in order:
        if index >= EARLY:
            copies[0, index].wait()
            gate = gate + product(index, part_of(gate_vmem, index))
        copies[1, index].wait()
        up = up + product(index, part_of(up_vmem, index))
    gate = gate * factor
    up = up * factor
    act = (gate / (1.0 + jnp.exp(-gate)) * up).astype(jnp.bfloat16)
    span = DOWN // 128
    for step in range(D // DOWN):
        copies[2, step].wait()
        block = jnp.dot(
            act, down_vmem[:, step * DOWN : step * DOWN + DOWN], preferred_element_type=jnp.float32
        )
        for column in range(span):
            result[pl.ds(step * span + column, DEVS, stride=ROWS), :] = block[
                :, column * 128 : column * 128 + 128
            ]
        last = (step + 1) * span
        if last % 16 == 0 and last < ROWS:
            for target in range(DEVS):
                out_ref[target, last - 16 : last, :] = result[
                    target * ROWS + last - 16 : target * ROWS + last, :
                ].astype(jnp.bfloat16)
    for target in range(DEVS):
        out_ref[target, ROWS - 16 : ROWS, :] = result[
            target * ROWS + ROWS - 16 : target * ROWS + ROWS, :
        ].astype(jnp.bfloat16)


def run_experts(place, hidden, gain, early, w_gate, w_up, w_down):
    return pl.pallas_call(
        expert_kernel,
        out_shape=(
            pltpu.HBM((DEVS, ROWS, 128), jnp.bfloat16),
            jax.ShapeDtypeStruct((2, HALF_D), jnp.float32),
        ),
        in_specs=[SMEM_BLOCK] + [VMEM_BLOCK] * 3 + [ANY_BLOCK] * 3,
        out_specs=(VMEM_BLOCK, VMEM_BLOCK),
        scratch_shapes=[
            pltpu.VMEM((DEVS, 2, HALF, UNITS), jnp.bfloat16),
            pltpu.VMEM((DEVS, 2, HALF, UNITS), jnp.bfloat16),
            pltpu.VMEM((UNITS, D), jnp.bfloat16),
            pltpu.VMEM((128, HALF_D), jnp.float32),
            pltpu.VMEM((128, HALF_D), jnp.bfloat16),
            pltpu.VMEM((DEVS * ROWS, 128), jnp.float32),
            pltpu.SemaphoreType.DMA((3, 2 * STEPS)),
        ],
        compiler_params=pltpu.CompilerParams(vmem_limit_bytes=40 << 20),
        name="experts",
    )(place, hidden, gain, *in_vmem(early), *in_hbm(w_gate, w_up, w_down))


def mix_kernel(core_ref, ids_ref, gates_ref, returned_ref, hidden_ref, kept_ref, given_ref):
    core = core_ref[0]
    total = hidden_ref[...]
    for expert in range(EXPERTS):
        share = jnp.float32(0.0)
        for choice in range(2):
            share = share + jnp.where(
                ids_ref[core, choice] == expert, gates_ref[core, choice], jnp.float32(0.0)
            )
        block = jnp.zeros((ROWS, 128), jnp.float32)
        for place in range(DEVS):
            if ORDER[place] // (DEVS // EXPERTS) == expert:
                block = block + returned_ref[place].astype(jnp.float32)
        total = total + block * share
    lower, upper = total[0 : ROWS // 2], total[ROWS // 2 : ROWS]
    kept_ref[...] = jnp.where(core == 0, lower, upper).astype(jnp.bfloat16)
    given_ref[...] = jnp.where(core == 0, upper, lower).astype(jnp.bfloat16)


def mix(core, expert_ids, gate_weights, returned, hidden):
    half = jax.ShapeDtypeStruct((ROWS // 2, 128), jnp.bfloat16)
    return pl.pallas_call(
        mix_kernel,
        out_shape=(half, half),
        in_specs=[SMEM_BLOCK, SMEM_BLOCK, SMEM_BLOCK, VMEM_BLOCK, VMEM_BLOCK],
        out_specs=(VMEM_BLOCK, VMEM_BLOCK),
        compiler_params=pltpu.CompilerParams(vmem_limit_bytes=8 << 20),
        name="mix",
    )(core, expert_ids, gate_weights, returned, hidden)


def exchange(parts):
    return lax.all_to_all(
        parts, "dev", split_axis=0, concat_axis=0, tiled=True, axis_index_groups=[ORDER]
    )


def local(
    query,
    new_key,
    new_value,
    key_cache,
    value_cache,
    cached,
    residual,
    out_weight,
    norm_gain,
    expert_ids,
    gate_weights,
    w_gate,
    w_up,
    w_down,
):
    core = lax.axis_index("side").astype(jnp.int32).reshape(1)
    chip = lax.axis_index("dev").astype(jnp.int32).reshape(1)
    place = jnp.asarray(PLACE, jnp.int32)[chip]
    outgoing, mark = attend(
        core, cached, query, new_key, new_value, residual, key_cache, value_cache
    )
    norm_gain, mark = lax.optimization_barrier((norm_gain, mark))
    gain = norm_gain.reshape(DEVS, 2, HALF).transpose(1, 0, 2).reshape(2, HALF_D)
    (projection,) = fetch(mark, out_weight.T)
    arrived = exchange(outgoing.reshape(DEVS, SENT // 2, 2, 128)).reshape(DEVS * SENT, 128)
    packed, mark = project(chip, arrived, projection)
    w_gate = w_gate.reshape(DEVS, 2, HALF, UNITS)
    w_up = w_up.reshape(DEVS, 2, HALF, UNITS)
    early = fetch_early(mark, w_gate)
    hidden = exchange(packed).reshape(HALF_D, 128)
    partial_value, own_hidden = run_experts(place, hidden, gain, early, w_gate, w_up, w_down)
    returned = exchange(partial_value)
    own_hidden = own_hidden.reshape(2, DEVS, HALF).transpose(1, 0, 2).reshape(ROWS, 128)
    kept, given = mix(core, expert_ids, gate_weights, returned, own_hidden)
    taken = lax.ppermute(given, "side", [(0, 1), (1, 0)])
    first = jnp.where(core == 0, kept, taken)
    second = jnp.where(core == 0, taken, kept)
    return jnp.stack([first.reshape(D // 2), second.reshape(D // 2)])


def solution(mesh):
    in_specs = (
        P("dev", None),
        P("dev", None),
        P("dev", None),
        P("dev", None, None),
        P("dev", None, None),
        P("dev"),
        P("dev", None),
        P(None, "dev"),
        P(),
        P("dev", None),
        P("dev", None),
        P(None, "dev"),
        P(None, "dev"),
        P("dev", None),
    )
    out_specs = P("dev", "side")
    return jax.shard_map(local, mesh=mesh, in_specs=in_specs, out_specs=out_specs, check_vma=False)
```

```python
import math

import jax
import jax.numpy as jnp
from jax import lax
from jax.experimental import pallas as pl
from jax.experimental.pallas import tpu as pltpu
from jax.sharding import PartitionSpec as P

D = 6144
HEADS = 48
KV_HEADS = 8
HEAD_DIM = 128
GROUP = HEADS // KV_HEADS
EXPERTS = 4
CACHE_LEN = 128
DEVS = 64
COLS = D // DEVS
HALF = COLS // 2
ROWS = D // 128
SENT = ROWS + 2
BATCH = 8
UNITS = 512
HALF_D = D // 2
CHUNK = 768
PART = CHUNK // HALF
STEPS = HALF_D // CHUNK
EARLY = 3
DOWN = 1024

epsilon = 1e-05


STRIDE, UNSTRIDE, FIRST = 43, 3, 42
ORDER = [step * STRIDE % DEVS ^ FIRST for step in range(DEVS)]
PLACE = [ORDER.index(chip) for chip in range(DEVS)]

VMEM_BLOCK = pl.BlockSpec(memory_space=pltpu.VMEM)
SMEM_BLOCK = pl.BlockSpec(memory_space=pltpu.SMEM)
ANY_BLOCK = pl.BlockSpec(memory_space=pl.ANY)


def in_hbm(*arrays):
    return tuple(pltpu.with_memory_space_constraint(array, pltpu.HBM) for array in arrays)


def in_vmem(*arrays):
    return tuple(pltpu.with_memory_space_constraint(array, pltpu.VMEM) for array in arrays)


def last_dims(left, right):
    return lax.dot_general(
        left, right, (((1,), (1,)), ((), ())), preferred_element_type=jnp.float32
    )


def attend_kernel(
    core_ref,
    cached_ref,
    query_ref,
    new_key_ref,
    new_value_ref,
    residual_ref,
    key_ref,
    value_ref,
    out_ref,
    mark_ref,
    query_rows,
    residual_rows,
    context_rows,
    pattern,
):
    core = core_ref[0]
    first_row = pl.multiple_of(core * 64, 64)

    def own(ref):
        both = ref[...].astype(jnp.float32)
        return jnp.where(core == 0, both[0:1], both[1:2])

    query_rows[...] = jnp.zeros_like(query_rows)
    residual_rows[...] = jnp.zeros_like(residual_rows)
    both = query_ref[...].astype(jnp.float32)
    for head in range(HEADS):
        row = head // GROUP * 8 + head % GROUP
        query_rows[pl.ds(row, 2, stride=64), :] = both[:, head * 128 : head * 128 + 128]
    both = residual_ref[...].astype(jnp.float32)
    for row in range(ROWS):
        residual_rows[pl.ds(row, 2, stride=64), :] = both[:, row * 128 : row * 128 + 128]
    queries = query_rows[pl.ds(first_row, 64), :]
    narrow = queries.astype(jnp.bfloat16)
    new_key = own(new_key_ref)
    new_value = own(new_value_ref)
    scale = 1.0 / math.sqrt(HEAD_DIM)
    scores = []
    own_keys = []
    for kv in range(KV_HEADS):
        lanes = slice(kv * 128, kv * 128 + 128)
        scores.append(last_dims(narrow[kv * 8 : kv * 8 + 8], key_ref[core, :, lanes]))
        own_keys.append(jnp.broadcast_to(new_key[:, lanes], (8, 128)))
    scores = jnp.concatenate(scores, axis=0) * scale
    own_score = jnp.sum(queries * jnp.concatenate(own_keys, axis=0), axis=1, keepdims=True) * scale
    visible = lax.broadcasted_iota(jnp.int32, scores.shape, 1) < cached_ref[core]
    scores = jnp.where(visible, scores, -jnp.inf)
    highest = jnp.maximum(jnp.max(scores, axis=1, keepdims=True), own_score)
    exponents = jnp.exp(scores - highest)
    own_exp = jnp.exp(own_score - highest)
    denominator = jnp.sum(exponents, axis=1, keepdims=True) + own_exp
    weights = (exponents / denominator).astype(jnp.bfloat16)
    own_weight = (own_exp / denominator).astype(jnp.bfloat16).astype(jnp.float32)
    for kv in range(KV_HEADS):
        lanes = slice(kv * 128, kv * 128 + 128)
        context = jnp.dot(
            weights[kv * 8 : kv * 8 + 8], value_ref[core, :, lanes], preferred_element_type=jnp.float32
        )
        context = context + own_weight[kv * 8 : kv * 8 + 8] * new_value[:, lanes]
        context_rows[kv * GROUP : kv * GROUP + 8, :] = context
    context = context_rows[0:ROWS, :]
    mark_ref[...] = context[0:8]
    for chip in range(BATCH):
        pattern[chip * SENT : chip * SENT + ROWS, :] = context
    for group in range(DEVS // BATCH):
        for chip in range(BATCH):
            wanted = COLS * ORDER[group * BATCH + chip] // 128
            pattern[chip * SENT + ROWS : chip * SENT + SENT, :] = residual_rows[
                pl.ds(first_row + wanted, 2), :
            ]
        first = group * BATCH * SENT
        out_ref[first : first + BATCH * SENT, :] = pattern[...].astype(jnp.bfloat16)


def attend(core, cached, query, new_key, new_value, residual, key_cache, value_cache):
    return pl.pallas_call(
        attend_kernel,
        out_shape=(
            jax.ShapeDtypeStruct((DEVS * SENT, 128), jnp.bfloat16),
            jax.ShapeDtypeStruct((8, 128), jnp.float32),
        ),
        in_specs=[SMEM_BLOCK, SMEM_BLOCK] + [VMEM_BLOCK] * 6,
        out_specs=(VMEM_BLOCK, VMEM_BLOCK),
        scratch_shapes=[
            pltpu.VMEM((128, 128), jnp.float32),
            pltpu.VMEM((128, 128), jnp.float32),
            pltpu.VMEM((ROWS + 8, 128), jnp.float32),
            pltpu.VMEM((BATCH * SENT, 128), jnp.float32),
        ],
        compiler_params=pltpu.CompilerParams(vmem_limit_bytes=8 << 20),
        name="attend",
    )(core, *in_hbm(cached, query, new_key, new_value, residual, key_cache, value_cache))


def fetch_kernel(after_ref, *refs):
    count = (len(refs) - 1) // 2
    copies = [
        pltpu.make_async_copy(refs[i], refs[count + i], refs[-1].at[i]) for i in range(count)
    ]
    for copy in copies:
        copy.start()
    for copy in copies:
        copy.wait()


def fetch(after, *arrays):
    size = sum(array.size * array.dtype.itemsize for array in arrays)
    return pl.pallas_call(
        fetch_kernel,
        out_shape=tuple(pltpu.VMEM(array.shape, array.dtype) for array in arrays),
        in_specs=[ANY_BLOCK] * (len(arrays) + 1),
        out_specs=(VMEM_BLOCK,) * len(arrays),
        scratch_shapes=[pltpu.SemaphoreType.DMA((len(arrays),))],
        compiler_params=pltpu.CompilerParams(vmem_limit_bytes=1 << 20),
        cost_estimate=pl.CostEstimate(flops=0, bytes_accessed=2 * size, transcendentals=0),
        name="fetch",
    )(after, *in_hbm(*arrays))


def project_kernel(chip_ref, arrived_ref, weight_ref, out_ref, mark_ref, rows, context):
    for source in range(0, DEVS * SENT, 400):
        rows[source : source + 400, :] = arrived_ref[source : source + 400, :].astype(jnp.float32)
    for head in range(HEADS):
        context[:, head * 128 : head * 128 + 128] = rows[pl.ds(head, DEVS, stride=SENT), :].astype(
            jnp.bfloat16
        )
    tokens = context[...]
    projected = last_dims(weight_ref[...], jnp.concatenate([tokens, tokens], axis=0))
    flipped = []
    for row in (ROWS, ROWS + 1):
        part = rows[pl.ds(row, DEVS, stride=SENT), :]
        flipped.append(jnp.concatenate([part, part], axis=0).T)
    rows[0:256, :] = jnp.concatenate(flipped, axis=0)
    first = pl.multiple_of(lax.rem(chip_ref[0] * COLS, 128), 32)
    hidden = rows[pl.ds(first, COLS), :] + projected
    lane = lax.broadcasted_iota(jnp.int32, (HALF, 128), 1)
    packed = jnp.where(lane < DEVS, hidden[0:HALF], hidden[HALF:COLS]).astype(jnp.bfloat16)
    mark_ref[...] = hidden[0:8]
    for target in range(DEVS):
        out_ref[target] = packed


def project(chip, arrived, weight):
    return pl.pallas_call(
        project_kernel,
        out_shape=(
            jax.ShapeDtypeStruct((DEVS, HALF, 128), jnp.bfloat16),
            jax.ShapeDtypeStruct((8, 128), jnp.float32),
        ),
        in_specs=[SMEM_BLOCK, VMEM_BLOCK, VMEM_BLOCK],
        out_specs=(VMEM_BLOCK, VMEM_BLOCK),
        scratch_shapes=[
            pltpu.VMEM((DEVS * SENT, 128), jnp.float32),
            pltpu.VMEM((DEVS, D), jnp.bfloat16),
        ],
        compiler_params=pltpu.CompilerParams(vmem_limit_bytes=16 << 20),
        name="project",
    )(chip, arrived, *in_vmem(weight))


def early_kernel(after_ref, gate_hbm, out_ref, sems):
    copies = [
        pltpu.make_async_copy(
            gate_hbm.at[pl.ds(step * PART, PART), 0], out_ref.at[step], sems.at[step]
        )
        for step in range(EARLY)
    ]
    for copy in copies:
        copy.start()
    for copy in copies:
        copy.wait()


def fetch_early(after, w_gate):
    return pl.pallas_call(
        early_kernel,
        out_shape=pltpu.VMEM((EARLY, PART, HALF, UNITS), w_gate.dtype),
        in_specs=[ANY_BLOCK] * 2,
        out_specs=VMEM_BLOCK,
        scratch_shapes=[pltpu.SemaphoreType.DMA((EARLY,))],
        compiler_params=pltpu.CompilerParams(vmem_limit_bytes=1 << 20),
        name="fetch_early",
    )(after, *in_hbm(w_gate))


def expert_kernel(
    chip_ref,
    hidden_ref,
    gain_ref,
    early_ref,
    gate_hbm,
    up_hbm,
    down_hbm,
    out_ref,
    own_ref,
    gate_vmem,
    up_vmem,
    down_vmem,
    flipped,
    scaled,
    result,
    sems,
):
    pieces = [(half, step) for half in range(2) for step in range(STEPS)]
    order = list(range(EARLY, len(pieces))) + list(range(EARLY))
    copies = {}
    for index in order:
        half, step = pieces[index]
        part = pl.ds(step * PART, PART)
        for which, source, target in ((0, gate_hbm, gate_vmem), (1, up_hbm, up_vmem)):
            if which == 1 or index >= EARLY:
                copies[which, index] = pltpu.make_async_copy(
                    source.at[part, half], target.at[part, half], sems.at[which, index]
                )
                copies[which, index].start()
    for step in range(D // DOWN):
        part = pl.ds(step * DOWN, DOWN)
        copies[2, step] = pltpu.make_async_copy(
            down_hbm.at[:, part], down_vmem.at[:, part], sems.at[2, step]
        )
        copies[2, step].start()

    squares = jnp.zeros((128, 128), jnp.float32)
    for block in range(HALF_D // 384):
        columns = jnp.concatenate(
            [
                hidden_ref[PLACE[chip] * HALF : PLACE[chip] * HALF + HALF, :].astype(jnp.float32)
                for chip in range(block * 8, block * 8 + 8)
            ],
            axis=0,
        )
        for third in range(3):
            turned = columns[third * 128 : third * 128 + 128].T
            lanes = slice(block * 384 + third * 128, block * 384 + third * 128 + 128)
            flipped[:, lanes] = turned
            squares = squares + turned * turned
            gain = gain_ref[:, lanes].astype(jnp.float32)
            scaled[0:DEVS, lanes] = (turned[0:DEVS] * gain[0:1]).astype(jnp.bfloat16)
            scaled[DEVS:128, lanes] = (turned[DEVS:128] * gain[1:2]).astype(jnp.bfloat16)
    place = lax.rem(jnp.bitwise_xor(chip_ref[0], FIRST) * UNSTRIDE, DEVS)
    own_ref[0:1, :] = flipped[pl.ds(place, 1), :]
    own_ref[1:2, :] = flipped[pl.ds(place + DEVS, 1), :]
    total = jnp.sum(squares, axis=1, keepdims=True)
    factor = lax.rsqrt((total[0:DEVS] + total[DEVS:128]) * (1.0 / D) + epsilon)

    def product(index, weights):
        half, step = pieces[index]
        rows = scaled[half * DEVS : half * DEVS + DEVS, step * CHUNK : step * CHUNK + CHUNK]
        return jnp.dot(rows, weights.reshape(CHUNK, UNITS), preferred_element_type=jnp.float32)

    def part_of(ref, index):
        half, step = pieces[index]
        return ref[step * PART : step * PART + PART, half]

    gate = jnp.zeros((DEVS, UNITS), jnp.float32)
    up = jnp.zeros((DEVS, UNITS), jnp.float32)
    for index in range(EARLY):
        gate = gate + product(index, early_ref[index])
    for index in order:
        if index >= EARLY:
            copies[0, index].wait()
            gate = gate + product(index, part_of(gate_vmem, index))
        copies[1, index].wait()
        up = up + product(index, part_of(up_vmem, index))
    gate = gate * factor
    up = up * factor
    act = (gate / (1.0 + jnp.exp(-gate)) * up).astype(jnp.bfloat16)
    span = DOWN // 128
    for step in range(D // DOWN):
        copies[2, step].wait()
        block = jnp.dot(
            act, down_vmem[:, step * DOWN : step * DOWN + DOWN], preferred_element_type=jnp.float32
        )
        for column in range(span):
            result[pl.ds(step * span + column, DEVS, stride=ROWS), :] = block[
                :, column * 128 : column * 128 + 128
            ]
        last = (step + 1) * span
        if last % 16 == 0 and last < ROWS:
            for target in range(DEVS):
                out_ref[target, last - 16 : last, :] = result[
                    target * ROWS + last - 16 : target * ROWS + last, :
                ].astype(jnp.bfloat16)
    for target in range(DEVS):
        out_ref[target, ROWS - 16 : ROWS, :] = result[
            target * ROWS + ROWS - 16 : target * ROWS + ROWS, :
        ].astype(jnp.bfloat16)


def run_experts(chip, hidden, gain, early, w_gate, w_up, w_down):
    return pl.pallas_call(
        expert_kernel,
        out_shape=(
            pltpu.HBM((DEVS, ROWS, 128), jnp.bfloat16),
            jax.ShapeDtypeStruct((2, HALF_D), jnp.float32),
        ),
        in_specs=[SMEM_BLOCK] + [VMEM_BLOCK] * 3 + [ANY_BLOCK] * 3,
        out_specs=(VMEM_BLOCK, VMEM_BLOCK),
        scratch_shapes=[
            pltpu.VMEM((DEVS, 2, HALF, UNITS), jnp.bfloat16),
            pltpu.VMEM((DEVS, 2, HALF, UNITS), jnp.bfloat16),
            pltpu.VMEM((UNITS, D), jnp.bfloat16),
            pltpu.VMEM((128, HALF_D), jnp.float32),
            pltpu.VMEM((128, HALF_D), jnp.bfloat16),
            pltpu.VMEM((DEVS * ROWS, 128), jnp.float32),
            pltpu.SemaphoreType.DMA((3, 2 * STEPS)),
        ],
        compiler_params=pltpu.CompilerParams(vmem_limit_bytes=40 << 20),
        name="experts",
    )(chip, hidden, gain, *in_vmem(early), *in_hbm(w_gate, w_up, w_down))


def mix_kernel(core_ref, ids_ref, gates_ref, returned_ref, hidden_ref, kept_ref, given_ref):
    core = core_ref[0]
    total = hidden_ref[...]
    for expert in range(EXPERTS):
        share = jnp.float32(0.0)
        for choice in range(2):
            share = share + jnp.where(
                ids_ref[core, choice] == expert, gates_ref[core, choice], jnp.float32(0.0)
            )
        block = jnp.zeros((ROWS, 128), jnp.float32)
        for place in range(DEVS):
            if ORDER[place] // (DEVS // EXPERTS) == expert:
                block = block + returned_ref[place].astype(jnp.float32)
        total = total + block * share
    lower, upper = total[0 : ROWS // 2], total[ROWS // 2 : ROWS]
    kept_ref[...] = jnp.where(core == 0, lower, upper).astype(jnp.bfloat16)
    given_ref[...] = jnp.where(core == 0, upper, lower).astype(jnp.bfloat16)


def mix(core, expert_ids, gate_weights, returned, hidden):
    half = jax.ShapeDtypeStruct((ROWS // 2, 128), jnp.bfloat16)
    return pl.pallas_call(
        mix_kernel,
        out_shape=(half, half),
        in_specs=[SMEM_BLOCK, SMEM_BLOCK, SMEM_BLOCK, VMEM_BLOCK, VMEM_BLOCK],
        out_specs=(VMEM_BLOCK, VMEM_BLOCK),
        compiler_params=pltpu.CompilerParams(vmem_limit_bytes=8 << 20),
        name="mix",
    )(core, expert_ids, gate_weights, returned, hidden)


def exchange(parts):
    return lax.all_to_all(
        parts, "dev", split_axis=0, concat_axis=0, tiled=True, axis_index_groups=[ORDER]
    )


def local(
    query,
    new_key,
    new_value,
    key_cache,
    value_cache,
    cached,
    residual,
    out_weight,
    norm_gain,
    expert_ids,
    gate_weights,
    w_gate,
    w_up,
    w_down,
):
    core = lax.axis_index("side").astype(jnp.int32).reshape(1)
    chip = lax.axis_index("dev").astype(jnp.int32).reshape(1)
    outgoing, mark = attend(
        core, cached, query, new_key, new_value, residual, key_cache, value_cache
    )
    norm_gain, mark = lax.optimization_barrier((norm_gain, mark))
    gain = norm_gain.reshape(DEVS, 2, HALF).transpose(1, 0, 2).reshape(2, HALF_D)
    (projection,) = fetch(mark, out_weight.T)
    arrived = exchange(outgoing.reshape(DEVS, SENT // 2, 2, 128)).reshape(DEVS * SENT, 128)
    packed, mark = project(chip, arrived, projection)
    w_gate = w_gate.reshape(DEVS, 2, HALF, UNITS)
    w_up = w_up.reshape(DEVS, 2, HALF, UNITS)
    early = fetch_early(mark, w_gate)
    hidden = exchange(packed).reshape(HALF_D, 128)
    partial_value, own_hidden = run_experts(chip, hidden, gain, early, w_gate, w_up, w_down)
    returned = exchange(partial_value)
    own_hidden = own_hidden.reshape(2, DEVS, HALF).transpose(1, 0, 2).reshape(ROWS, 128)
    kept, given = mix(core, expert_ids, gate_weights, returned, own_hidden)
    taken = lax.ppermute(given, "side", [(0, 1), (1, 0)])
    first = jnp.where(core == 0, kept, taken)
    second = jnp.where(core == 0, taken, kept)
    return jnp.stack([first.reshape(D // 2), second.reshape(D // 2)])


def solution(mesh):
    in_specs = (
        P("dev", None),
        P("dev", None),
        P("dev", None),
        P("dev", None, None),
        P("dev", None, None),
        P("dev"),
        P("dev", None),
        P(None, "dev"),
        P(),
        P("dev", None),
        P("dev", None),
        P(None, "dev"),
        P(None, "dev"),
        P("dev", None),
    )
    out_specs = P("dev", "side")
    return jax.shard_map(local, mesh=mesh, in_specs=in_specs, out_specs=out_specs, check_vma=False)
```

```python
import math

import jax
import jax.numpy as jnp
from jax import lax
from jax.experimental import pallas as pl
from jax.experimental.pallas import tpu as pltpu
from jax.sharding import PartitionSpec as P

D = 6144
HEADS = 48
KV_HEADS = 8
HEAD_DIM = 128
GROUP = HEADS // KV_HEADS
EXPERTS = 4
CACHE_LEN = 128
DEVS = 64
COLS = D // DEVS
HALF = COLS // 2
ROWS = D // 128
SENT = ROWS + 2
BATCH = 8
UNITS = 512
HALF_D = D // 2
CHUNK = 768
PART = CHUNK // HALF
STEPS = HALF_D // CHUNK
EARLY = 3
DOWN = 1024

epsilon = 1e-05


STRIDE, UNSTRIDE, FIRST = 3, 43, 42
ORDER = [step * STRIDE % DEVS ^ FIRST for step in range(DEVS)]
PLACE = [ORDER.index(chip) for chip in range(DEVS)]

VMEM_BLOCK = pl.BlockSpec(memory_space=pltpu.VMEM)
SMEM_BLOCK = pl.BlockSpec(memory_space=pltpu.SMEM)
ANY_BLOCK = pl.BlockSpec(memory_space=pl.ANY)


def in_hbm(*arrays):
    return tuple(pltpu.with_memory_space_constraint(array, pltpu.HBM) for array in arrays)


def in_vmem(*arrays):
    return tuple(pltpu.with_memory_space_constraint(array, pltpu.VMEM) for array in arrays)


def last_dims(left, right):
    return lax.dot_general(
        left, right, (((1,), (1,)), ((), ())), preferred_element_type=jnp.float32
    )


def attend_kernel(
    core_ref,
    cached_ref,
    query_ref,
    new_key_ref,
    new_value_ref,
    residual_ref,
    key_ref,
    value_ref,
    out_ref,
    mark_ref,
    query_rows,
    residual_rows,
    context_rows,
    pattern,
):
    core = core_ref[0]
    first_row = pl.multiple_of(core * 64, 64)

    def own(ref):
        both = ref[...].astype(jnp.float32)
        return jnp.where(core == 0, both[0:1], both[1:2])

    query_rows[...] = jnp.zeros_like(query_rows)
    residual_rows[...] = jnp.zeros_like(residual_rows)
    both = query_ref[...].astype(jnp.float32)
    for head in range(HEADS):
        row = head // GROUP * 8 + head % GROUP
        query_rows[pl.ds(row, 2, stride=64), :] = both[:, head * 128 : head * 128 + 128]
    both = residual_ref[...].astype(jnp.float32)
    for row in range(ROWS):
        residual_rows[pl.ds(row, 2, stride=64), :] = both[:, row * 128 : row * 128 + 128]
    queries = query_rows[pl.ds(first_row, 64), :]
    narrow = queries.astype(jnp.bfloat16)
    new_key = own(new_key_ref)
    new_value = own(new_value_ref)
    scale = 1.0 / math.sqrt(HEAD_DIM)
    scores = []
    own_keys = []
    for kv in range(KV_HEADS):
        lanes = slice(kv * 128, kv * 128 + 128)
        scores.append(last_dims(narrow[kv * 8 : kv * 8 + 8], key_ref[0, :, lanes]))
        own_keys.append(jnp.broadcast_to(new_key[:, lanes], (8, 128)))
    scores = jnp.concatenate(scores, axis=0) * scale
    own_score = jnp.sum(queries * jnp.concatenate(own_keys, axis=0), axis=1, keepdims=True) * scale
    visible = lax.broadcasted_iota(jnp.int32, scores.shape, 1) < cached_ref[core]
    scores = jnp.where(visible, scores, -jnp.inf)
    highest = jnp.maximum(jnp.max(scores, axis=1, keepdims=True), own_score)
    exponents = jnp.exp(scores - highest)
    own_exp = jnp.exp(own_score - highest)
    denominator = jnp.sum(exponents, axis=1, keepdims=True) + own_exp
    weights = (exponents / denominator).astype(jnp.bfloat16)
    own_weight = (own_exp / denominator).astype(jnp.bfloat16).astype(jnp.float32)
    for kv in range(KV_HEADS):
        lanes = slice(kv * 128, kv * 128 + 128)
        context = jnp.dot(
            weights[kv * 8 : kv * 8 + 8], value_ref[0, :, lanes], preferred_element_type=jnp.float32
        )
        context = context + own_weight[kv * 8 : kv * 8 + 8] * new_value[:, lanes]
        context_rows[kv * GROUP : kv * GROUP + 8, :] = context
    context = context_rows[0:ROWS, :]
    mark_ref[...] = context[0:8]
    for chip in range(BATCH):
        pattern[chip * SENT : chip * SENT + ROWS, :] = context
    for group in range(DEVS // BATCH):
        for chip in range(BATCH):
            wanted = COLS * ORDER[group * BATCH + chip] // 128
            pattern[chip * SENT + ROWS : chip * SENT + SENT, :] = residual_rows[
                pl.ds(first_row + wanted, 2), :
            ]
        first = group * BATCH * SENT
        out_ref[first : first + BATCH * SENT, :] = pattern[...].astype(jnp.bfloat16)


def attend(core, cached, query, new_key, new_value, residual, key_cache, value_cache):
    def whole(shape):
        return pl.BlockSpec(shape, lambda step, core: (0,) * len(shape))

    cache = pl.BlockSpec((1, CACHE_LEN, 1024), lambda step, core: (core[0], 0, 0))
    return pl.pallas_call(
        attend_kernel,
        out_shape=(
            jax.ShapeDtypeStruct((DEVS * SENT, 128), jnp.bfloat16),
            jax.ShapeDtypeStruct((8, 128), jnp.float32),
        ),
        grid_spec=pltpu.PrefetchScalarGridSpec(
            num_scalar_prefetch=1,
            grid=(1,),
            in_specs=[
                SMEM_BLOCK,
                whole((2, D)),
                whole((2, 1024)),
                whole((2, 1024)),
                whole((2, D)),
                cache,
                cache,
            ],
            out_specs=(whole((DEVS * SENT, 128)), whole((8, 128))),
            scratch_shapes=[
                pltpu.VMEM((128, 128), jnp.float32),
                pltpu.VMEM((128, 128), jnp.float32),
                pltpu.VMEM((ROWS + 8, 128), jnp.float32),
                pltpu.VMEM((BATCH * SENT, 128), jnp.float32),
            ],
        ),
        compiler_params=pltpu.CompilerParams(vmem_limit_bytes=8 << 20),
        name="attend",
    )(core, *in_hbm(cached, query, new_key, new_value, residual, key_cache, value_cache))


def fetch_kernel(after_ref, *refs):
    count = (len(refs) - 1) // 2
    copies = [
        pltpu.make_async_copy(refs[i], refs[count + i], refs[-1].at[i]) for i in range(count)
    ]
    for copy in copies:
        copy.start()
    for copy in copies:
        copy.wait()


def fetch(after, *arrays):
    size = sum(array.size * array.dtype.itemsize for array in arrays)
    return pl.pallas_call(
        fetch_kernel,
        out_shape=tuple(pltpu.VMEM(array.shape, array.dtype) for array in arrays),
        in_specs=[ANY_BLOCK] * (len(arrays) + 1),
        out_specs=(VMEM_BLOCK,) * len(arrays),
        scratch_shapes=[pltpu.SemaphoreType.DMA((len(arrays),))],
        compiler_params=pltpu.CompilerParams(vmem_limit_bytes=1 << 20),
        cost_estimate=pl.CostEstimate(flops=0, bytes_accessed=2 * size, transcendentals=0),
        name="fetch",
    )(after, *in_hbm(*arrays))


def project_kernel(chip_ref, arrived_ref, weight_ref, out_ref, mark_ref, rows, context):
    for source in range(0, DEVS * SENT, 400):
        rows[source : source + 400, :] = arrived_ref[source : source + 400, :].astype(jnp.float32)
    for head in range(HEADS):
        context[:, head * 128 : head * 128 + 128] = rows[pl.ds(head, DEVS, stride=SENT), :].astype(
            jnp.bfloat16
        )
    tokens = context[...]
    projected = last_dims(weight_ref[...], jnp.concatenate([tokens, tokens], axis=0))
    flipped = []
    for row in (ROWS, ROWS + 1):
        part = rows[pl.ds(row, DEVS, stride=SENT), :]
        flipped.append(jnp.concatenate([part, part], axis=0).T)
    rows[0:256, :] = jnp.concatenate(flipped, axis=0)
    first = pl.multiple_of(lax.rem(chip_ref[0] * COLS, 128), 32)
    hidden = rows[pl.ds(first, COLS), :] + projected
    lane = lax.broadcasted_iota(jnp.int32, (HALF, 128), 1)
    packed = jnp.where(lane < DEVS, hidden[0:HALF], hidden[HALF:COLS]).astype(jnp.bfloat16)
    mark_ref[...] = hidden[0:8]
    for target in range(DEVS):
        out_ref[target] = packed


def project(chip, arrived, weight):
    return pl.pallas_call(
        project_kernel,
        out_shape=(
            jax.ShapeDtypeStruct((DEVS, HALF, 128), jnp.bfloat16),
            jax.ShapeDtypeStruct((8, 128), jnp.float32),
        ),
        in_specs=[SMEM_BLOCK, VMEM_BLOCK, VMEM_BLOCK],
        out_specs=(VMEM_BLOCK, VMEM_BLOCK),
        scratch_shapes=[
            pltpu.VMEM((DEVS * SENT, 128), jnp.float32),
            pltpu.VMEM((DEVS, D), jnp.bfloat16),
        ],
        compiler_params=pltpu.CompilerParams(vmem_limit_bytes=16 << 20),
        name="project",
    )(chip, arrived, *in_vmem(weight))


def early_kernel(after_ref, gate_hbm, out_ref, sems):
    copies = [
        pltpu.make_async_copy(
            gate_hbm.at[pl.ds(step * PART, PART), 0], out_ref.at[step], sems.at[step]
        )
        for step in range(EARLY)
    ]
    for copy in copies:
        copy.start()
    for copy in copies:
        copy.wait()


def fetch_early(after, w_gate):
    return pl.pallas_call(
        early_kernel,
        out_shape=pltpu.VMEM((EARLY, PART, HALF, UNITS), w_gate.dtype),
        in_specs=[ANY_BLOCK] * 2,
        out_specs=VMEM_BLOCK,
        scratch_shapes=[pltpu.SemaphoreType.DMA((EARLY,))],
        compiler_params=pltpu.CompilerParams(vmem_limit_bytes=1 << 20),
        name="fetch_early",
    )(after, *in_hbm(w_gate))


def expert_kernel(
    chip_ref,
    hidden_ref,
    gain_ref,
    early_ref,
    gate_hbm,
    up_hbm,
    down_hbm,
    out_ref,
    own_ref,
    gate_vmem,
    up_vmem,
    down_vmem,
    flipped,
    scaled,
    result,
    sems,
):
    pieces = [(half, step) for half in range(2) for step in range(STEPS)]
    order = list(range(EARLY, len(pieces))) + list(range(EARLY))
    copies = {}
    for index in order:
        half, step = pieces[index]
        part = pl.ds(step * PART, PART)
        for which, source, target in ((0, gate_hbm, gate_vmem), (1, up_hbm, up_vmem)):
            if which == 1 or index >= EARLY:
                copies[which, index] = pltpu.make_async_copy(
                    source.at[part, half], target.at[part, half], sems.at[which, index]
                )
                copies[which, index].start()
    for step in range(D // DOWN):
        part = pl.ds(step * DOWN, DOWN)
        copies[2, step] = pltpu.make_async_copy(
            down_hbm.at[:, part], down_vmem.at[:, part], sems.at[2, step]
        )
        copies[2, step].start()

    squares = jnp.zeros((128, 128), jnp.float32)
    for block in range(HALF_D // 384):
        columns = jnp.concatenate(
            [
                hidden_ref[PLACE[chip] * HALF : PLACE[chip] * HALF + HALF, :].astype(jnp.float32)
                for chip in range(block * 8, block * 8 + 8)
            ],
            axis=0,
        )
        for third in range(3):
            turned = columns[third * 128 : third * 128 + 128].T
            lanes = slice(block * 384 + third * 128, block * 384 + third * 128 + 128)
            flipped[:, lanes] = turned
            squares = squares + turned * turned
            gain = gain_ref[:, lanes].astype(jnp.float32)
            scaled[0:DEVS, lanes] = (turned[0:DEVS] * gain[0:1]).astype(jnp.bfloat16)
            scaled[DEVS:128, lanes] = (turned[DEVS:128] * gain[1:2]).astype(jnp.bfloat16)
    place = lax.rem(jnp.bitwise_xor(chip_ref[0], FIRST) * UNSTRIDE, DEVS)
    own_ref[0:1, :] = flipped[pl.ds(place, 1), :]
    own_ref[1:2, :] = flipped[pl.ds(place + DEVS, 1), :]
    total = jnp.sum(squares, axis=1, keepdims=True)
    factor = lax.rsqrt((total[0:DEVS] + total[DEVS:128]) * (1.0 / D) + epsilon)

    def product(index, weights):
        half, step = pieces[index]
        rows = scaled[half * DEVS : half * DEVS + DEVS, step * CHUNK : step * CHUNK + CHUNK]
        return jnp.dot(rows, weights.reshape(CHUNK, UNITS), preferred_element_type=jnp.float32)

    def part_of(ref, index):
        half, step = pieces[index]
        return ref[step * PART : step * PART + PART, half]

    gate = jnp.zeros((DEVS, UNITS), jnp.float32)
    up = jnp.zeros((DEVS, UNITS), jnp.float32)
    for index in range(EARLY):
        gate = gate + product(index, early_ref[index])
    for index in order:
        if index >= EARLY:
            copies[0, index].wait()
            gate = gate + product(index, part_of(gate_vmem, index))
        copies[1, index].wait()
        up = up + product(index, part_of(up_vmem, index))
    gate = gate * factor
    up = up * factor
    act = (gate / (1.0 + jnp.exp(-gate)) * up).astype(jnp.bfloat16)
    span = DOWN // 128
    for step in range(D // DOWN):
        copies[2, step].wait()
        block = jnp.dot(
            act, down_vmem[:, step * DOWN : step * DOWN + DOWN], preferred_element_type=jnp.float32
        )
        for column in range(span):
            result[pl.ds(step * span + column, DEVS, stride=ROWS), :] = block[
                :, column * 128 : column * 128 + 128
            ]
        last = (step + 1) * span
        if last % 16 == 0 and last < ROWS:
            for target in range(DEVS):
                out_ref[target, last - 16 : last, :] = result[
                    target * ROWS + last - 16 : target * ROWS + last, :
                ].astype(jnp.bfloat16)
    for target in range(DEVS):
        out_ref[target, ROWS - 16 : ROWS, :] = result[
            target * ROWS + ROWS - 16 : target * ROWS + ROWS, :
        ].astype(jnp.bfloat16)


def run_experts(chip, hidden, gain, early, w_gate, w_up, w_down):
    return pl.pallas_call(
        expert_kernel,
        out_shape=(
            pltpu.HBM((DEVS, ROWS, 128), jnp.bfloat16),
            jax.ShapeDtypeStruct((2, HALF_D), jnp.float32),
        ),
        in_specs=[SMEM_BLOCK] + [VMEM_BLOCK] * 3 + [ANY_BLOCK] * 3,
        out_specs=(VMEM_BLOCK, VMEM_BLOCK),
        scratch_shapes=[
            pltpu.VMEM((DEVS, 2, HALF, UNITS), jnp.bfloat16),
            pltpu.VMEM((DEVS, 2, HALF, UNITS), jnp.bfloat16),
            pltpu.VMEM((UNITS, D), jnp.bfloat16),
            pltpu.VMEM((128, HALF_D), jnp.float32),
            pltpu.VMEM((128, HALF_D), jnp.bfloat16),
            pltpu.VMEM((DEVS * ROWS, 128), jnp.float32),
            pltpu.SemaphoreType.DMA((3, 2 * STEPS)),
        ],
        compiler_params=pltpu.CompilerParams(vmem_limit_bytes=40 << 20),
        name="experts",
    )(chip, hidden, gain, *in_vmem(early), *in_hbm(w_gate, w_up, w_down))


def mix_kernel(core_ref, ids_ref, gates_ref, returned_ref, hidden_ref, kept_ref, given_ref):
    core = core_ref[0]
    total = hidden_ref[...]
    for expert in range(EXPERTS):
        share = jnp.float32(0.0)
        for choice in range(2):
            share = share + jnp.where(
                ids_ref[core, choice] == expert, gates_ref[core, choice], jnp.float32(0.0)
            )
        block = jnp.zeros((ROWS, 128), jnp.float32)
        for place in range(DEVS):
            if ORDER[place] // (DEVS // EXPERTS) == expert:
                block = block + returned_ref[place].astype(jnp.float32)
        total = total + block * share
    lower, upper = total[0 : ROWS // 2], total[ROWS // 2 : ROWS]
    kept_ref[...] = jnp.where(core == 0, lower, upper).astype(jnp.bfloat16)
    given_ref[...] = jnp.where(core == 0, upper, lower).astype(jnp.bfloat16)


def mix(core, expert_ids, gate_weights, returned, hidden):
    half = jax.ShapeDtypeStruct((ROWS // 2, 128), jnp.bfloat16)
    return pl.pallas_call(
        mix_kernel,
        out_shape=(half, half),
        in_specs=[SMEM_BLOCK, SMEM_BLOCK, SMEM_BLOCK, VMEM_BLOCK, VMEM_BLOCK],
        out_specs=(VMEM_BLOCK, VMEM_BLOCK),
        compiler_params=pltpu.CompilerParams(vmem_limit_bytes=8 << 20),
        name="mix",
    )(core, expert_ids, gate_weights, returned, hidden)


def exchange(parts):
    return lax.all_to_all(
        parts, "dev", split_axis=0, concat_axis=0, tiled=True, axis_index_groups=[ORDER]
    )


def local(
    query,
    new_key,
    new_value,
    key_cache,
    value_cache,
    cached,
    residual,
    out_weight,
    norm_gain,
    expert_ids,
    gate_weights,
    w_gate,
    w_up,
    w_down,
):
    core = lax.axis_index("side").astype(jnp.int32).reshape(1)
    chip = lax.axis_index("dev").astype(jnp.int32).reshape(1)
    outgoing, mark = attend(
        core, cached, query, new_key, new_value, residual, key_cache, value_cache
    )
    norm_gain, mark = lax.optimization_barrier((norm_gain, mark))
    gain = norm_gain.reshape(DEVS, 2, HALF).transpose(1, 0, 2).reshape(2, HALF_D)
    (projection,) = fetch(mark, out_weight.T)
    arrived = exchange(outgoing.reshape(DEVS, SENT // 2, 2, 128)).reshape(DEVS * SENT, 128)
    packed, mark = project(chip, arrived, projection)
    w_gate = w_gate.reshape(DEVS, 2, HALF, UNITS)
    w_up = w_up.reshape(DEVS, 2, HALF, UNITS)
    early = fetch_early(mark, w_gate)
    hidden = exchange(packed).reshape(HALF_D, 128)
    partial_value, own_hidden = run_experts(chip, hidden, gain, early, w_gate, w_up, w_down)
    returned = exchange(partial_value)
    own_hidden = own_hidden.reshape(2, DEVS, HALF).transpose(1, 0, 2).reshape(ROWS, 128)
    kept, given = mix(core, expert_ids, gate_weights, returned, own_hidden)
    taken = lax.ppermute(given, "side", [(0, 1), (1, 0)])
    first = jnp.where(core == 0, kept, taken)
    second = jnp.where(core == 0, taken, kept)
    return jnp.stack([first.reshape(D // 2), second.reshape(D // 2)])


def solution(mesh):
    in_specs = (
        P("dev", None),
        P("dev", None),
        P("dev", None),
        P("dev", None, None),
        P("dev", None, None),
        P("dev"),
        P("dev", None),
        P(None, "dev"),
        P(),
        P("dev", None),
        P("dev", None),
        P(None, "dev"),
        P(None, "dev"),
        P("dev", None),
    )
    out_specs = P("dev", "side")
    return jax.shard_map(local, mesh=mesh, in_specs=in_specs, out_specs=out_specs, check_vma=False)
```

```python
import math

import jax
import jax.numpy as jnp
from jax import lax
from jax.experimental import pallas as pl
from jax.experimental.pallas import tpu as pltpu
from jax.sharding import PartitionSpec as P

D = 6144
HEADS = 48
KV_HEADS = 8
HEAD_DIM = 128
GROUP = HEADS // KV_HEADS
EXPERTS = 4
CACHE_LEN = 128
DEVS = 64
COLS = D // DEVS
HALF = COLS // 2
ROWS = D // 128
SENT = ROWS + 2
BATCH = 8
UNITS = 512
HALF_D = D // 2
CHUNK = 768
PART = CHUNK // HALF
STEPS = HALF_D // CHUNK
EARLY = 3
DOWN = 1024

epsilon = 1e-05


FIRST = 42
STRIDE, UNSTRIDE = 3, 43
HIDDEN_STRIDE, BACK_STRIDE = 13, 47


def order_by(stride):
    return [step * stride % DEVS ^ FIRST for step in range(DEVS)]


ORDER = order_by(STRIDE)
PLACE = [ORDER.index(chip) for chip in range(DEVS)]
HIDDEN_ORDER = order_by(HIDDEN_STRIDE)
HIDDEN_PLACE = [HIDDEN_ORDER.index(chip) for chip in range(DEVS)]
BACK_ORDER = order_by(BACK_STRIDE)

VMEM_BLOCK = pl.BlockSpec(memory_space=pltpu.VMEM)
SMEM_BLOCK = pl.BlockSpec(memory_space=pltpu.SMEM)
ANY_BLOCK = pl.BlockSpec(memory_space=pl.ANY)


def in_hbm(*arrays):
    return tuple(pltpu.with_memory_space_constraint(array, pltpu.HBM) for array in arrays)


def in_vmem(*arrays):
    return tuple(pltpu.with_memory_space_constraint(array, pltpu.VMEM) for array in arrays)


def last_dims(left, right):
    return lax.dot_general(
        left, right, (((1,), (1,)), ((), ())), preferred_element_type=jnp.float32
    )


def attend_kernel(
    core_ref,
    cached_ref,
    query_ref,
    new_key_ref,
    new_value_ref,
    residual_ref,
    key_ref,
    value_ref,
    out_ref,
    mark_ref,
    query_rows,
    residual_rows,
    context_rows,
    pattern,
):
    core = core_ref[0]
    first_row = pl.multiple_of(core * 64, 64)

    def own(ref):
        both = ref[...].astype(jnp.float32)
        return jnp.where(core == 0, both[0:1], both[1:2])

    query_rows[...] = jnp.zeros_like(query_rows)
    residual_rows[...] = jnp.zeros_like(residual_rows)
    both = query_ref[...].astype(jnp.float32)
    for head in range(HEADS):
        row = head // GROUP * 8 + head % GROUP
        query_rows[pl.ds(row, 2, stride=64), :] = both[:, head * 128 : head * 128 + 128]
    both = residual_ref[...].astype(jnp.float32)
    for row in range(ROWS):
        residual_rows[pl.ds(row, 2, stride=64), :] = both[:, row * 128 : row * 128 + 128]
    queries = query_rows[pl.ds(first_row, 64), :]
    narrow = queries.astype(jnp.bfloat16)
    new_key = own(new_key_ref)
    new_value = own(new_value_ref)
    scale = 1.0 / math.sqrt(HEAD_DIM)
    scores = []
    own_keys = []
    for kv in range(KV_HEADS):
        lanes = slice(kv * 128, kv * 128 + 128)
        scores.append(last_dims(narrow[kv * 8 : kv * 8 + 8], key_ref[0, :, lanes]))
        own_keys.append(jnp.broadcast_to(new_key[:, lanes], (8, 128)))
    scores = jnp.concatenate(scores, axis=0) * scale
    own_score = jnp.sum(queries * jnp.concatenate(own_keys, axis=0), axis=1, keepdims=True) * scale
    visible = lax.broadcasted_iota(jnp.int32, scores.shape, 1) < cached_ref[core]
    scores = jnp.where(visible, scores, -jnp.inf)
    highest = jnp.maximum(jnp.max(scores, axis=1, keepdims=True), own_score)
    exponents = jnp.exp(scores - highest)
    own_exp = jnp.exp(own_score - highest)
    denominator = jnp.sum(exponents, axis=1, keepdims=True) + own_exp
    weights = (exponents / denominator).astype(jnp.bfloat16)
    own_weight = (own_exp / denominator).astype(jnp.bfloat16).astype(jnp.float32)
    for kv in range(KV_HEADS):
        lanes = slice(kv * 128, kv * 128 + 128)
        context = jnp.dot(
            weights[kv * 8 : kv * 8 + 8], value_ref[0, :, lanes], preferred_element_type=jnp.float32
        )
        context = context + own_weight[kv * 8 : kv * 8 + 8] * new_value[:, lanes]
        context_rows[kv * GROUP : kv * GROUP + 8, :] = context
    context = context_rows[0:ROWS, :]
    mark_ref[...] = context[0:8]
    for chip in range(BATCH):
        pattern[chip * SENT : chip * SENT + ROWS, :] = context
    for group in range(DEVS // BATCH):
        for chip in range(BATCH):
            wanted = COLS * ORDER[group * BATCH + chip] // 128
            pattern[chip * SENT + ROWS : chip * SENT + SENT, :] = residual_rows[
                pl.ds(first_row + wanted, 2), :
            ]
        first = group * BATCH * SENT
        out_ref[first : first + BATCH * SENT, :] = pattern[...].astype(jnp.bfloat16)


def attend(core, cached, query, new_key, new_value, residual, key_cache, value_cache):
    def whole(shape):
        return pl.BlockSpec(shape, lambda step, core: (0,) * len(shape))

    cache = pl.BlockSpec((1, CACHE_LEN, 1024), lambda step, core: (core[0], 0, 0))
    return pl.pallas_call(
        attend_kernel,
        out_shape=(
            jax.ShapeDtypeStruct((DEVS * SENT, 128), jnp.bfloat16),
            jax.ShapeDtypeStruct((8, 128), jnp.float32),
        ),
        grid_spec=pltpu.PrefetchScalarGridSpec(
            num_scalar_prefetch=1,
            grid=(1,),
            in_specs=[
                SMEM_BLOCK,
                whole((2, D)),
                whole((2, 1024)),
                whole((2, 1024)),
                whole((2, D)),
                cache,
                cache,
            ],
            out_specs=(whole((DEVS * SENT, 128)), whole((8, 128))),
            scratch_shapes=[
                pltpu.VMEM((192, 128), jnp.float32),
                pltpu.VMEM((192, 128), jnp.float32),
                pltpu.VMEM((ROWS + 8, 128), jnp.float32),
                pltpu.VMEM((BATCH * SENT, 128), jnp.float32),
            ],
        ),
        compiler_params=pltpu.CompilerParams(vmem_limit_bytes=8 << 20),
        name="attend",
    )(core, *in_hbm(cached, query, new_key, new_value, residual, key_cache, value_cache))


def fetch_kernel(after_ref, *refs):
    count = (len(refs) - 1) // 2
    copies = [
        pltpu.make_async_copy(refs[i], refs[count + i], refs[-1].at[i]) for i in range(count)
    ]
    for copy in copies:
        copy.start()
    for copy in copies:
        copy.wait()


def fetch(after, *arrays):
    size = sum(array.size * array.dtype.itemsize for array in arrays)
    return pl.pallas_call(
        fetch_kernel,
        out_shape=tuple(pltpu.VMEM(array.shape, array.dtype) for array in arrays),
        in_specs=[ANY_BLOCK] * (len(arrays) + 1),
        out_specs=(VMEM_BLOCK,) * len(arrays),
        scratch_shapes=[pltpu.SemaphoreType.DMA((len(arrays),))],
        compiler_params=pltpu.CompilerParams(vmem_limit_bytes=1 << 20),
        cost_estimate=pl.CostEstimate(flops=0, bytes_accessed=2 * size, transcendentals=0),
        name="fetch",
    )(after, *in_hbm(*arrays))


def project_kernel(chip_ref, arrived_ref, weight_ref, out_ref, mark_ref, rows, context):
    for source in range(0, DEVS * SENT, 400):
        rows[source : source + 400, :] = arrived_ref[source : source + 400, :].astype(jnp.float32)
    for head in range(HEADS):
        context[:, head * 128 : head * 128 + 128] = rows[pl.ds(head, DEVS, stride=SENT), :].astype(
            jnp.bfloat16
        )
    tokens = context[...]
    projected = last_dims(weight_ref[...], jnp.concatenate([tokens, tokens], axis=0))
    flipped = []
    for row in (ROWS, ROWS + 1):
        part = rows[pl.ds(row, DEVS, stride=SENT), :]
        flipped.append(jnp.concatenate([part, part], axis=0).T)
    rows[0:256, :] = jnp.concatenate(flipped, axis=0)
    first = pl.multiple_of(lax.rem(chip_ref[0] * COLS, 128), 32)
    hidden = rows[pl.ds(first, COLS), :] + projected
    lane = lax.broadcasted_iota(jnp.int32, (HALF, 128), 1)
    packed = jnp.where(lane < DEVS, hidden[0:HALF], hidden[HALF:COLS]).astype(jnp.bfloat16)
    mark_ref[...] = hidden[0:8]
    for target in range(DEVS):
        out_ref[target] = packed


def project(chip, arrived, weight):
    return pl.pallas_call(
        project_kernel,
        out_shape=(
            jax.ShapeDtypeStruct((DEVS, HALF, 128), jnp.bfloat16),
            jax.ShapeDtypeStruct((8, 128), jnp.float32),
        ),
        in_specs=[SMEM_BLOCK, VMEM_BLOCK, VMEM_BLOCK],
        out_specs=(VMEM_BLOCK, VMEM_BLOCK),
        scratch_shapes=[
            pltpu.VMEM((DEVS * SENT + 56, 128), jnp.float32),
            pltpu.VMEM((DEVS, D), jnp.bfloat16),
        ],
        compiler_params=pltpu.CompilerParams(vmem_limit_bytes=16 << 20),
        name="project",
    )(chip, arrived, *in_vmem(weight))


def early_kernel(after_ref, gate_hbm, out_ref, sems):
    copies = [
        pltpu.make_async_copy(
            gate_hbm.at[pl.ds(step * PART, PART), 0], out_ref.at[step], sems.at[step]
        )
        for step in range(EARLY)
    ]
    for copy in copies:
        copy.start()
    for copy in copies:
        copy.wait()


def fetch_early(after, w_gate):
    return pl.pallas_call(
        early_kernel,
        out_shape=pltpu.VMEM((EARLY, PART, HALF, UNITS), w_gate.dtype),
        in_specs=[ANY_BLOCK] * 2,
        out_specs=VMEM_BLOCK,
        scratch_shapes=[pltpu.SemaphoreType.DMA((EARLY,))],
        compiler_params=pltpu.CompilerParams(vmem_limit_bytes=1 << 20),
        name="fetch_early",
    )(after, *in_hbm(w_gate))


def expert_kernel(
    chip_ref,
    hidden_ref,
    gain_ref,
    early_ref,
    gate_hbm,
    up_hbm,
    down_hbm,
    out_ref,
    own_ref,
    gate_vmem,
    up_vmem,
    down_vmem,
    flipped,
    scaled,
    result,
    sems,
):
    pieces = [(half, step) for half in range(2) for step in range(STEPS)]
    order = list(range(EARLY, len(pieces))) + list(range(EARLY))
    copies = {}
    for index in order:
        half, step = pieces[index]
        part = pl.ds(step * PART, PART)
        for which, source, target in ((0, gate_hbm, gate_vmem), (1, up_hbm, up_vmem)):
            if which == 1 or index >= EARLY:
                copies[which, index] = pltpu.make_async_copy(
                    source.at[part, half], target.at[part, half], sems.at[which, index]
                )
                copies[which, index].start()
    for step in range(D // DOWN):
        part = pl.ds(step * DOWN, DOWN)
        copies[2, step] = pltpu.make_async_copy(
            down_hbm.at[:, part], down_vmem.at[:, part], sems.at[2, step]
        )
        copies[2, step].start()

    squares = jnp.zeros((128, 128), jnp.float32)
    for block in range(HALF_D // 384):
        columns = jnp.concatenate(
            [
                hidden_ref[HIDDEN_PLACE[chip] * HALF : HIDDEN_PLACE[chip] * HALF + HALF, :].astype(jnp.float32)
                for chip in range(block * 8, block * 8 + 8)
            ],
            axis=0,
        )
        for third in range(3):
            turned = columns[third * 128 : third * 128 + 128].T
            lanes = slice(block * 384 + third * 128, block * 384 + third * 128 + 128)
            flipped[:, lanes] = turned
            squares = squares + turned * turned
            gain = gain_ref[:, lanes].astype(jnp.float32)
            scaled[0:DEVS, lanes] = (turned[0:DEVS] * gain[0:1]).astype(jnp.bfloat16)
            scaled[DEVS:128, lanes] = (turned[DEVS:128] * gain[1:2]).astype(jnp.bfloat16)
    place = lax.rem(jnp.bitwise_xor(chip_ref[0], FIRST) * UNSTRIDE, DEVS)
    own_ref[0:1, :] = flipped[pl.ds(place, 1), :]
    own_ref[1:2, :] = flipped[pl.ds(place + DEVS, 1), :]
    total = jnp.sum(squares, axis=1, keepdims=True)
    factor = lax.rsqrt((total[0:DEVS] + total[DEVS:128]) * (1.0 / D) + epsilon)

    def product(index, weights):
        half, step = pieces[index]
        rows = scaled[half * DEVS : half * DEVS + DEVS, step * CHUNK : step * CHUNK + CHUNK]
        return jnp.dot(rows, weights.reshape(CHUNK, UNITS), preferred_element_type=jnp.float32)

    def part_of(ref, index):
        half, step = pieces[index]
        return ref[step * PART : step * PART + PART, half]

    gate = jnp.zeros((DEVS, UNITS), jnp.float32)
    up = jnp.zeros((DEVS, UNITS), jnp.float32)
    for index in range(EARLY):
        gate = gate + product(index, early_ref[index])
    for index in order:
        if index >= EARLY:
            copies[0, index].wait()
            gate = gate + product(index, part_of(gate_vmem, index))
        copies[1, index].wait()
        up = up + product(index, part_of(up_vmem, index))
    gate = gate * factor
    up = up * factor
    act = (gate / (1.0 + jnp.exp(-gate)) * up).astype(jnp.bfloat16)
    span = DOWN // 128
    token_rows = [PLACE[chip] * ROWS for chip in BACK_ORDER]
    for step in range(D // DOWN):
        copies[2, step].wait()
        block = jnp.dot(
            act, down_vmem[:, step * DOWN : step * DOWN + DOWN], preferred_element_type=jnp.float32
        )
        for column in range(span):
            result[pl.ds(step * span + column, DEVS, stride=ROWS), :] = block[
                :, column * 128 : column * 128 + 128
            ]
        last = (step + 1) * span
        if last % 16 == 0 and last < ROWS:
            for target, first in enumerate(token_rows):
                out_ref[target, last - 16 : last, :] = result[
                    first + last - 16 : first + last, :
                ].astype(jnp.bfloat16)
    for target, first in enumerate(token_rows):
        out_ref[target, ROWS - 16 : ROWS, :] = result[
            first + ROWS - 16 : first + ROWS, :
        ].astype(jnp.bfloat16)


def run_experts(chip, hidden, gain, early, w_gate, w_up, w_down):
    return pl.pallas_call(
        expert_kernel,
        out_shape=(
            pltpu.HBM((DEVS, ROWS, 128), jnp.bfloat16),
            jax.ShapeDtypeStruct((2, HALF_D), jnp.float32),
        ),
        in_specs=[SMEM_BLOCK] + [VMEM_BLOCK] * 3 + [ANY_BLOCK] * 3,
        out_specs=(VMEM_BLOCK, VMEM_BLOCK),
        scratch_shapes=[
            pltpu.VMEM((DEVS, 2, HALF, UNITS), jnp.bfloat16),
            pltpu.VMEM((DEVS, 2, HALF, UNITS), jnp.bfloat16),
            pltpu.VMEM((UNITS, D), jnp.bfloat16),
            pltpu.VMEM((128, HALF_D), jnp.float32),
            pltpu.VMEM((128, HALF_D), jnp.bfloat16),
            pltpu.VMEM((DEVS * ROWS + ROWS, 128), jnp.float32),
            pltpu.SemaphoreType.DMA((3, 2 * STEPS)),
        ],
        compiler_params=pltpu.CompilerParams(vmem_limit_bytes=40 << 20),
        name="experts",
    )(chip, hidden, gain, *in_vmem(early), *in_hbm(w_gate, w_up, w_down))


def mix_kernel(core_ref, ids_ref, gates_ref, returned_ref, hidden_ref, kept_ref, given_ref):
    core = core_ref[0]
    total = hidden_ref[...]
    for expert in range(EXPERTS):
        share = jnp.float32(0.0)
        for choice in range(2):
            share = share + jnp.where(
                ids_ref[core, choice] == expert, gates_ref[core, choice], jnp.float32(0.0)
            )
        block = jnp.zeros((ROWS, 128), jnp.float32)
        for place in range(DEVS):
            if BACK_ORDER[place] // (DEVS // EXPERTS) == expert:
                block = block + returned_ref[place].astype(jnp.float32)
        total = total + block * share
    lower, upper = total[0 : ROWS // 2], total[ROWS // 2 : ROWS]
    kept_ref[...] = jnp.where(core == 0, lower, upper).astype(jnp.bfloat16)
    given_ref[...] = jnp.where(core == 0, upper, lower).astype(jnp.bfloat16)


def mix(core, expert_ids, gate_weights, returned, hidden):
    half = jax.ShapeDtypeStruct((ROWS // 2, 128), jnp.bfloat16)
    return pl.pallas_call(
        mix_kernel,
        out_shape=(half, half),
        in_specs=[SMEM_BLOCK, SMEM_BLOCK, SMEM_BLOCK, VMEM_BLOCK, VMEM_BLOCK],
        out_specs=(VMEM_BLOCK, VMEM_BLOCK),
        compiler_params=pltpu.CompilerParams(vmem_limit_bytes=8 << 20),
        name="mix",
    )(core, expert_ids, gate_weights, returned, hidden)


def exchange(parts, order):
    return lax.all_to_all(
        parts, "dev", split_axis=0, concat_axis=0, tiled=True, axis_index_groups=[order]
    )


def local(
    query,
    new_key,
    new_value,
    key_cache,
    value_cache,
    cached,
    residual,
    out_weight,
    norm_gain,
    expert_ids,
    gate_weights,
    w_gate,
    w_up,
    w_down,
):
    core = lax.axis_index("side").astype(jnp.int32).reshape(1)
    chip = lax.axis_index("dev").astype(jnp.int32).reshape(1)
    outgoing, mark = attend(
        core, cached, query, new_key, new_value, residual, key_cache, value_cache
    )
    norm_gain, mark = lax.optimization_barrier((norm_gain, mark))
    gain = norm_gain.reshape(DEVS, 2, HALF).transpose(1, 0, 2).reshape(2, HALF_D)
    (projection,) = fetch(mark, out_weight.T)
    arrived = exchange(outgoing.reshape(DEVS, SENT // 2, 2, 128), ORDER).reshape(DEVS * SENT, 128)
    packed, mark = project(chip, arrived, projection)
    w_gate = w_gate.reshape(DEVS, 2, HALF, UNITS)
    w_up = w_up.reshape(DEVS, 2, HALF, UNITS)
    early = fetch_early(mark, w_gate)
    hidden = exchange(packed, HIDDEN_ORDER).reshape(HALF_D, 128)
    partial_value, own_hidden = run_experts(chip, hidden, gain, early, w_gate, w_up, w_down)
    returned = exchange(partial_value, BACK_ORDER)
    own_hidden = own_hidden.reshape(2, DEVS, HALF).transpose(1, 0, 2).reshape(ROWS, 128)
    kept, given = mix(core, expert_ids, gate_weights, returned, own_hidden)
    taken = lax.ppermute(given, "side", [(0, 1), (1, 0)])
    first = jnp.where(core == 0, kept, taken)
    second = jnp.where(core == 0, taken, kept)
    return jnp.stack([first.reshape(D // 2), second.reshape(D // 2)])


def solution(mesh):
    in_specs = (
        P("dev", None),
        P("dev", None),
        P("dev", None),
        P("dev", None, None),
        P("dev", None, None),
        P("dev"),
        P("dev", None),
        P(None, "dev"),
        P(),
        P("dev", None),
        P("dev", None),
        P(None, "dev"),
        P(None, "dev"),
        P("dev", None),
    )
    out_specs = P("dev", "side")
    return jax.shard_map(local, mesh=mesh, in_specs=in_specs, out_specs=out_specs, check_vma=False)
```

```python
import math

import jax
import jax.numpy as jnp
from jax import lax
from jax.experimental import pallas as pl
from jax.experimental.pallas import tpu as pltpu
from jax.sharding import PartitionSpec as P

D = 6144
HEADS = 48
KV_HEADS = 8
HEAD_DIM = 128
GROUP = HEADS // KV_HEADS
EXPERTS = 4
CACHE_LEN = 128
DEVS = 64
COLS = D // DEVS
HALF = COLS // 2
ROWS = D // 128
SENT = ROWS + 2
BATCH = 8
UNITS = 512
HALF_D = D // 2
CHUNK = 768
PART = CHUNK // HALF
STEPS = HALF_D // CHUNK
EARLY = 3
DOWN = 1024

epsilon = 1e-05


FIRST = 42
STRIDE, UNSTRIDE = 3, 43
HIDDEN_STRIDE, BACK_STRIDE = 13, 47


def order_by(stride):
    return [step * stride % DEVS ^ FIRST for step in range(DEVS)]


ORDER = order_by(STRIDE)
PLACE = [ORDER.index(chip) for chip in range(DEVS)]
HIDDEN_ORDER = order_by(HIDDEN_STRIDE)
HIDDEN_PLACE = [HIDDEN_ORDER.index(chip) for chip in range(DEVS)]
BACK_ORDER = order_by(BACK_STRIDE)

VMEM_BLOCK = pl.BlockSpec(memory_space=pltpu.VMEM)
SMEM_BLOCK = pl.BlockSpec(memory_space=pltpu.SMEM)
ANY_BLOCK = pl.BlockSpec(memory_space=pl.ANY)


def in_hbm(*arrays):
    return tuple(pltpu.with_memory_space_constraint(array, pltpu.HBM) for array in arrays)


def in_vmem(*arrays):
    return tuple(pltpu.with_memory_space_constraint(array, pltpu.VMEM) for array in arrays)


def last_dims(left, right):
    return lax.dot_general(
        left, right, (((1,), (1,)), ((), ())), preferred_element_type=jnp.float32
    )


def attend_kernel(
    core_ref,
    cached_ref,
    query_ref,
    new_key_ref,
    new_value_ref,
    residual_ref,
    key_ref,
    value_ref,
    out_ref,
    mark_ref,
    query_rows,
    residual_rows,
    context_rows,
    pattern,
):
    core = core_ref[0]
    first_row = pl.multiple_of(core * 64, 64)

    def own(ref):
        both = ref[...].astype(jnp.float32)
        return jnp.where(core == 0, both[0:1], both[1:2])

    query_rows[...] = jnp.zeros_like(query_rows)
    residual_rows[...] = jnp.zeros_like(residual_rows)
    both = query_ref[...].astype(jnp.float32)
    for head in range(HEADS):
        row = head // GROUP * 8 + head % GROUP
        query_rows[pl.ds(row, 2, stride=64), :] = both[:, head * 128 : head * 128 + 128]
    both = residual_ref[...].astype(jnp.float32)
    for row in range(ROWS):
        residual_rows[pl.ds(row, 2, stride=64), :] = both[:, row * 128 : row * 128 + 128]
    queries = query_rows[pl.ds(first_row, 64), :]
    narrow = queries.astype(jnp.bfloat16)
    new_key = own(new_key_ref)
    new_value = own(new_value_ref)
    scale = 1.0 / math.sqrt(HEAD_DIM)
    scores = []
    own_keys = []
    for kv in range(KV_HEADS):
        lanes = slice(kv * 128, kv * 128 + 128)
        scores.append(last_dims(narrow[kv * 8 : kv * 8 + 8], key_ref[0, :, lanes]))
        own_keys.append(jnp.broadcast_to(new_key[:, lanes], (8, 128)))
    scores = jnp.concatenate(scores, axis=0) * scale
    own_score = jnp.sum(queries * jnp.concatenate(own_keys, axis=0), axis=1, keepdims=True) * scale
    visible = lax.broadcasted_iota(jnp.int32, scores.shape, 1) < cached_ref[core]
    scores = jnp.where(visible, scores, -jnp.inf)
    highest = jnp.maximum(jnp.max(scores, axis=1, keepdims=True), own_score)
    exponents = jnp.exp(scores - highest)
    own_exp = jnp.exp(own_score - highest)
    denominator = jnp.sum(exponents, axis=1, keepdims=True) + own_exp
    weights = (exponents / denominator).astype(jnp.bfloat16)
    own_weight = (own_exp / denominator).astype(jnp.bfloat16).astype(jnp.float32)
    for kv in range(KV_HEADS):
        lanes = slice(kv * 128, kv * 128 + 128)
        context = jnp.dot(
            weights[kv * 8 : kv * 8 + 8], value_ref[0, :, lanes], preferred_element_type=jnp.float32
        )
        context = context + own_weight[kv * 8 : kv * 8 + 8] * new_value[:, lanes]
        context_rows[kv * GROUP : kv * GROUP + 8, :] = context
    context = context_rows[0:ROWS, :]
    mark_ref[...] = context[0:8]
    for chip in range(BATCH):
        pattern[chip * SENT : chip * SENT + ROWS, :] = context
    for group in range(DEVS // BATCH):
        for chip in range(BATCH):
            wanted = COLS * ORDER[group * BATCH + chip] // 128
            pattern[chip * SENT + ROWS : chip * SENT + SENT, :] = residual_rows[
                pl.ds(first_row + wanted, 2), :
            ]
        first = group * BATCH * SENT
        out_ref[first : first + BATCH * SENT, :] = pattern[...].astype(jnp.bfloat16)


def attend(core, cached, query, new_key, new_value, residual, key_cache, value_cache):
    def whole(shape):
        return pl.BlockSpec(shape, lambda step, core: (0,) * len(shape))

    cache = pl.BlockSpec((1, CACHE_LEN, 1024), lambda step, core: (core[0], 0, 0))
    return pl.pallas_call(
        attend_kernel,
        out_shape=(
            jax.ShapeDtypeStruct((DEVS * SENT, 128), jnp.bfloat16),
            jax.ShapeDtypeStruct((8, 128), jnp.float32),
        ),
        grid_spec=pltpu.PrefetchScalarGridSpec(
            num_scalar_prefetch=1,
            grid=(1,),
            in_specs=[
                SMEM_BLOCK,
                whole((2, D)),
                whole((2, 1024)),
                whole((2, 1024)),
                whole((2, D)),
                cache,
                cache,
            ],
            out_specs=(whole((DEVS * SENT, 128)), whole((8, 128))),
            scratch_shapes=[
                pltpu.VMEM((192, 128), jnp.float32),
                pltpu.VMEM((192, 128), jnp.float32),
                pltpu.VMEM((ROWS + 8, 128), jnp.float32),
                pltpu.VMEM((BATCH * SENT, 128), jnp.float32),
            ],
        ),
        compiler_params=pltpu.CompilerParams(vmem_limit_bytes=8 << 20),
        name="attend",
    )(core, *in_hbm(cached, query, new_key, new_value, residual, key_cache, value_cache))


def fetch_kernel(after_ref, *refs):
    count = (len(refs) - 1) // 2
    copies = [
        pltpu.make_async_copy(refs[i], refs[count + i], refs[-1].at[i]) for i in range(count)
    ]
    for copy in copies:
        copy.start()
    for copy in copies:
        copy.wait()


def fetch(after, *arrays):
    size = sum(array.size * array.dtype.itemsize for array in arrays)
    return pl.pallas_call(
        fetch_kernel,
        out_shape=tuple(pltpu.VMEM(array.shape, array.dtype) for array in arrays),
        in_specs=[ANY_BLOCK] * (len(arrays) + 1),
        out_specs=(VMEM_BLOCK,) * len(arrays),
        scratch_shapes=[pltpu.SemaphoreType.DMA((len(arrays),))],
        compiler_params=pltpu.CompilerParams(vmem_limit_bytes=1 << 20),
        cost_estimate=pl.CostEstimate(flops=0, bytes_accessed=2 * size, transcendentals=0),
        name="fetch",
    )(after, *in_hbm(*arrays))


def project_kernel(chip_ref, arrived_ref, weight_ref, out_ref, mark_ref, rows):
    for source in range(0, DEVS * SENT, 400):
        rows[source : source + 400, :] = arrived_ref[source : source + 400, :].astype(jnp.float32)
    projected = jnp.zeros((COLS, 128), jnp.float32)
    for group in range(0, HEADS, 8):
        tokens = jnp.concatenate(
            [
                rows[pl.ds(head, DEVS, stride=SENT), :].astype(jnp.bfloat16)
                for head in range(group, group + 8)
            ],
            axis=1,
        )
        projected = projected + last_dims(
            weight_ref[:, group * 128 : (group + 8) * 128],
            jnp.concatenate([tokens, tokens], axis=0),
        )
    flipped = []
    for row in (ROWS, ROWS + 1):
        part = rows[pl.ds(row, DEVS, stride=SENT), :]
        flipped.append(jnp.concatenate([part, part], axis=0).T)
    rows[0:256, :] = jnp.concatenate(flipped, axis=0)
    first = pl.multiple_of(lax.rem(chip_ref[0] * COLS, 128), 32)
    hidden = rows[pl.ds(first, COLS), :] + projected
    lane = lax.broadcasted_iota(jnp.int32, (HALF, 128), 1)
    packed = jnp.where(lane < DEVS, hidden[0:HALF], hidden[HALF:COLS]).astype(jnp.bfloat16)
    mark_ref[...] = hidden[0:8]
    for target in range(DEVS):
        out_ref[target] = packed


def project(chip, arrived, weight):
    return pl.pallas_call(
        project_kernel,
        out_shape=(
            jax.ShapeDtypeStruct((DEVS, HALF, 128), jnp.bfloat16),
            jax.ShapeDtypeStruct((8, 128), jnp.float32),
        ),
        in_specs=[SMEM_BLOCK, VMEM_BLOCK, VMEM_BLOCK],
        out_specs=(VMEM_BLOCK, VMEM_BLOCK),
        scratch_shapes=[
            pltpu.VMEM((DEVS * SENT + 56, 128), jnp.float32),
        ],
        compiler_params=pltpu.CompilerParams(vmem_limit_bytes=16 << 20),
        name="project",
    )(chip, arrived, *in_vmem(weight))


def early_kernel(after_ref, gate_hbm, out_ref, sems):
    copies = [
        pltpu.make_async_copy(
            gate_hbm.at[pl.ds(step * PART, PART), 0], out_ref.at[step], sems.at[step]
        )
        for step in range(EARLY)
    ]
    for copy in copies:
        copy.start()
    for copy in copies:
        copy.wait()


def fetch_early(after, w_gate):
    return pl.pallas_call(
        early_kernel,
        out_shape=pltpu.VMEM((EARLY, PART, HALF, UNITS), w_gate.dtype),
        in_specs=[ANY_BLOCK] * 2,
        out_specs=VMEM_BLOCK,
        scratch_shapes=[pltpu.SemaphoreType.DMA((EARLY,))],
        compiler_params=pltpu.CompilerParams(vmem_limit_bytes=1 << 20),
        name="fetch_early",
    )(after, *in_hbm(w_gate))


def expert_kernel(
    chip_ref,
    hidden_ref,
    gain_ref,
    early_ref,
    gate_hbm,
    up_hbm,
    down_hbm,
    out_ref,
    own_ref,
    gate_vmem,
    up_vmem,
    down_vmem,
    flipped,
    scaled,
    result,
    sems,
):
    pieces = [(half, step) for half in range(2) for step in range(STEPS)]
    order = list(range(EARLY, len(pieces))) + list(range(EARLY))
    copies = {}
    for index in order:
        half, step = pieces[index]
        part = pl.ds(step * PART, PART)
        for which, source, target in ((0, gate_hbm, gate_vmem), (1, up_hbm, up_vmem)):
            if which == 1 or index >= EARLY:
                copies[which, index] = pltpu.make_async_copy(
                    source.at[part, half], target.at[part, half], sems.at[which, index]
                )
                copies[which, index].start()
    for step in range(D // DOWN):
        part = pl.ds(step * DOWN, DOWN)
        copies[2, step] = pltpu.make_async_copy(
            down_hbm.at[:, part], down_vmem.at[:, part], sems.at[2, step]
        )
        copies[2, step].start()

    squares = jnp.zeros((128, 128), jnp.float32)
    for block in range(HALF_D // 384):
        columns = jnp.concatenate(
            [
                hidden_ref[HIDDEN_PLACE[chip] * HALF : HIDDEN_PLACE[chip] * HALF + HALF, :].astype(jnp.float32)
                for chip in range(block * 8, block * 8 + 8)
            ],
            axis=0,
        )
        for third in range(3):
            turned = columns[third * 128 : third * 128 + 128].T
            lanes = slice(block * 384 + third * 128, block * 384 + third * 128 + 128)
            flipped[:, lanes] = turned
            squares = squares + turned * turned
            gain = gain_ref[:, lanes].astype(jnp.float32)
            scaled[0:DEVS, lanes] = (turned[0:DEVS] * gain[0:1]).astype(jnp.bfloat16)
            scaled[DEVS:128, lanes] = (turned[DEVS:128] * gain[1:2]).astype(jnp.bfloat16)
    place = lax.rem(jnp.bitwise_xor(chip_ref[0], FIRST) * UNSTRIDE, DEVS)
    own_ref[0:1, :] = flipped[pl.ds(place, 1), :]
    own_ref[1:2, :] = flipped[pl.ds(place + DEVS, 1), :]
    total = jnp.sum(squares, axis=1, keepdims=True)
    factor = lax.rsqrt((total[0:DEVS] + total[DEVS:128]) * (1.0 / D) + epsilon)

    def product(index, weights):
        half, step = pieces[index]
        rows = scaled[half * DEVS : half * DEVS + DEVS, step * CHUNK : step * CHUNK + CHUNK]
        return jnp.dot(rows, weights.reshape(CHUNK, UNITS), preferred_element_type=jnp.float32)

    def part_of(ref, index):
        half, step = pieces[index]
        return ref[step * PART : step * PART + PART, half]

    gate = jnp.zeros((DEVS, UNITS), jnp.float32)
    up = jnp.zeros((DEVS, UNITS), jnp.float32)
    for index in range(EARLY):
        gate = gate + product(index, early_ref[index])
    for index in order:
        if index >= EARLY:
            copies[0, index].wait()
            gate = gate + product(index, part_of(gate_vmem, index))
        copies[1, index].wait()
        up = up + product(index, part_of(up_vmem, index))
    gate = gate * factor
    up = up * factor
    act = (gate / (1.0 + jnp.exp(-gate)) * up).astype(jnp.bfloat16)
    span = DOWN // 128
    token_rows = [PLACE[chip] * ROWS for chip in BACK_ORDER]
    for step in range(D // DOWN):
        copies[2, step].wait()
        block = jnp.dot(
            act, down_vmem[:, step * DOWN : step * DOWN + DOWN], preferred_element_type=jnp.float32
        )
        for column in range(span):
            result[pl.ds(step * span + column, DEVS, stride=ROWS), :] = block[
                :, column * 128 : column * 128 + 128
            ]
        last = (step + 1) * span
        if last % 16 == 0 and last < ROWS:
            for target, first in enumerate(token_rows):
                out_ref[target, last - 16 : last, :] = result[
                    first + last - 16 : first + last, :
                ].astype(jnp.bfloat16)
    for target, first in enumerate(token_rows):
        out_ref[target, ROWS - 16 : ROWS, :] = result[
            first + ROWS - 16 : first + ROWS, :
        ].astype(jnp.bfloat16)


def run_experts(chip, hidden, gain, early, w_gate, w_up, w_down):
    return pl.pallas_call(
        expert_kernel,
        out_shape=(
            pltpu.HBM((DEVS, ROWS, 128), jnp.bfloat16),
            jax.ShapeDtypeStruct((2, HALF_D), jnp.float32),
        ),
        in_specs=[SMEM_BLOCK] + [VMEM_BLOCK] * 3 + [ANY_BLOCK] * 3,
        out_specs=(VMEM_BLOCK, VMEM_BLOCK),
        scratch_shapes=[
            pltpu.VMEM((DEVS, 2, HALF, UNITS), jnp.bfloat16),
            pltpu.VMEM((DEVS, 2, HALF, UNITS), jnp.bfloat16),
            pltpu.VMEM((UNITS, D), jnp.bfloat16),
            pltpu.VMEM((128, HALF_D), jnp.float32),
            pltpu.VMEM((128, HALF_D), jnp.bfloat16),
            pltpu.VMEM((DEVS * ROWS + ROWS, 128), jnp.float32),
            pltpu.SemaphoreType.DMA((3, 2 * STEPS)),
        ],
        compiler_params=pltpu.CompilerParams(vmem_limit_bytes=40 << 20),
        name="experts",
    )(chip, hidden, gain, *in_vmem(early), *in_hbm(w_gate, w_up, w_down))


def mix_kernel(core_ref, ids_ref, gates_ref, returned_ref, hidden_ref, kept_ref, given_ref):
    core = core_ref[0]
    total = hidden_ref[...]
    for expert in range(EXPERTS):
        share = jnp.float32(0.0)
        for choice in range(2):
            share = share + jnp.where(
                ids_ref[core, choice] == expert, gates_ref[core, choice], jnp.float32(0.0)
            )
        block = jnp.zeros((ROWS, 128), jnp.float32)
        for place in range(DEVS):
            if BACK_ORDER[place] // (DEVS // EXPERTS) == expert:
                block = block + returned_ref[place].astype(jnp.float32)
        total = total + block * share
    lower, upper = total[0 : ROWS // 2], total[ROWS // 2 : ROWS]
    kept_ref[...] = jnp.where(core == 0, lower, upper).astype(jnp.bfloat16)
    given_ref[...] = jnp.where(core == 0, upper, lower).astype(jnp.bfloat16)


def mix(core, expert_ids, gate_weights, returned, hidden):
    half = jax.ShapeDtypeStruct((ROWS // 2, 128), jnp.bfloat16)
    return pl.pallas_call(
        mix_kernel,
        out_shape=(half, half),
        in_specs=[SMEM_BLOCK, SMEM_BLOCK, SMEM_BLOCK, VMEM_BLOCK, VMEM_BLOCK],
        out_specs=(VMEM_BLOCK, VMEM_BLOCK),
        compiler_params=pltpu.CompilerParams(vmem_limit_bytes=8 << 20),
        name="mix",
    )(core, expert_ids, gate_weights, returned, hidden)


def exchange(parts, order):
    return lax.all_to_all(
        parts, "dev", split_axis=0, concat_axis=0, tiled=True, axis_index_groups=[order]
    )


def local(
    query,
    new_key,
    new_value,
    key_cache,
    value_cache,
    cached,
    residual,
    out_weight,
    norm_gain,
    expert_ids,
    gate_weights,
    w_gate,
    w_up,
    w_down,
):
    core = lax.axis_index("side").astype(jnp.int32).reshape(1)
    chip = lax.axis_index("dev").astype(jnp.int32).reshape(1)
    outgoing, mark = attend(
        core, cached, query, new_key, new_value, residual, key_cache, value_cache
    )
    norm_gain, mark = lax.optimization_barrier((norm_gain, mark))
    gain = norm_gain.reshape(DEVS, 2, HALF).transpose(1, 0, 2).reshape(2, HALF_D)
    (projection,) = fetch(mark, out_weight.T)
    arrived = exchange(outgoing.reshape(DEVS, SENT // 2, 2, 128), ORDER).reshape(DEVS * SENT, 128)
    packed, mark = project(chip, arrived, projection)
    w_gate = w_gate.reshape(DEVS, 2, HALF, UNITS)
    w_up = w_up.reshape(DEVS, 2, HALF, UNITS)
    early = fetch_early(mark, w_gate)
    hidden = exchange(packed, HIDDEN_ORDER).reshape(HALF_D, 128)
    partial_value, own_hidden = run_experts(chip, hidden, gain, early, w_gate, w_up, w_down)
    returned = exchange(partial_value, BACK_ORDER)
    own_hidden = own_hidden.reshape(2, DEVS, HALF).transpose(1, 0, 2).reshape(ROWS, 128)
    kept, given = mix(core, expert_ids, gate_weights, returned, own_hidden)
    taken = lax.ppermute(given, "side", [(0, 1), (1, 0)])
    first = jnp.where(core == 0, kept, taken)
    second = jnp.where(core == 0, taken, kept)
    return jnp.stack([first.reshape(D // 2), second.reshape(D // 2)])


def solution(mesh):
    in_specs = (
        P("dev", None),
        P("dev", None),
        P("dev", None),
        P("dev", None, None),
        P("dev", None, None),
        P("dev"),
        P("dev", None),
        P(None, "dev"),
        P(),
        P("dev", None),
        P("dev", None),
        P(None, "dev"),
        P(None, "dev"),
        P("dev", None),
    )
    out_specs = P("dev", "side")
    return jax.shard_map(local, mesh=mesh, in_specs=in_specs, out_specs=out_specs, check_vma=False)
```
